32 devices in a mesh: pipe: 2 (over y), expert: 4 (over x, core), dp: 4 (over z).
Axes of the slice: x: 2, y: 2, z: 4, core: 2. Of those that a mesh axis runs over, the one named last changes fastest.
Arguments:
- x_forward: bfloat16 [2, 1024, 7168], P('pipe', ('expert', 'dp')), may hold values from -6 to 6
- route_forward: int32 [2, 1024, 1], P('pipe', ('expert', 'dp')), may hold values from 0 to 1; in each aligned block of 64 rows (0 to 63, 64 to 127, ..., all dimensions but the last counted through in order) at most 40 rows name the same one
- prob_forward: float32 [2, 1024], P('pipe', ('expert', 'dp')), may hold values from 0.3 to 1
- x_backward: bfloat16 [2, 1024, 7168], P('pipe', ('expert', 'dp')), may hold values from -6 to 6
- route_backward: int32 [2, 1024, 1], P('pipe', ('expert', 'dp')), may hold values from 0 to 1; in each aligned block of 64 rows (0 to 63, 64 to 127, ..., all dimensions but the last counted through in order) at most 40 rows name the same one
- prob_backward: float32 [2, 1024], P('pipe', ('expert', 'dp')), may hold values from 0.3 to 1
- grad_output: bfloat16 [2, 1024, 7168], P('pipe', ('expert', 'dp')), may hold values from -6 to 6
- w_gate: bfloat16 [2, 4, 7168, 512], P('pipe', 'expert', None, 'dp'), may hold values from -0.0625 to 0.0625
- w_up: bfloat16 [2, 4, 7168, 512], P('pipe', 'expert', None, 'dp'), may hold values from -0.0625 to 0.0625
- w_down: bfloat16 [2, 4, 512, 7168], P('pipe', 'expert', 'dp'), may hold values from -0.1875 to 0.1875
Outputs:
- next_input: bfloat16 [2, 1024, 7168], P('pipe', ('expert', 'dp'))
- next_grad: bfloat16 [2, 1024, 7168], P('pipe', ('expert', 'dp'))
The draws below stay inside these ranges and needn't reach their ends.
Inputs may be any that keep to these rules, and one draw needn't show every extreme that they name: `route_forward`: in every aligned block of 64 rows (the rows of one device) no expert is named by more than 40 tokens, a bound that some block reaches. `route_backward`: as for route_forward.
All inputs are finite; a program needn't handle non-finite values.
Results may differ from the reference program's by a relative error of at most 0.0044.
Values may be sent and summed in bfloat16 or wider, within the bound.
No kernel may reach another device: no remote copies, remote signals or barrier semaphores. Data moves between devices by JAX's collectives and lax.ppermute only.
A program may use at most 128 MiB of HBM per device.

```python
import math
import jax
import jax.numpy as jnp
import numpy as np
from jax import lax

D = 7168
HID = 1024
TOK_DEV = 64
EXPERTS = 2
CAP = 40
TOKENS = 1024
N_PIPE = 2
N_EXPERT = 4


def block_levels(own_key, dims, pieces, least, largest):
    level, own = 1.0, jax.random.fold_in(own_key, 6)
    for dim, parts in pieces:
        steps = jnp.exp(jax.random.uniform(jax.random.fold_in(own, dim), (parts,), jnp.float32, least / len(pieces), largest / len(pieces)))
        level = level * jnp.repeat(steps, dims[dim] // parts).reshape([-1 if axis == dim else 1 for axis in range(len(dims))])
    return level


def shared_out(rng, own, number, rows, count, top, bound, slope):
    order = jax.random.permutation(rng, count)
    heavy_load, ordinary = load_shares(count, rows * top, bound, slope, True), load_shares(count, rows * top, bound, slope, False)
    places = jnp.arange(count)

    def named(tallies, offset_by):
        used = int((tallies > 0).sum())
        fixed = max(1, used // 4)
        shifted = fixed + (places - fixed + offset_by * (used - fixed)) % max(1, count - fixed)
        return jnp.zeros((count,), jnp.int32).at[order[jnp.where(places < fixed, places, shifted)]].set(jnp.asarray(tallies, jnp.int32))

    tallies = jnp.where(number % 4 == 0, named(heavy_load, number // 4), named(ordinary, number - number // 4 - 1))
    mixed = jax.random.permutation(jax.random.fold_in(own, 3), count)
    donor, receiver = mixed[0:count // 2 * 2:2], mixed[1:count // 2 * 2:2]
    slack = jnp.minimum(tallies[donor] - 1, bound - tallies[receiver]) // 2
    slack = jnp.where((donor == order[0]) | (receiver == order[0]) | (tallies[receiver] == 0), 0, jnp.maximum(slack, 0))
    shifted = jax.random.randint(jax.random.fold_in(own, 4), (count // 2,), 0, 1 << 20) % (slack + 1)
    tallies = tallies.at[donor].add(-shifted).at[receiver].add(shifted)
    items = jnp.searchsorted(jnp.cumsum(tallies), jnp.arange(rows * top), side="right").astype(jnp.int32)
    table = items.reshape(top, rows).T
    table = table[jax.random.permutation(jax.random.fold_in(own, 1), rows)]
    offset_by = jax.random.randint(jax.random.fold_in(own, 2), (rows, 1), 0, top)
    return jnp.take_along_axis(table, (jnp.arange(top)[None, :] + offset_by) % top, axis=1)


def load_shares(number_of, total, limit, slope, full):
    weights = [(1 << 20) // math.isqrt(standing ** slope) + 1 for standing in range(1, number_of + 1)]
    largest = limit if full else min(limit, max(-(-total // number_of), total * weights[0] // sum(weights)))
    least = 1 if total - largest >= number_of - 1 else 0
    counts, spare = [largest] + [least] * (number_of - 1), total - largest - least * (number_of - 1)
    while spare > 0:
        free = [i for i in range(1, number_of) if counts[i] < largest] or [i for i in range(1, number_of) if counts[i] < limit]
        mass, left = sum([weights[i] for i in free]), spare
        for i in free:
            addition = min(limit - counts[i], max(1, left * weights[i] // mass), spare)
            counts[i] = counts[i] + addition
            spare = spare - addition
    return np.array(counts)


def scatter_about(key, shape, scale, limit, split=(), kind=jnp.bfloat16):
    result = jax.random.normal(key, shape, jnp.float32) * scale
    if len(split) > 0:
        result = block_levels(key, shape, split, -0.22, 0.18) * result
    return jnp.clip(result, min=-limit, max=limit).astype(kind)


def setup_inputs(seed: int = 0) -> dict:
    key_of = jax.random.split(jax.random.key(seed), 11)
    x_forward = scatter_about(key_of[0], (N_PIPE, TOKENS, D), 1.0, 6.0, ((0, 2), (1, 16)))
    route_forward_keys = jax.random.split(jax.random.fold_in(key_of[1], 1), N_PIPE * TOKENS // TOK_DEV)
    route_forward_turns = jax.random.permutation(jax.random.fold_in(key_of[1], 3), N_PIPE * TOKENS // TOK_DEV)
    route_forward = jax.vmap(lambda own, number: shared_out(jax.random.fold_in(key_of[1], 2), own, number, TOK_DEV, EXPERTS, 1, CAP, 1))(route_forward_keys, route_forward_turns).reshape((N_PIPE, TOKENS, 1))
    prob_forward = jnp.clip(0.3 + 0.7 * jax.random.uniform(key_of[2], (N_PIPE, TOKENS), jnp.float32) ** block_levels(key_of[2], (N_PIPE, TOKENS), ((0, 2), (1, 16)), -0.2, 0.2), 0.3, 1.0)
    x_backward = scatter_about(key_of[3], (N_PIPE, TOKENS, D), 1.0, 6.0, ((0, 2), (1, 16)))
    route_backward_keys = jax.random.split(jax.random.fold_in(key_of[4], 1), N_PIPE * TOKENS // TOK_DEV)
    route_backward_turns = jax.random.permutation(jax.random.fold_in(key_of[4], 3), N_PIPE * TOKENS // TOK_DEV)
    route_backward = jax.vmap(lambda own, number: shared_out(jax.random.fold_in(key_of[4], 2), own, number, TOK_DEV, EXPERTS, 1, CAP, 1))(route_backward_keys, route_backward_turns).reshape((N_PIPE, TOKENS, 1))
    prob_backward = jnp.clip(0.3 + 0.7 * jax.random.uniform(key_of[5], (N_PIPE, TOKENS), jnp.float32) ** block_levels(key_of[5], (N_PIPE, TOKENS), ((0, 2), (1, 16)), -0.2, 0.2), 0.3, 1.0)
    grad_output = scatter_about(key_of[6], (N_PIPE, TOKENS, D), 1.0, 6.0, ((0, 2), (1, 16)))
    w_gate = scatter_about(key_of[7], (N_PIPE, N_EXPERT, D, HID // 2), D ** -0.5, 0.0625, ((0, 2), (1, 4), (3, 4)))
    w_up = scatter_about(key_of[8], (N_PIPE, N_EXPERT, D, HID // 2), D ** -0.5, 0.0625, ((0, 2), (1, 4), (3, 4)))
    w_down = scatter_about(key_of[9], (N_PIPE, N_EXPERT, HID // 2, D), HID ** -0.5, 0.1875, ((0, 2), (1, 4), (2, 4)))
    return dict(x_forward=x_forward, route_forward=route_forward, prob_forward=prob_forward, x_backward=x_backward, route_backward=route_backward, prob_backward=prob_backward, grad_output=grad_output, w_gate=w_gate, w_up=w_up, w_down=w_down)


def silu_parts(pre_gate):
    sigma_gate = jax.nn.sigmoid(pre_gate)
    return pre_gate * sigma_gate, sigma_gate


def contract_last(left_side, weights):
    return lax.dot_general(left_side, weights, (((1,), (1,)), ((), ())), preferred_element_type=jnp.float32)


def expert_pass(forward_rows, backward_rows, scaled_rows, gate_weight, up_weight, down_weight):
    gate_fwd = jnp.dot(forward_rows, gate_weight, preferred_element_type=jnp.float32)
    up_fwd = jnp.dot(forward_rows, up_weight, preferred_element_type=jnp.float32)
    silu_fwd, sigma_fwd = silu_parts(gate_fwd)
    hidden_fwd = (silu_fwd * up_fwd).astype(jnp.bfloat16)
    expert_out = jnp.dot(hidden_fwd, down_weight, preferred_element_type=jnp.float32)
    gate_bwd = jnp.dot(backward_rows, gate_weight, preferred_element_type=jnp.float32)
    up_bwd = jnp.dot(backward_rows, up_weight, preferred_element_type=jnp.float32)
    silu_bwd, sigma_bwd = silu_parts(gate_bwd)
    grad_hidden = contract_last(scaled_rows, down_weight)
    grad_gate = (grad_hidden * up_bwd * (sigma_bwd + silu_bwd * (1.0 - sigma_bwd))).astype(jnp.bfloat16)
    grad_up = (grad_hidden * silu_bwd).astype(jnp.bfloat16)
    grad_rows = contract_last(grad_gate, gate_weight) + contract_last(grad_up, up_weight)
    return expert_out, grad_rows


def positions(routes, block_count):
    blocks = routes[:, 0].reshape(block_count, TOK_DEV)
    route_hits = (blocks[:, :, None] == jnp.arange(EXPERTS, dtype=jnp.int32)[None, None, :]).astype(jnp.int32)
    before = jnp.cumsum(route_hits, axis=1) - route_hits
    slot_index = jnp.sum(before * route_hits, axis=2)
    block_owner = jnp.arange(block_count, dtype=jnp.int32)[:, None]
    return ((blocks * block_count + block_owner) * CAP + slot_index).reshape(TOKENS).astype(jnp.int32)


def gather_rows(values, position, block_count):
    gather_index = jnp.full((EXPERTS * block_count * CAP,), TOKENS, dtype=jnp.int32)
    gather_index = gather_index.at[position].set(jnp.arange(TOKENS, dtype=jnp.int32))
    padded = jnp.concatenate([values, jnp.zeros((1, D), values.dtype)], axis=0)
    return padded[gather_index].reshape(EXPERTS, block_count * CAP, D)


def reference(x_forward, route_forward, prob_forward, x_backward, route_backward, prob_backward, grad_output, w_gate, w_up, w_down):
    half_hidden = HID // 2
    block_count = TOKENS // TOK_DEV
    forward_list = []
    backward_list = []
    for section_num in range(N_PIPE):
        gate_full = w_gate[section_num].reshape(EXPERTS, 2, D, half_hidden).transpose(0, 2, 1, 3).reshape(EXPERTS, D, HID)
        up_full = w_up[section_num].reshape(EXPERTS, 2, D, half_hidden).transpose(0, 2, 1, 3).reshape(EXPERTS, D, HID)
        down_full = w_down[section_num].reshape(EXPERTS, HID, D)
        pos_fwd = positions(route_forward[section_num], block_count)
        pos_bwd = positions(route_backward[section_num], block_count)
        scaled_grad = (prob_backward[section_num][:, None] * grad_output[section_num].astype(jnp.float32)).astype(jnp.bfloat16)
        rows_fwd = gather_rows(x_forward[section_num], pos_fwd, block_count)
        rows_bwd = gather_rows(x_backward[section_num], pos_bwd, block_count)
        rows_scaled = gather_rows(scaled_grad, pos_bwd, block_count)
        expert_out, grad_rows = lax.map(lambda packed_args: expert_pass(*packed_args), (rows_fwd, rows_bwd, rows_scaled, gate_full, up_full, down_full))
        moved_fwd = expert_out.reshape(EXPERTS * block_count * CAP, D)[pos_fwd]
        moved_bwd = grad_rows.reshape(EXPERTS * block_count * CAP, D)[pos_bwd]
        layer_out = (x_forward[section_num].astype(jnp.float32) + prob_forward[section_num][:, None] * moved_fwd).astype(jnp.bfloat16)
        grad_in = (grad_output[section_num].astype(jnp.float32) + moved_bwd).astype(jnp.bfloat16)
        forward_list.append(layer_out)
        backward_list.append(grad_in)
    next_input = jnp.roll(jnp.stack(forward_list), 1, axis=0)
    next_grad = jnp.roll(jnp.stack(backward_list), -1, axis=0)
    return next_input, next_grad
```

```python
import functools

import jax
import jax.numpy as jnp
from jax import lax
from jax.experimental import pallas as pl
from jax.experimental.pallas import tpu as pltpu
from jax.sharding import PartitionSpec as P

BF16, F32 = jnp.bfloat16, jnp.float32
VMEM_LIMIT = 56 * 1024 * 1024


def contract_last(left_side, weights):
    return lax.dot_general(
        left_side, weights, (((1,), (1,)), ((), ())), preferred_element_type=F32
    )


def flipped(block, axis, stride):
    route = [(i, i ^ stride) for i in range(lax.axis_size(axis))]
    return lax.ppermute(block, axis, route)


def shifted(block, axis, distance):
    count = lax.axis_size(axis)
    return lax.ppermute(block, axis, [((i - distance) % count, i) for i in range(count)])


def chunk_of(width, most):
    best = 128
    for size in range(128, most + 1, 128):
        if width % size == 0:
            best = size
    return best


def own_columns(mask, hidden):
    column = lax.broadcasted_iota(jnp.int32, (mask.shape[0], hidden), 1)
    return (mask > 0) == (column < hidden // 2)


def joined(refs, axis):
    return jnp.concatenate([ref[...] for ref in refs], axis=axis)


def gates_kernel(pieces, x_ref, *refs):
    gates, ups = refs[:pieces], refs[pieces : 2 * pieces]
    c_ref, e_ref = refs[2 * pieces :]

    @pl.when(pl.program_id(0) == 0)
    def _():
        c_ref[...] = jnp.zeros_like(c_ref)
        e_ref[...] = jnp.zeros_like(e_ref)

    x = x_ref[...]
    c_ref[...] += jnp.dot(x, joined(gates, 1), preferred_element_type=F32)
    e_ref[...] += jnp.dot(x, joined(ups, 1), preferred_element_type=F32)


def gates_call(x, gates, ups):
    rows, width = x.shape
    pieces, hid = len(gates), gates[0].shape[1]
    chunk = chunk_of(width, 1024)
    hidden = pieces * hid
    weight_spec = pl.BlockSpec((chunk, hid), lambda i: (i, 0))
    return pl.pallas_call(
        functools.partial(gates_kernel, pieces),
        grid=(width // chunk,),
        in_specs=[pl.BlockSpec((rows, chunk), lambda i: (0, i))] + [weight_spec] * (2 * pieces),
        out_specs=[pl.BlockSpec((rows, hidden), lambda i: (0, 0))] * 2,
        out_shape=[jax.ShapeDtypeStruct((rows, hidden), F32)] * 2,
        compiler_params=pltpu.CompilerParams(vmem_limit_bytes=VMEM_LIMIT),
        cost_estimate=pl.CostEstimate(
            flops=4 * rows * width * hidden,
            bytes_accessed=2 * rows * width + 4 * width * hidden + 8 * rows * hidden,
            transcendentals=0,
        ),
    )(x, *gates, *ups)


def backward_kernel(pieces, steps, mask_ref, s_ref, c_ref, e_ref, *refs):
    downs, gates, ups = refs[:pieces], refs[pieces : 2 * pieces], refs[2 * pieces : 3 * pieces]
    out_ref, dh_ref, ga_ref, gb_ref = refs[3 * pieces :]
    step = pl.program_id(0)

    @pl.when(step == 0)
    def _():
        dh_ref[...] = jnp.zeros_like(dh_ref)

    @pl.when(step < steps)
    def _():
        dh_ref[...] += contract_last(s_ref[...], joined(downs, 0))

    @pl.when(step == steps - 1)
    def _():
        c, e, dh = c_ref[...], e_ref[...], dh_ref[...]
        s = jax.nn.sigmoid(c)
        silu = c * s
        keep = own_columns(mask_ref[...], c.shape[1])
        ga_ref[...] = jnp.where(keep, dh * e * (s + silu * (1.0 - s)), 0.0).astype(BF16)
        gb_ref[...] = jnp.where(keep, dh * silu, 0.0).astype(BF16)

    @pl.when(step >= steps)
    def _():
        total = contract_last(ga_ref[...], joined(gates, 1))
        total += contract_last(gb_ref[...], joined(ups, 1))
        out_ref[...] = total.astype(BF16)


def backward_call(mask, scaled, c, e, downs, gates, ups):
    rows, width = scaled.shape
    pieces, hid = len(gates), gates[0].shape[1]
    chunk = chunk_of(width, 1024)
    steps = width // chunk
    hidden = pieces * hid
    first = lambda i: jnp.minimum(i, steps - 1)
    second = lambda i: jnp.maximum(i - steps, 0)
    whole = lambda i: (0, 0)
    return pl.pallas_call(
        functools.partial(backward_kernel, pieces, steps),
        grid=(2 * steps,),
        in_specs=[
            pl.BlockSpec((rows, 1), whole),
            pl.BlockSpec((rows, chunk), lambda i: (0, first(i))),
            pl.BlockSpec((rows, hidden), whole),
            pl.BlockSpec((rows, hidden), whole),
        ]
        + [pl.BlockSpec((hid, chunk), lambda i: (0, first(i)))] * pieces
        + [pl.BlockSpec((chunk, hid), lambda i: (second(i), 0))] * (2 * pieces),
        out_specs=pl.BlockSpec((rows, chunk), lambda i: (0, second(i))),
        out_shape=jax.ShapeDtypeStruct((rows, width), BF16),
        scratch_shapes=[
            pltpu.VMEM((rows, hidden), F32),
            pltpu.VMEM((rows, hidden), BF16),
            pltpu.VMEM((rows, hidden), BF16),
        ],
        compiler_params=pltpu.CompilerParams(vmem_limit_bytes=VMEM_LIMIT),
        cost_estimate=pl.CostEstimate(
            flops=6 * rows * width * hidden,
            bytes_accessed=4 * rows * width + 6 * width * hidden + 8 * rows * hidden,
            transcendentals=rows * hidden,
        ),
    )(mask, scaled, c, e, *downs, *gates, *ups)


def forward_kernel(pieces, steps, mask_ref, x_ref, *refs):
    gates, ups, downs = refs[:pieces], refs[pieces : 2 * pieces], refs[2 * pieces : 3 * pieces]
    out_ref, a_ref, b_ref, hidden_ref = refs[3 * pieces :]
    step = pl.program_id(0)

    @pl.when(step == 0)
    def _():
        a_ref[...] = jnp.zeros_like(a_ref)
        b_ref[...] = jnp.zeros_like(b_ref)

    @pl.when(step < steps)
    def _():
        x = x_ref[...]
        a_ref[...] += jnp.dot(x, joined(gates, 1), preferred_element_type=F32)
        b_ref[...] += jnp.dot(x, joined(ups, 1), preferred_element_type=F32)

    @pl.when(step == steps - 1)
    def _():
        a, b = a_ref[...], b_ref[...]
        keep = own_columns(mask_ref[...], a.shape[1])
        hidden_ref[...] = jnp.where(keep, a * jax.nn.sigmoid(a) * b, 0.0).astype(BF16)

    @pl.when(step >= steps)
    def _():
        out_ref[...] = jnp.dot(
            hidden_ref[...], joined(downs, 0), preferred_element_type=F32
        ).astype(BF16)


def forward_call(mask, x, gates, ups, downs):
    rows, width = x.shape
    pieces, hid = len(gates), gates[0].shape[1]
    chunk = chunk_of(width, 1024)
    steps = width // chunk
    hidden = pieces * hid
    first = lambda i: jnp.minimum(i, steps - 1)
    second = lambda i: jnp.maximum(i - steps, 0)
    return pl.pallas_call(
        functools.partial(forward_kernel, pieces, steps),
        grid=(2 * steps,),
        in_specs=[
            pl.BlockSpec((rows, 1), lambda i: (0, 0)),
            pl.BlockSpec((rows, chunk), lambda i: (0, first(i))),
        ]
        + [pl.BlockSpec((chunk, hid), lambda i: (first(i), 0))] * (2 * pieces)
        + [pl.BlockSpec((hid, chunk), lambda i: (0, second(i)))] * pieces,
        out_specs=pl.BlockSpec((rows, chunk), lambda i: (0, second(i))),
        out_shape=jax.ShapeDtypeStruct((rows, width), BF16),
        scratch_shapes=[
            pltpu.VMEM((rows, hidden), F32),
            pltpu.VMEM((rows, hidden), F32),
            pltpu.VMEM((rows, hidden), BF16),
        ],
        compiler_params=pltpu.CompilerParams(vmem_limit_bytes=VMEM_LIMIT),
        cost_estimate=pl.CostEstimate(
            flops=6 * rows * width * hidden,
            bytes_accessed=4 * rows * width + 6 * width * hidden,
            transcendentals=rows * hidden,
        ),
    )(mask, x, *gates, *ups, *downs)


def summed_home(partial, axis):
    count, here = lax.axis_size(axis), lax.axis_index(axis)
    rows = partial.shape[0] // count

    def block(index):
        start = jnp.clip(index, 0, count - 1) * rows
        return lax.dynamic_slice_in_dim(partial, start, rows, 0).astype(F32)

    up, down = None, None
    for step in range(1, count):
        to_up, to_down = block(here + count - step), block(here - count + step)
        if up is not None:
            to_up, to_down = to_up + up.astype(F32), to_down + down.astype(F32)
        up = lax.ppermute(to_up.astype(BF16), axis, [(i, i + 1) for i in range(step)])
        down = lax.ppermute(
            to_down.astype(BF16), axis, [(i, i - 1) for i in range(count - step, count)]
        )
    return block(here) + up.astype(F32) + down.astype(F32)


def few_experts(
    x_forward,
    route_forward,
    prob_forward,
    x_backward,
    route_backward,
    prob_backward,
    grad_output,
    w_gate,
    w_up,
    w_down,
):
    tokens_here = x_forward.shape[1]
    expert_here = lax.axis_index("expert") // 2

    def with_neighbours(weight):
        across = flipped(weight, "expert", 2)
        return [weight, flipped(weight, "expert", 1), across, flipped(across, "expert", 1)]

    def gathered(rows):
        return lax.all_gather(rows, "dp", axis=0, tiled=True)

    routes = jnp.concatenate([route_forward[0], route_backward[0]], axis=1)
    mine = (gathered(routes) == expert_here).astype(F32)
    mask_fwd, mask_bwd = mine[:, 0:1], mine[:, 1:2]
    scaled_grad = (prob_backward[0][:, None] * grad_output[0].astype(F32)).astype(BF16)
    gates, ups, downs = (with_neighbours(w[0, 0]) for w in (w_gate, w_up, w_down))

    c, e = gates_call(gathered(x_backward[0]), gates, ups)
    partial_bwd = backward_call(mask_bwd, gathered(scaled_grad), c, e, downs, gates, ups)
    grad_in = (grad_output[0].astype(F32) + summed_home(partial_bwd, "dp")).astype(BF16)
    sent_bwd = shifted(grad_in, "pipe", -1)

    parts, sent_fwd = 2, []
    size = tokens_here // parts
    count = lax.axis_size("dp")
    for part in range(parts):
        rows = slice(part * size, (part + 1) * size)
        x_part = x_forward[0, rows]
        mask = mask_fwd.reshape(count, tokens_here, 1)[:, rows].reshape(count * size, 1)
        partial_fwd = forward_call(mask, gathered(x_part), gates, ups, downs)
        total = summed_home(partial_fwd, "dp")
        layer_out = (x_part.astype(F32) + prob_forward[0, rows][:, None] * total).astype(BF16)
        sent_fwd.append(shifted(layer_out, "pipe", 1))
    return (jnp.concatenate(sent_fwd, axis=0)[None], sent_bwd[None])


def from_partner(block, axis, stride):
    count = lax.axis_size(axis)
    route = []
    for low in range(count):
        high = low | 1 << stride
        if high != low and high < count:
            route += [(low, high), (high, low)]
    return lax.ppermute(block, axis, route)


def silu_parts(pre_gate):
    sigma_gate = jax.nn.sigmoid(pre_gate)
    return (pre_gate * sigma_gate, sigma_gate)


def expert_pass(forward_rows, backward_rows, scaled_rows, gate_weight, up_weight, down_weight):
    gate_fwd = jnp.dot(forward_rows, gate_weight, preferred_element_type=jnp.float32)
    up_fwd = jnp.dot(forward_rows, up_weight, preferred_element_type=jnp.float32)
    silu_fwd, sigma_fwd = silu_parts(gate_fwd)
    hidden_fwd = (silu_fwd * up_fwd).astype(jnp.bfloat16)
    expert_out = jnp.dot(hidden_fwd, down_weight, preferred_element_type=jnp.float32)
    gate_bwd = jnp.dot(backward_rows, gate_weight, preferred_element_type=jnp.float32)
    up_bwd = jnp.dot(backward_rows, up_weight, preferred_element_type=jnp.float32)
    silu_bwd, sigma_bwd = silu_parts(gate_bwd)
    grad_hidden = contract_last(scaled_rows, down_weight)
    grad_gate = (grad_hidden * up_bwd * (sigma_bwd + silu_bwd * (1.0 - sigma_bwd))).astype(
        jnp.bfloat16
    )
    grad_up = (grad_hidden * silu_bwd).astype(jnp.bfloat16)
    grad_rows = contract_last(grad_gate, gate_weight) + contract_last(grad_up, up_weight)
    return (expert_out, grad_rows)


def placing(routes, experts_here, capacity):
    route_hits = (routes[:, None] == jnp.arange(experts_here, dtype=jnp.int32)[None, :]).astype(
        jnp.int32
    )
    before = jnp.cumsum(route_hits, axis=0) - route_hits
    slot_index = jnp.sum(before * route_hits, axis=1)
    position = routes * capacity + slot_index
    selector = (
        position[None, :] == jnp.arange(experts_here * capacity, dtype=jnp.int32)[:, None]
    ).astype(jnp.bfloat16)
    return (position, selector)


def packing(selector, values):
    return jnp.dot(selector, values, preferred_element_type=jnp.float32).astype(jnp.bfloat16)


def many_experts(
    x_forward,
    route_forward,
    prob_forward,
    x_backward,
    route_backward,
    prob_backward,
    grad_output,
    w_gate,
    w_up,
    w_down,
):
    tokens_here = x_forward.shape[1]
    feature_width = x_forward.shape[2]
    groups = lax.axis_size("expert")
    experts_here = groups // 2
    capacity = min(tokens_here, (tokens_here * 5 + 4 * experts_here - 1) // (4 * experts_here))
    pair_side = lax.axis_index("expert") % 2
    gate_full, up_full, down_full = (
        lax.all_gather(w_gate[0, 0], "dp", axis=1, tiled=True),
        lax.all_gather(w_up[0, 0], "dp", axis=1, tiled=True),
        lax.all_gather(w_down[0, 0], "dp", axis=0, tiled=True),
    )
    pos_fwd, select_fwd = placing(route_forward[0, :, 0], experts_here, capacity)
    pos_bwd, select_bwd = placing(route_backward[0, :, 0], experts_here, capacity)
    scaled_grad = (prob_backward[0][:, None] * grad_output[0].astype(jnp.float32)).astype(
        jnp.bfloat16
    )
    stacked = jnp.stack(
        [
            packing(select_fwd, x_forward[0]),
            packing(select_bwd, x_backward[0]),
            packing(select_bwd, scaled_grad),
        ]
    )
    stacked = stacked.reshape(3, experts_here, capacity, feature_width)
    split_rows = stacked.reshape(3, experts_here, capacity, 2, feature_width // 2).transpose(
        0, 1, 3, 2, 4
    )
    split_rows = split_rows.reshape(3, groups, capacity, feature_width // 2)
    own_half = lax.all_to_all(split_rows, "expert", split_axis=1, concat_axis=1, tiled=True)
    partner_half = from_partner(own_half, "expert", 0)
    arrived = jnp.where(
        pair_side == 0,
        jnp.concatenate([own_half, partner_half], axis=3),
        jnp.concatenate([partner_half, own_half], axis=3),
    )
    expert_rows = arrived.reshape(3, groups * capacity, feature_width)
    expert_out, grad_rows = expert_pass(
        expert_rows[0], expert_rows[1], expert_rows[2], gate_full, up_full, down_full
    )
    results = jnp.stack([expert_out, grad_rows]).reshape(2, groups, capacity, feature_width)
    quarters = results.reshape(2, groups, capacity, 2, feature_width // 2)
    keep_part = jnp.where(pair_side == 0, quarters[:, :, :, 0], quarters[:, :, :, 1])
    give_part = jnp.where(pair_side == 0, quarters[:, :, :, 1], quarters[:, :, :, 0])
    finished = keep_part + from_partner(give_part.astype(jnp.bfloat16), "expert", 0).astype(
        give_part.dtype
    )
    returned = lax.all_to_all(finished, "expert", split_axis=1, concat_axis=1, tiled=True)
    combined = returned.reshape(2, experts_here, 2, capacity, feature_width // 2).transpose(
        0, 1, 3, 2, 4
    )
    combined = combined.reshape(2, experts_here, capacity, feature_width)
    flat_out = combined.reshape(2, experts_here * capacity, feature_width)
    moved_fwd = jnp.take(flat_out[0], pos_fwd, axis=0)
    moved_bwd = jnp.take(flat_out[1], pos_bwd, axis=0)
    layer_out = (x_forward[0].astype(jnp.float32) + prob_forward[0][:, None] * moved_fwd).astype(
        jnp.bfloat16
    )
    grad_in = (grad_output[0].astype(jnp.float32) + moved_bwd).astype(jnp.bfloat16)
    sent_fwd = shifted(layer_out, "pipe", 1)
    sent_bwd = shifted(grad_in, "pipe", -1)
    return (sent_fwd[None], sent_bwd[None])


def solution(mesh):
    few = mesh.shape["expert"] == 4
    return jax.shard_map(
        few_experts if few else many_experts,
        mesh=mesh,
        in_specs=(
            P("pipe", ("expert", "dp"), None),
            P("pipe", ("expert", "dp"), None),
            P("pipe", ("expert", "dp")),
            P("pipe", ("expert", "dp"), None),
            P("pipe", ("expert", "dp"), None),
            P("pipe", ("expert", "dp")),
            P("pipe", ("expert", "dp"), None),
            P("pipe", "expert", None, "dp"),
            P("pipe", "expert", None, "dp"),
            P("pipe", "expert", "dp", None),
        ),
        out_specs=(P("pipe", ("expert", "dp"), None), P("pipe", ("expert", "dp"), None)),
        check_vma=False,
    )
```

```python
import functools
import math

import jax
import jax.numpy as jnp
from jax import lax
from jax.experimental import pallas as pl
from jax.experimental.pallas import tpu as pltpu
from jax.sharding import PartitionSpec as P

BF16, F32 = jnp.bfloat16, jnp.float32
VMEM_LIMIT = 56 * 1024 * 1024
LAST_ROWS = 16


def contract_last(left_side, weights):
    return lax.dot_general(
        left_side, weights, (((1,), (1,)), ((), ())), preferred_element_type=F32
    )


def flipped(block, axis, stride):
    route = [(i, i ^ stride) for i in range(lax.axis_size(axis))]
    return lax.ppermute(block, axis, route)


def shifted(block, axis, distance):
    count = lax.axis_size(axis)
    return lax.ppermute(block, axis, [((i - distance) % count, i) for i in range(count)])


def chunk_of(width, most):
    best = 128
    for size in range(128, most + 1, 128):
        if width % size == 0:
            best = size
    return best


def own_columns(mask, hidden):
    column = lax.broadcasted_iota(jnp.int32, (mask.shape[0], hidden), 1)
    return (mask > 0) == (column < hidden // 2)


def joined(refs, axis):
    return jnp.concatenate([ref[...] for ref in refs], axis=axis)


def stacked(refs):
    return jnp.concatenate([ref[0] for ref in refs], axis=0)


def put_blocks(out_refs, total):
    rows = out_refs[0].shape[0]
    for index, ref in enumerate(out_refs):
        ref[...] = total[index * rows : (index + 1) * rows].astype(ref.dtype)


def turned_specs(count, begin, rows, chunk, column):
    unit = math.gcd(begin, rows)
    return [
        pl.BlockSpec(
            (1, unit, chunk),
            lambda i, at, turn=turn, piece=piece: (lax.rem(at[0] + turn, count), piece, column(i)),
        )
        for turn in range(count)
        for piece in range(begin // unit, (begin + rows) // unit)
    ]


def gates_kernel(inputs, pieces, at_ref, *refs):
    xs, refs = refs[:inputs], refs[inputs:]
    gates, ups = refs[:pieces], refs[pieces : 2 * pieces]
    c_ref, e_ref = refs[2 * pieces :]

    @pl.when(pl.program_id(0) == 0)
    def _():
        c_ref[...] = jnp.zeros_like(c_ref)
        e_ref[...] = jnp.zeros_like(e_ref)

    x = stacked(xs)
    c = jnp.dot(x, joined(gates, 1), preferred_element_type=F32)
    e = jnp.dot(x, joined(ups, 1), preferred_element_type=F32)
    c_ref[...] += c.reshape(c_ref.shape)
    e_ref[...] += e.reshape(e_ref.shape)


def gates_call(at, x, begin, rows, gates, ups):
    count, _, width = x.shape
    pieces, hid = len(gates), gates[0].shape[1]
    chunk = chunk_of(width, 1792)
    hidden = pieces * hid
    x_specs = turned_specs(count, begin, rows, chunk, lambda i: i)
    weight_spec = pl.BlockSpec((chunk, hid), lambda i, at: (i, 0))
    return pl.pallas_call(
        functools.partial(gates_kernel, len(x_specs), pieces),
        grid_spec=pltpu.PrefetchScalarGridSpec(
            num_scalar_prefetch=1,
            grid=(width // chunk,),
            in_specs=x_specs + [weight_spec] * (2 * pieces),
            out_specs=[pl.BlockSpec((count, rows, hidden), lambda i, at: (0, 0, 0))] * 2,
        ),
        out_shape=[jax.ShapeDtypeStruct((count, rows, hidden), F32)] * 2,
        compiler_params=pltpu.CompilerParams(vmem_limit_bytes=VMEM_LIMIT),
        cost_estimate=pl.CostEstimate(
            flops=4 * count * rows * width * hidden,
            bytes_accessed=2 * count * rows * width + 4 * width * hidden,
            transcendentals=0,
        ),
    )(at, *[x] * len(x_specs), *gates, *ups)


def backward_kernel(count, inputs, pieces, steps, at_ref, mask_ref, c_ref, e_ref, *refs):
    scaled, refs = refs[:inputs], refs[inputs:]
    downs, gates, ups = refs[:pieces], refs[pieces : 2 * pieces], refs[2 * pieces : 3 * pieces]
    outs = refs[3 * pieces : 3 * pieces + count]
    dh_ref, ga_ref, gb_ref = refs[3 * pieces + count :]
    step = pl.program_id(0)

    @pl.when(step == 0)
    def _():
        dh_ref[...] = jnp.zeros_like(dh_ref)

    @pl.when(step < steps)
    def _():
        dh_ref[...] += contract_last(stacked(scaled), joined(downs, 0))

    @pl.when(step == steps - 1)
    def _():
        dh = dh_ref[...]
        c, e = c_ref[...].reshape(dh.shape), e_ref[...].reshape(dh.shape)
        s = jax.nn.sigmoid(c)
        silu = c * s
        keep = own_columns(mask_ref[...], c.shape[1])
        ga_ref[...] = jnp.where(keep, dh * e * (s + silu * (1.0 - s)), 0.0).astype(BF16)
        gb_ref[...] = jnp.where(keep, dh * silu, 0.0).astype(BF16)

    @pl.when(step >= steps)
    def _():
        total = contract_last(ga_ref[...], joined(gates, 1))
        total += contract_last(gb_ref[...], joined(ups, 1))
        put_blocks(outs, total)


def backward_call(at, mask, scaled, begin, rows, part, c, e, downs, gates, ups):
    count, _, width = scaled.shape
    pieces, hid = len(gates), gates[0].shape[1]
    chunk = chunk_of(width, 1792)
    steps = width // chunk
    hidden = pieces * hid
    first = lambda i: jnp.minimum(i, steps - 1)
    second = lambda i: jnp.maximum(i - steps, 0)
    scaled_specs = turned_specs(count, begin, rows, chunk, first)
    pre_spec = pl.BlockSpec((count, rows, hidden), lambda i, at: (0, part, 0))
    out_spec = pl.BlockSpec((rows, chunk), lambda i, at: (0, second(i)))
    return pl.pallas_call(
        functools.partial(backward_kernel, count, len(scaled_specs), pieces, steps),
        grid_spec=pltpu.PrefetchScalarGridSpec(
            num_scalar_prefetch=1,
            grid=(2 * steps,),
            in_specs=[
                pl.BlockSpec((count * rows, 1), lambda i, at: (0, 0)),
                pre_spec,
                pre_spec,
            ]
            + scaled_specs
            + [pl.BlockSpec((hid, chunk), lambda i, at: (0, first(i)))] * pieces
            + [pl.BlockSpec((chunk, hid), lambda i, at: (second(i), 0))] * (2 * pieces),
            out_specs=[out_spec] * count,
            scratch_shapes=[
                pltpu.VMEM((count * rows, hidden), F32),
                pltpu.VMEM((count * rows, hidden), BF16),
                pltpu.VMEM((count * rows, hidden), BF16),
            ],
        ),
        out_shape=[jax.ShapeDtypeStruct((rows, width), F32)]
        + [jax.ShapeDtypeStruct((rows, width), BF16)] * (count - 1),
        compiler_params=pltpu.CompilerParams(vmem_limit_bytes=VMEM_LIMIT),
        cost_estimate=pl.CostEstimate(
            flops=6 * count * rows * width * hidden,
            bytes_accessed=4 * count * rows * width + 6 * width * hidden,
            transcendentals=count * rows * hidden,
        ),
    )(at, mask, c, e, *[scaled] * len(scaled_specs), *downs, *gates, *ups)


def forward_kernel(count, pieces, steps, mask_ref, own_ref, *refs):
    ups_in, downs_in, refs = refs[: count - 1], refs[count - 1 : 2 * count - 2], refs[2 * count - 2 :]
    gates, ups, downs = refs[:pieces], refs[pieces : 2 * pieces], refs[2 * pieces : 3 * pieces]
    outs = refs[3 * pieces : 3 * pieces + count]
    a_ref, b_ref, hidden_ref = refs[3 * pieces + count :]
    step = pl.program_id(0)

    @pl.when(step == 0)
    def _():
        a_ref[...] = jnp.zeros_like(a_ref)
        b_ref[...] = jnp.zeros_like(b_ref)

    @pl.when(step < steps)
    def _():
        blocks = [own_ref[...]] + [
            downs_in[away - 1][...] + ups_in[count - away - 1][...] for away in range(1, count)
        ]
        x = jnp.concatenate(blocks, axis=0)
        a_ref[...] += jnp.dot(x, joined(gates, 1), preferred_element_type=F32)
        b_ref[...] += jnp.dot(x, joined(ups, 1), preferred_element_type=F32)

    @pl.when(step == steps - 1)
    def _():
        a, b = a_ref[...], b_ref[...]
        keep = own_columns(mask_ref[...], a.shape[1])
        hidden_ref[...] = jnp.where(keep, a * jax.nn.sigmoid(a) * b, 0.0).astype(BF16)

    @pl.when(step >= steps)
    def _():
        total = jnp.dot(hidden_ref[...], joined(downs, 0), preferred_element_type=F32)
        put_blocks(outs, total)


def forward_call(mask, own, ups_in, downs_in, gates, ups, downs):
    rows, width = own.shape
    count = len(ups_in) + 1
    pieces, hid = len(gates), gates[0].shape[1]
    chunk = chunk_of(width, 1792)
    steps = width // chunk
    hidden = pieces * hid
    first = lambda i: jnp.minimum(i, steps - 1)
    second = lambda i: jnp.maximum(i - steps, 0)
    x_spec = pl.BlockSpec((rows, chunk), lambda i: (0, first(i)))
    return pl.pallas_call(
        functools.partial(forward_kernel, count, pieces, steps),
        grid=(2 * steps,),
        in_specs=[pl.BlockSpec((count * rows, 1), lambda i: (0, 0))]
        + [x_spec] * (2 * count - 1)
        + [pl.BlockSpec((chunk, hid), lambda i: (first(i), 0))] * (2 * pieces)
        + [pl.BlockSpec((hid, chunk), lambda i: (0, second(i)))] * pieces,
        out_specs=[pl.BlockSpec((rows, chunk), lambda i: (0, second(i)))] * count,
        out_shape=[jax.ShapeDtypeStruct((rows, width), F32)]
        + [jax.ShapeDtypeStruct((rows, width), BF16)] * (count - 1),
        scratch_shapes=[
            pltpu.VMEM((count * rows, hidden), F32),
            pltpu.VMEM((count * rows, hidden), F32),
            pltpu.VMEM((count * rows, hidden), BF16),
        ],
        compiler_params=pltpu.CompilerParams(vmem_limit_bytes=VMEM_LIMIT),
        cost_estimate=pl.CostEstimate(
            flops=6 * count * rows * width * hidden,
            bytes_accessed=6 * count * rows * width + 6 * width * hidden,
            transcendentals=count * rows * hidden,
        ),
    )(mask, own, *ups_in, *downs_in, *gates, *ups, *downs)


def after(value, *earlier):
    return lax.optimization_barrier((value,) + earlier)[0]


def sent_along(block, axis):
    count = lax.axis_size(axis)
    from_below, from_above = [block], [block]
    for step in range(1, count):
        up = [(i, i + 1) for i in range(step - 1, count - 1)]
        down = [(i, i - 1) for i in range(1, count - step + 1)]
        from_below.append(lax.ppermute(from_below[-1], axis, up))
        from_above.append(lax.ppermute(from_above[-1], axis, down))
    return from_below[1:], from_above[1:]


def steps_home(blocks, axis):
    count = lax.axis_size(axis)
    up, down = None, None
    for step in range(1, count):
        to_up, to_down = blocks[count - step], blocks[step]
        if up is not None:
            to_up = (to_up.astype(F32) + up.astype(F32)).astype(BF16)
            to_down = (to_down.astype(F32) + down.astype(F32)).astype(BF16)
        up = lax.ppermute(to_up, axis, [(i, i + 1) for i in range(step)])
        down = lax.ppermute(to_down, axis, [(i, i - 1) for i in range(count - step, count)])
        yield up, down


def summed(block, arrived):
    for part in arrived:
        block = block + part.astype(F32)
    return block


def sent_home(blocks, axis):
    total = blocks[0]
    for away in range(1, len(blocks)):
        total = total + shifted(blocks[away], axis, away).astype(F32)
    return total


def few_experts(
    x_forward,
    route_forward,
    prob_forward,
    x_backward,
    route_backward,
    prob_backward,
    grad_output,
    w_gate,
    w_up,
    w_down,
):
    tokens_here = x_forward.shape[1]
    expert_here = lax.axis_index("expert") // 2
    count = lax.axis_size("dp")
    at = lax.axis_index("dp").reshape(1).astype(jnp.int32)

    last = min(LAST_ROWS, tokens_here // 2)
    early = tokens_here - last
    scaled_grad = (prob_backward[0][:, None] * grad_output[0].astype(F32)).astype(BF16)
    routes = jnp.concatenate([route_forward[0], route_backward[0]], axis=1)
    bundle = jnp.concatenate([x_backward[0], scaled_grad[:early]], axis=0)
    x_fwd, bundle, routes, scaled_last = lax.optimization_barrier(
        (x_forward[0], bundle, routes, scaled_grad[early:])
    )
    bundle = lax.all_gather(bundle, "dp")
    routes = jnp.stack([routes] + [shifted(routes, "dp", -away) for away in range(1, count)])
    mine = (routes == expert_here).astype(F32)
    mask_fwd, mask_bwd = mine[:, :, 0:1], mine[:, :, 1:2]

    def neighbours(weight, across):
        return [weight, flipped(weight, "expert", 1), across, flipped(across, "expert", 1)]

    gate, up, down = w_gate[0, 0], w_up[0, 0], w_down[0, 0]
    gate_across, up_across, down_across = (flipped(w, "expert", 2) for w in (gate, up, down))
    from_below, from_above = sent_along(x_fwd, "dp")
    gate_across = after(gate_across, from_below[0], from_above[0])
    up_across = after(up_across, from_below[1], from_above[1])
    down_across = after(down_across, from_below[2], from_above[2])
    gates = neighbours(gate, gate_across)
    ups = neighbours(up, up_across)
    downs = neighbours(down, down_across)

    partial_fwd = forward_call(
        mask_fwd.reshape(count * tokens_here, 1), x_fwd, from_below, from_above, gates, ups, downs
    )
    home_fwd = list(steps_home(partial_fwd, "dp"))
    scaled_last = lax.all_gather(after(scaled_last, bundle), "dp")
    bundle = after(bundle, *home_fwd[0])
    c, e = gates_call(at, bundle, 0, tokens_here, gates, ups)
    c = after(c, *home_fwd[1])
    mask_early = mask_bwd[:, :early].reshape(count * early, 1)
    blocks_early = backward_call(
        at, mask_early, bundle, tokens_here, early, 0, c, e, downs, gates, ups
    )
    home_early = list(steps_home(blocks_early, "dp"))
    total_fwd = summed(partial_fwd[0], home_fwd[-1])
    layer_out = (x_forward[0].astype(F32) + prob_forward[0][:, None] * total_fwd).astype(BF16)
    sent_fwd = shifted(layer_out, "pipe", 1)

    mask_last = mask_bwd[:, early:].reshape(count * last, 1)
    scaled_last = after(scaled_last, *home_early[0], *home_fwd[-1])
    blocks = backward_call(
        at, mask_last, scaled_last, 0, last, early // last, c, e, downs, gates, ups
    )
    total_early = summed(blocks_early[0], home_early[-1])
    total_last = sent_home(blocks, "dp")
    sent_bwd = []
    for rows, total in ((slice(0, early), total_early), (slice(early, None), total_last)):
        grad_in = (grad_output[0, rows].astype(F32) + total).astype(BF16)
        sent_bwd.append(shifted(grad_in, "pipe", -1))
    return (sent_fwd[None], jnp.concatenate(sent_bwd, axis=0)[None])


def from_partner(block, axis, stride):
    count = lax.axis_size(axis)
    route = []
    for low in range(count):
        high = low | 1 << stride
        if high != low and high < count:
            route += [(low, high), (high, low)]
    return lax.ppermute(block, axis, route)


def silu_parts(pre_gate):
    sigma_gate = jax.nn.sigmoid(pre_gate)
    return (pre_gate * sigma_gate, sigma_gate)


def expert_pass(forward_rows, backward_rows, scaled_rows, gate_weight, up_weight, down_weight):
    gate_fwd = jnp.dot(forward_rows, gate_weight, preferred_element_type=jnp.float32)
    up_fwd = jnp.dot(forward_rows, up_weight, preferred_element_type=jnp.float32)
    silu_fwd, sigma_fwd = silu_parts(gate_fwd)
    hidden_fwd = (silu_fwd * up_fwd).astype(jnp.bfloat16)
    expert_out = jnp.dot(hidden_fwd, down_weight, preferred_element_type=jnp.float32)
    gate_bwd = jnp.dot(backward_rows, gate_weight, preferred_element_type=jnp.float32)
    up_bwd = jnp.dot(backward_rows, up_weight, preferred_element_type=jnp.float32)
    silu_bwd, sigma_bwd = silu_parts(gate_bwd)
    grad_hidden = contract_last(scaled_rows, down_weight)
    grad_gate = (grad_hidden * up_bwd * (sigma_bwd + silu_bwd * (1.0 - sigma_bwd))).astype(
        jnp.bfloat16
    )
    grad_up = (grad_hidden * silu_bwd).astype(jnp.bfloat16)
    grad_rows = contract_last(grad_gate, gate_weight) + contract_last(grad_up, up_weight)
    return (expert_out, grad_rows)


def placing(routes, experts_here, capacity):
    route_hits = (routes[:, None] == jnp.arange(experts_here, dtype=jnp.int32)[None, :]).astype(
        jnp.int32
    )
    before = jnp.cumsum(route_hits, axis=0) - route_hits
    slot_index = jnp.sum(before * route_hits, axis=1)
    position = routes * capacity + slot_index
    selector = (
        position[None, :] == jnp.arange(experts_here * capacity, dtype=jnp.int32)[:, None]
    ).astype(jnp.bfloat16)
    return (position, selector)


def packing(selector, values):
    return jnp.dot(selector, values, preferred_element_type=jnp.float32).astype(jnp.bfloat16)


def many_experts(
    x_forward,
    route_forward,
    prob_forward,
    x_backward,
    route_backward,
    prob_backward,
    grad_output,
    w_gate,
    w_up,
    w_down,
):
    tokens_here = x_forward.shape[1]
    feature_width = x_forward.shape[2]
    groups = lax.axis_size("expert")
    experts_here = groups // 2
    capacity = min(tokens_here, (tokens_here * 5 + 4 * experts_here - 1) // (4 * experts_here))
    pair_side = lax.axis_index("expert") % 2
    gate_full, up_full, down_full = (
        lax.all_gather(w_gate[0, 0], "dp", axis=1, tiled=True),
        lax.all_gather(w_up[0, 0], "dp", axis=1, tiled=True),
        lax.all_gather(w_down[0, 0], "dp", axis=0, tiled=True),
    )
    pos_fwd, select_fwd = placing(route_forward[0, :, 0], experts_here, capacity)
    pos_bwd, select_bwd = placing(route_backward[0, :, 0], experts_here, capacity)
    scaled_grad = (prob_backward[0][:, None] * grad_output[0].astype(jnp.float32)).astype(
        jnp.bfloat16
    )
    stacked = jnp.stack(
        [
            packing(select_fwd, x_forward[0]),
            packing(select_bwd, x_backward[0]),
            packing(select_bwd, scaled_grad),
        ]
    )
    stacked = stacked.reshape(3, experts_here, capacity, feature_width)
    split_rows = stacked.reshape(3, experts_here, capacity, 2, feature_width // 2).transpose(
        0, 1, 3, 2, 4
    )
    split_rows = split_rows.reshape(3, groups, capacity, feature_width // 2)
    own_half = lax.all_to_all(split_rows, "expert", split_axis=1, concat_axis=1, tiled=True)
    partner_half = from_partner(own_half, "expert", 0)
    arrived = jnp.where(
        pair_side == 0,
        jnp.concatenate([own_half, partner_half], axis=3),
        jnp.concatenate([partner_half, own_half], axis=3),
    )
    expert_rows = arrived.reshape(3, groups * capacity, feature_width)
    expert_out, grad_rows = expert_pass(
        expert_rows[0], expert_rows[1], expert_rows[2], gate_full, up_full, down_full
    )
    results = jnp.stack([expert_out, grad_rows]).reshape(2, groups, capacity, feature_width)
    quarters = results.reshape(2, groups, capacity, 2, feature_width // 2)
    keep_part = jnp.where(pair_side == 0, quarters[:, :, :, 0], quarters[:, :, :, 1])
    give_part = jnp.where(pair_side == 0, quarters[:, :, :, 1], quarters[:, :, :, 0])
    finished = keep_part + from_partner(give_part.astype(jnp.bfloat16), "expert", 0).astype(
        give_part.dtype
    )
    returned = lax.all_to_all(finished, "expert", split_axis=1, concat_axis=1, tiled=True)
    combined = returned.reshape(2, experts_here, 2, capacity, feature_width // 2).transpose(
        0, 1, 3, 2, 4
    )
    combined = combined.reshape(2, experts_here, capacity, feature_width)
    flat_out = combined.reshape(2, experts_here * capacity, feature_width)
    moved_fwd = jnp.take(flat_out[0], pos_fwd, axis=0)
    moved_bwd = jnp.take(flat_out[1], pos_bwd, axis=0)
    layer_out = (x_forward[0].astype(jnp.float32) + prob_forward[0][:, None] * moved_fwd).astype(
        jnp.bfloat16
    )
    grad_in = (grad_output[0].astype(jnp.float32) + moved_bwd).astype(jnp.bfloat16)
    sent_fwd = shifted(layer_out, "pipe", 1)
    sent_bwd = shifted(grad_in, "pipe", -1)
    return (sent_fwd[None], sent_bwd[None])


def solution(mesh):
    few = mesh.shape["expert"] == 4
    return jax.shard_map(
        few_experts if few else many_experts,
        mesh=mesh,
        in_specs=(
            P("pipe", ("expert", "dp"), None),
            P("pipe", ("expert", "dp"), None),
            P("pipe", ("expert", "dp")),
            P("pipe", ("expert", "dp"), None),
            P("pipe", ("expert", "dp"), None),
            P("pipe", ("expert", "dp")),
            P("pipe", ("expert", "dp"), None),
            P("pipe", "expert", None, "dp"),
            P("pipe", "expert", None, "dp"),
            P("pipe", "expert", "dp", None),
        ),
        out_specs=(P("pipe", ("expert", "dp"), None), P("pipe", ("expert", "dp"), None)),
        check_vma=False,
    )
```

```python
import functools
import math

import jax
import jax.numpy as jnp
from jax import lax
from jax.experimental import pallas as pl
from jax.experimental.pallas import tpu as pltpu
from jax.sharding import PartitionSpec as P

BF16, F32 = jnp.bfloat16, jnp.float32
VMEM_LIMIT = 20 * 1024 * 1024
LAST_ROWS = 32


def contract_last(left_side, weights):
    return lax.dot_general(
        left_side, weights, (((1,), (1,)), ((), ())), preferred_element_type=F32
    )


def flipped(block, axis, stride):
    route = [(i, i ^ stride) for i in range(lax.axis_size(axis))]
    return lax.ppermute(block, axis, route)


def shifted(block, axis, distance):
    count = lax.axis_size(axis)
    return lax.ppermute(block, axis, [((i - distance) % count, i) for i in range(count)])


def chunk_of(width, most):
    best = 128
    for size in range(128, most + 1, 128):
        if width % size == 0:
            best = size
    return best


def own_columns(mask, hidden):
    column = lax.broadcasted_iota(jnp.int32, (mask.shape[0], hidden), 1)
    return (mask > 0) == (column < hidden // 2)


def joined(refs, axis):
    return jnp.concatenate([ref[...] for ref in refs], axis=axis)


def stacked(refs):
    return jnp.concatenate([ref[0] for ref in refs], axis=0)


def put_blocks(out_refs, total):
    rows = out_refs[0].shape[0]
    for index, ref in enumerate(out_refs):
        ref[...] = total[index * rows : (index + 1) * rows].astype(ref.dtype)


def turned_specs(count, begin, rows, chunk, column):
    unit = math.gcd(begin, rows)
    return [
        pl.BlockSpec(
            (1, unit, chunk),
            lambda i, at, turn=turn, piece=piece: (lax.rem(at[0] + turn, count), piece, column(i)),
        )
        for turn in range(count)
        for piece in range(begin // unit, (begin + rows) // unit)
    ]


def gates_kernel(inputs, pieces, at_ref, *refs):
    xs, refs = refs[:inputs], refs[inputs:]
    gates, ups = refs[:pieces], refs[pieces : 2 * pieces]
    c_ref, e_ref = refs[2 * pieces :]

    @pl.when(pl.program_id(0) == 0)
    def _():
        c_ref[...] = jnp.zeros_like(c_ref)
        e_ref[...] = jnp.zeros_like(e_ref)

    x = stacked(xs)
    c = jnp.dot(x, joined(gates, 1), preferred_element_type=F32)
    e = jnp.dot(x, joined(ups, 1), preferred_element_type=F32)
    c_ref[...] += c.reshape(c_ref.shape)
    e_ref[...] += e.reshape(e_ref.shape)


def gates_call(at, x, begin, rows, gates, ups):
    count, _, width = x.shape
    pieces, hid = len(gates), gates[0].shape[1]
    chunk = chunk_of(width, 1024)
    hidden = pieces * hid
    x_specs = turned_specs(count, begin, rows, chunk, lambda i: i)
    weight_spec = pl.BlockSpec((chunk, hid), lambda i, at: (i, 0))
    return pl.pallas_call(
        functools.partial(gates_kernel, len(x_specs), pieces),
        grid_spec=pltpu.PrefetchScalarGridSpec(
            num_scalar_prefetch=1,
            grid=(width // chunk,),
            in_specs=x_specs + [weight_spec] * (2 * pieces),
            out_specs=[pl.BlockSpec((count, rows, hidden), lambda i, at: (0, 0, 0))] * 2,
        ),
        out_shape=[jax.ShapeDtypeStruct((count, rows, hidden), F32)] * 2,
        compiler_params=pltpu.CompilerParams(vmem_limit_bytes=VMEM_LIMIT),
        cost_estimate=pl.CostEstimate(
            flops=4 * count * rows * width * hidden,
            bytes_accessed=2 * count * rows * width + 4 * width * hidden,
            transcendentals=0,
        ),
    )(at, *[x] * len(x_specs), *gates, *ups)


def backward_kernel(count, inputs, pieces, steps, at_ref, mask_ref, c_ref, e_ref, *refs):
    scaled, refs = refs[:inputs], refs[inputs:]
    downs, gates, ups = refs[:pieces], refs[pieces : 2 * pieces], refs[2 * pieces : 3 * pieces]
    outs = refs[3 * pieces : 3 * pieces + count]
    dh_ref, ga_ref, gb_ref = refs[3 * pieces + count :]
    step = pl.program_id(0)

    @pl.when(step == 0)
    def _():
        dh_ref[...] = jnp.zeros_like(dh_ref)

    @pl.when(step < steps)
    def _():
        dh_ref[...] += contract_last(stacked(scaled), joined(downs, 0))

    @pl.when(step == steps - 1)
    def _():
        dh = dh_ref[...]
        c, e = c_ref[...].reshape(dh.shape), e_ref[...].reshape(dh.shape)
        s = jax.nn.sigmoid(c)
        silu = c * s
        keep = own_columns(mask_ref[...], c.shape[1])
        ga_ref[...] = jnp.where(keep, dh * e * (s + silu * (1.0 - s)), 0.0).astype(BF16)
        gb_ref[...] = jnp.where(keep, dh * silu, 0.0).astype(BF16)

    @pl.when(step >= steps)
    def _():
        total = contract_last(ga_ref[...], joined(gates, 1))
        total += contract_last(gb_ref[...], joined(ups, 1))
        put_blocks(outs, total)


def backward_call(at, mask, scaled, begin, rows, part, c, e, downs, gates, ups):
    count, _, width = scaled.shape
    pieces, hid = len(gates), gates[0].shape[1]
    chunk = chunk_of(width, 1024)
    steps = width // chunk
    hidden = pieces * hid
    first = lambda i: jnp.minimum(i, steps - 1)
    second = lambda i: jnp.maximum(i - steps, 0)
    scaled_specs = turned_specs(count, begin, rows, chunk, first)
    pre_spec = pl.BlockSpec((count, rows, hidden), lambda i, at: (0, part, 0))
    out_spec = pl.BlockSpec((rows, chunk), lambda i, at: (0, second(i)))
    return pl.pallas_call(
        functools.partial(backward_kernel, count, len(scaled_specs), pieces, steps),
        grid_spec=pltpu.PrefetchScalarGridSpec(
            num_scalar_prefetch=1,
            grid=(2 * steps,),
            in_specs=[
                pl.BlockSpec((count * rows, 1), lambda i, at: (0, 0)),
                pre_spec,
                pre_spec,
            ]
            + scaled_specs
            + [pl.BlockSpec((hid, chunk), lambda i, at: (0, first(i)))] * pieces
            + [pl.BlockSpec((chunk, hid), lambda i, at: (second(i), 0))] * (2 * pieces),
            out_specs=[out_spec] * count,
            scratch_shapes=[
                pltpu.VMEM((count * rows, hidden), F32),
                pltpu.VMEM((count * rows, hidden), BF16),
                pltpu.VMEM((count * rows, hidden), BF16),
            ],
        ),
        out_shape=[jax.ShapeDtypeStruct((rows, width), F32)]
        + [jax.ShapeDtypeStruct((rows, width), BF16)] * (count - 1),
        compiler_params=pltpu.CompilerParams(vmem_limit_bytes=VMEM_LIMIT),
        cost_estimate=pl.CostEstimate(
            flops=6 * count * rows * width * hidden,
            bytes_accessed=4 * count * rows * width + 6 * width * hidden,
            transcendentals=count * rows * hidden,
        ),
    )(at, mask, c, e, *[scaled] * len(scaled_specs), *downs, *gates, *ups)


def forward_kernel(count, pieces, steps, mask_ref, own_ref, *refs):
    ups_in, downs_in, refs = refs[: count - 1], refs[count - 1 : 2 * count - 2], refs[2 * count - 2 :]
    gates, ups, downs = refs[:pieces], refs[pieces : 2 * pieces], refs[2 * pieces : 3 * pieces]
    outs = refs[3 * pieces : 3 * pieces + count]
    a_ref, b_ref, hidden_ref = refs[3 * pieces + count :]
    step = pl.program_id(0)

    @pl.when(step == 0)
    def _():
        a_ref[...] = jnp.zeros_like(a_ref)
        b_ref[...] = jnp.zeros_like(b_ref)

    @pl.when(step < steps)
    def _():
        blocks = [own_ref[...]] + [
            downs_in[away - 1][...] + ups_in[count - away - 1][...] for away in range(1, count)
        ]
        x = jnp.concatenate(blocks, axis=0)
        a_ref[...] += jnp.dot(x, joined(gates, 1), preferred_element_type=F32)
        b_ref[...] += jnp.dot(x, joined(ups, 1), preferred_element_type=F32)

    @pl.when(step == steps - 1)
    def _():
        a, b = a_ref[...], b_ref[...]
        keep = own_columns(mask_ref[...], a.shape[1])
        hidden_ref[...] = jnp.where(keep, a * jax.nn.sigmoid(a) * b, 0.0).astype(BF16)

    @pl.when(step >= steps)
    def _():
        total = jnp.dot(hidden_ref[...], joined(downs, 0), preferred_element_type=F32)
        put_blocks(outs, total)


def forward_call(mask, own, ups_in, downs_in, gates, ups, downs):
    rows, width = own.shape
    count = len(ups_in) + 1
    pieces, hid = len(gates), gates[0].shape[1]
    chunk = chunk_of(width, 1024)
    steps = width // chunk
    hidden = pieces * hid
    first = lambda i: jnp.minimum(i, steps - 1)
    second = lambda i: jnp.maximum(i - steps, 0)
    x_spec = pl.BlockSpec((rows, chunk), lambda i: (0, first(i)))
    return pl.pallas_call(
        functools.partial(forward_kernel, count, pieces, steps),
        grid=(2 * steps,),
        in_specs=[pl.BlockSpec((count * rows, 1), lambda i: (0, 0))]
        + [x_spec] * (2 * count - 1)
        + [pl.BlockSpec((chunk, hid), lambda i: (first(i), 0))] * (2 * pieces)
        + [pl.BlockSpec((hid, chunk), lambda i: (0, second(i)))] * pieces,
        out_specs=[pl.BlockSpec((rows, chunk), lambda i: (0, second(i)))] * count,
        out_shape=[jax.ShapeDtypeStruct((rows, width), F32)]
        + [jax.ShapeDtypeStruct((rows, width), BF16)] * (count - 1),
        scratch_shapes=[
            pltpu.VMEM((count * rows, hidden), F32),
            pltpu.VMEM((count * rows, hidden), F32),
            pltpu.VMEM((count * rows, hidden), BF16),
        ],
        compiler_params=pltpu.CompilerParams(vmem_limit_bytes=VMEM_LIMIT),
        cost_estimate=pl.CostEstimate(
            flops=6 * count * rows * width * hidden,
            bytes_accessed=6 * count * rows * width + 6 * width * hidden,
            transcendentals=count * rows * hidden,
        ),
    )(mask, own, *ups_in, *downs_in, *gates, *ups, *downs)


def after(value, *earlier):
    return lax.optimization_barrier((value,) + earlier)[0]


def hop(below, above, axis, step):
    count = lax.axis_size(axis)
    up = [(i, i + 1) for i in range(step - 1, count - 1)]
    down = [(i, i - 1) for i in range(1, count - step + 1)]
    return lax.ppermute(below, axis, up), lax.ppermute(above, axis, down)


def steps_home(blocks, axis):
    count = lax.axis_size(axis)
    sends, arrivals = [], []
    for step in range(1, count):
        pair = (blocks[count - step], blocks[step])
        if arrivals:
            pair = tuple(
                (own.astype(F32) + other.astype(F32)).astype(BF16)
                for own, other in zip(pair, arrivals[-1])
            )
        up = lax.ppermute(pair[0], axis, [(i, i + 1) for i in range(step)])
        down = lax.ppermute(pair[1], axis, [(i, i - 1) for i in range(count - step, count)])
        sends.append(pair)
        arrivals.append((up, down))
    return sends, arrivals


def summed(block, arrived):
    for part in arrived:
        block = block + part.astype(F32)
    return block


def sent_home(blocks, axis):
    total = blocks[0]
    for away in range(1, len(blocks)):
        total = total + shifted(blocks[away], axis, away).astype(F32)
    return total


def few_experts(
    x_forward,
    route_forward,
    prob_forward,
    x_backward,
    route_backward,
    prob_backward,
    grad_output,
    w_gate,
    w_up,
    w_down,
):
    tokens_here = x_forward.shape[1]
    expert_here = lax.axis_index("expert") // 2
    count = lax.axis_size("dp")
    at = lax.axis_index("dp").reshape(1).astype(jnp.int32)

    last = min(LAST_ROWS, tokens_here // 2)
    early = tokens_here - last
    scaled_grad = (prob_backward[0][:, None] * grad_output[0].astype(F32)).astype(BF16)
    routes = jnp.concatenate([route_forward[0], route_backward[0]], axis=1)
    bundle = jnp.concatenate([x_backward[0], scaled_grad[:early]], axis=0)
    x_fwd, bundle, routes, scaled_last = lax.optimization_barrier(
        (x_forward[0], bundle, routes, scaled_grad[early:])
    )
    bundle = lax.all_gather(bundle, "dp")
    routes = jnp.stack([routes] + [shifted(routes, "dp", -away) for away in range(1, count)])
    mine = (routes == expert_here).astype(F32)
    mask_fwd, mask_bwd = mine[:, :, 0:1], mine[:, :, 1:2]

    own = [w_gate[0, 0], w_up[0, 0], w_down[0, 0]]
    across = [flipped(weight, "expert", 2) for weight in own]
    own_flips = [flipped(weight, "expert", 1) for weight in own]
    x_sent = jnp.where(jnp.min(routes) >= 0, x_fwd, jnp.zeros_like(x_fwd))
    from_below, from_above = [], []
    earlier = [[], own_flips, [flipped(across[0], "expert", 1)]]
    across_flips = [earlier[2][0]] + [flipped(weight, "expert", 1) for weight in across[1:]]
    below, above = x_sent, x_sent
    for step in range(1, count):
        if step > 1:
            below, above = after(below, *earlier[step - 1]), after(above, *earlier[step - 1])
        below, above = hop(below, above, "dp", step)
        from_below.append(below)
        from_above.append(above)
    gates, ups, downs = zip(own, own_flips, across, across_flips)

    partial_fwd = forward_call(
        mask_fwd.reshape(count * tokens_here, 1), x_fwd, from_below, from_above, gates, ups, downs
    )
    sends_fwd, arrivals_fwd = steps_home(partial_fwd, "dp")
    scaled_last = lax.all_gather(scaled_last, "dp")
    bundle = after(bundle, *sends_fwd[1])
    c, e = gates_call(at, bundle, 0, tokens_here, gates, ups)
    mask_early = mask_bwd[:, :early].reshape(count * early, 1)
    blocks_early = backward_call(
        at, mask_early, bundle, tokens_here, early, 0, c, e, downs, gates, ups
    )
    sends_early, arrivals_early = steps_home(blocks_early, "dp")
    total_fwd = summed(partial_fwd[0], arrivals_fwd[-1])
    layer_out = (x_forward[0].astype(F32) + prob_forward[0][:, None] * total_fwd).astype(BF16)
    sent_fwd = shifted(layer_out, "pipe", 1)

    mask_last = mask_bwd[:, early:].reshape(count * last, 1)
    scaled_last = after(scaled_last, *sends_early[1], *sends_fwd[-1])
    blocks = backward_call(
        at, mask_last, scaled_last, 0, last, early // last, c, e, downs, gates, ups
    )
    total_early = summed(blocks_early[0], arrivals_early[-1])
    total_last = sent_home(blocks, "dp")
    sent_bwd = []
    for rows, total in ((slice(0, early), total_early), (slice(early, None), total_last)):
        grad_in = (grad_output[0, rows].astype(F32) + total).astype(BF16)
        sent_bwd.append(shifted(grad_in, "pipe", -1))
    return (sent_fwd[None], jnp.concatenate(sent_bwd, axis=0)[None])


def from_partner(block, axis, stride):
    count = lax.axis_size(axis)
    route = []
    for low in range(count):
        high = low | 1 << stride
        if high != low and high < count:
            route += [(low, high), (high, low)]
    return lax.ppermute(block, axis, route)


def silu_parts(pre_gate):
    sigma_gate = jax.nn.sigmoid(pre_gate)
    return (pre_gate * sigma_gate, sigma_gate)


def expert_pass(forward_rows, backward_rows, scaled_rows, gate_weight, up_weight, down_weight):
    gate_fwd = jnp.dot(forward_rows, gate_weight, preferred_element_type=jnp.float32)
    up_fwd = jnp.dot(forward_rows, up_weight, preferred_element_type=jnp.float32)
    silu_fwd, sigma_fwd = silu_parts(gate_fwd)
    hidden_fwd = (silu_fwd * up_fwd).astype(jnp.bfloat16)
    expert_out = jnp.dot(hidden_fwd, down_weight, preferred_element_type=jnp.float32)
    gate_bwd = jnp.dot(backward_rows, gate_weight, preferred_element_type=jnp.float32)
    up_bwd = jnp.dot(backward_rows, up_weight, preferred_element_type=jnp.float32)
    silu_bwd, sigma_bwd = silu_parts(gate_bwd)
    grad_hidden = contract_last(scaled_rows, down_weight)
    grad_gate = (grad_hidden * up_bwd * (sigma_bwd + silu_bwd * (1.0 - sigma_bwd))).astype(
        jnp.bfloat16
    )
    grad_up = (grad_hidden * silu_bwd).astype(jnp.bfloat16)
    grad_rows = contract_last(grad_gate, gate_weight) + contract_last(grad_up, up_weight)
    return (expert_out, grad_rows)


def placing(routes, experts_here, capacity):
    route_hits = (routes[:, None] == jnp.arange(experts_here, dtype=jnp.int32)[None, :]).astype(
        jnp.int32
    )
    before = jnp.cumsum(route_hits, axis=0) - route_hits
    slot_index = jnp.sum(before * route_hits, axis=1)
    position = routes * capacity + slot_index
    selector = (
        position[None, :] == jnp.arange(experts_here * capacity, dtype=jnp.int32)[:, None]
    ).astype(jnp.bfloat16)
    return (position, selector)


def packing(selector, values):
    return jnp.dot(selector, values, preferred_element_type=jnp.float32).astype(jnp.bfloat16)


def many_experts(
    x_forward,
    route_forward,
    prob_forward,
    x_backward,
    route_backward,
    prob_backward,
    grad_output,
    w_gate,
    w_up,
    w_down,
):
    tokens_here = x_forward.shape[1]
    feature_width = x_forward.shape[2]
    groups = lax.axis_size("expert")
    experts_here = groups // 2
    capacity = min(tokens_here, (tokens_here * 5 + 4 * experts_here - 1) // (4 * experts_here))
    pair_side = lax.axis_index("expert") % 2
    gate_full, up_full, down_full = (
        lax.all_gather(w_gate[0, 0], "dp", axis=1, tiled=True),
        lax.all_gather(w_up[0, 0], "dp", axis=1, tiled=True),
        lax.all_gather(w_down[0, 0], "dp", axis=0, tiled=True),
    )
    pos_fwd, select_fwd = placing(route_forward[0, :, 0], experts_here, capacity)
    pos_bwd, select_bwd = placing(route_backward[0, :, 0], experts_here, capacity)
    scaled_grad = (prob_backward[0][:, None] * grad_output[0].astype(jnp.float32)).astype(
        jnp.bfloat16
    )
    stacked = jnp.stack(
        [
            packing(select_fwd, x_forward[0]),
            packing(select_bwd, x_backward[0]),
            packing(select_bwd, scaled_grad),
        ]
    )
    stacked = stacked.reshape(3, experts_here, capacity, feature_width)
    split_rows = stacked.reshape(3, experts_here, capacity, 2, feature_width // 2).transpose(
        0, 1, 3, 2, 4
    )
    split_rows = split_rows.reshape(3, groups, capacity, feature_width // 2)
    own_half = lax.all_to_all(split_rows, "expert", split_axis=1, concat_axis=1, tiled=True)
    partner_half = from_partner(own_half, "expert", 0)
    arrived = jnp.where(
        pair_side == 0,
        jnp.concatenate([own_half, partner_half], axis=3),
        jnp.concatenate([partner_half, own_half], axis=3),
    )
    expert_rows = arrived.reshape(3, groups * capacity, feature_width)
    expert_out, grad_rows = expert_pass(
        expert_rows[0], expert_rows[1], expert_rows[2], gate_full, up_full, down_full
    )
    results = jnp.stack([expert_out, grad_rows]).reshape(2, groups, capacity, feature_width)
    quarters = results.reshape(2, groups, capacity, 2, feature_width // 2)
    keep_part = jnp.where(pair_side == 0, quarters[:, :, :, 0], quarters[:, :, :, 1])
    give_part = jnp.where(pair_side == 0, quarters[:, :, :, 1], quarters[:, :, :, 0])
    finished = keep_part + from_partner(give_part.astype(jnp.bfloat16), "expert", 0).astype(
        give_part.dtype
    )
    returned = lax.all_to_all(finished, "expert", split_axis=1, concat_axis=1, tiled=True)
    combined = returned.reshape(2, experts_here, 2, capacity, feature_width // 2).transpose(
        0, 1, 3, 2, 4
    )
    combined = combined.reshape(2, experts_here, capacity, feature_width)
    flat_out = combined.reshape(2, experts_here * capacity, feature_width)
    moved_fwd = jnp.take(flat_out[0], pos_fwd, axis=0)
    moved_bwd = jnp.take(flat_out[1], pos_bwd, axis=0)
    layer_out = (x_forward[0].astype(jnp.float32) + prob_forward[0][:, None] * moved_fwd).astype(
        jnp.bfloat16
    )
    grad_in = (grad_output[0].astype(jnp.float32) + moved_bwd).astype(jnp.bfloat16)
    sent_fwd = shifted(layer_out, "pipe", 1)
    sent_bwd = shifted(grad_in, "pipe", -1)
    return (sent_fwd[None], sent_bwd[None])


def solution(mesh):
    few = mesh.shape["expert"] == 4
    return jax.shard_map(
        few_experts if few else many_experts,
        mesh=mesh,
        in_specs=(
            P("pipe", ("expert", "dp"), None),
            P("pipe", ("expert", "dp"), None),
            P("pipe", ("expert", "dp")),
            P("pipe", ("expert", "dp"), None),
            P("pipe", ("expert", "dp"), None),
            P("pipe", ("expert", "dp")),
            P("pipe", ("expert", "dp"), None),
            P("pipe", "expert", None, "dp"),
            P("pipe", "expert", None, "dp"),
            P("pipe", "expert", "dp", None),
        ),
        out_specs=(P("pipe", ("expert", "dp"), None), P("pipe", ("expert", "dp"), None)),
        check_vma=False,
    )
```

```python
import functools
import math

import jax
import jax.numpy as jnp
from jax import lax
from jax.experimental import pallas as pl
from jax.experimental.pallas import tpu as pltpu
from jax.sharding import PartitionSpec as P

BF16, F32 = jnp.bfloat16, jnp.float32
VMEM_LIMIT = 20 * 1024 * 1024
LAST_ROWS = 32


def contract_last(left_side, weights):
    return lax.dot_general(
        left_side, weights, (((1,), (1,)), ((), ())), preferred_element_type=F32
    )


def flipped(block, axis, stride):
    route = [(i, i ^ stride) for i in range(lax.axis_size(axis))]
    return lax.ppermute(block, axis, route)


def shifted(block, axis, distance):
    count = lax.axis_size(axis)
    return lax.ppermute(block, axis, [((i - distance) % count, i) for i in range(count)])


def chunk_of(width, most):
    best = 128
    for size in range(128, most + 1, 128):
        if width % size == 0:
            best = size
    return best


def own_columns(mask, hidden):
    column = lax.broadcasted_iota(jnp.int32, (mask.shape[0], hidden), 1)
    return (mask > 0) == (column < hidden // 2)


def joined(refs, axis, index=None):
    pick = (lambda ref: ref[...]) if index is None else (lambda ref: ref[index])
    return jnp.concatenate([pick(ref) for ref in refs], axis=axis)


def gathered_rows(refs):
    return jnp.concatenate([ref[0] for ref in refs], axis=0)


def chained_rows(refs):
    others = len(refs) // 2
    own, below, above = refs[0][...], refs[1 : 1 + others], refs[1 + others :]
    return jnp.concatenate(
        [own] + [above[away][...] + below[others - 1 - away][...] for away in range(others)],
        axis=0,
    )


def put_blocks(out_refs, total):
    rows = out_refs[0].shape[0]
    for index, ref in enumerate(out_refs):
        ref[...] = total[index * rows : (index + 1) * rows].astype(ref.dtype)


def gathered_input(x, begin, rows):
    count, unit = x.shape[0], math.gcd(begin, rows)
    arrays, specs = [], []
    for turn in range(count):
        for piece in range(begin // unit, (begin + rows) // unit):
            arrays.append(x)
            specs.append(
                lambda chunk, column, turn=turn, piece=piece: pl.BlockSpec(
                    (1, unit, chunk),
                    lambda i, at: (lax.rem(at[0] + turn, count), piece, column(i)),
                )
            )
    return gathered_rows, arrays, specs, rows


def chained_input(own, from_below, from_above):
    rows = own.shape[0]
    spec = lambda chunk, column: pl.BlockSpec((rows, chunk), lambda i, at: (0, column(i)))
    arrays = [own, *from_below, *from_above]
    return chained_rows, arrays, [spec] * len(arrays), rows


def gates_kernel(read, inputs, pieces, at_ref, *refs):
    xs, gate_ups = refs[:inputs], refs[inputs : inputs + pieces]
    c_ref, e_ref = refs[inputs + pieces :]

    @pl.when(pl.program_id(0) == 0)
    def _():
        c_ref[...] = jnp.zeros_like(c_ref)
        e_ref[...] = jnp.zeros_like(e_ref)

    x = read(xs)
    c = jnp.dot(x, joined(gate_ups, 1, 0), preferred_element_type=F32)
    e = jnp.dot(x, joined(gate_ups, 1, 1), preferred_element_type=F32)
    c_ref[...] += c.reshape(c_ref.shape)
    e_ref[...] += e.reshape(e_ref.shape)


def gates_call(at, count, x_input, gate_ups):
    read, arrays, specs, rows = x_input
    width = arrays[0].shape[-1]
    pieces, hid = len(gate_ups), gate_ups[0].shape[2]
    chunk = chunk_of(width, 1024)
    hidden = pieces * hid
    weight_spec = pl.BlockSpec((2, chunk, hid), lambda i, at: (0, i, 0))
    return pl.pallas_call(
        functools.partial(gates_kernel, read, len(arrays), pieces),
        grid_spec=pltpu.PrefetchScalarGridSpec(
            num_scalar_prefetch=1,
            grid=(width // chunk,),
            in_specs=[spec(chunk, lambda i: i) for spec in specs] + [weight_spec] * pieces,
            out_specs=[pl.BlockSpec((count, rows, hidden), lambda i, at: (0, 0, 0))] * 2,
        ),
        out_shape=[jax.ShapeDtypeStruct((count, rows, hidden), F32)] * 2,
        compiler_params=pltpu.CompilerParams(vmem_limit_bytes=VMEM_LIMIT),
        cost_estimate=pl.CostEstimate(
            flops=4 * count * rows * width * hidden,
            bytes_accessed=2 * count * rows * width + 4 * width * hidden,
            transcendentals=0,
        ),
    )(at, *arrays, *gate_ups)


def backward_kernel(read, inputs, count, pieces, steps, at_ref, mask_ref, c_ref, e_ref, *refs):
    scaled, refs = refs[:inputs], refs[inputs:]
    downs, gate_ups = refs[:pieces], refs[pieces : 2 * pieces]
    outs = refs[2 * pieces : 2 * pieces + count]
    dh_ref, ga_ref, gb_ref = refs[2 * pieces + count :]
    step = pl.program_id(0)

    @pl.when(step == 0)
    def _():
        dh_ref[...] = jnp.zeros_like(dh_ref)

    @pl.when(step < steps)
    def _():
        dh_ref[...] += contract_last(read(scaled), joined(downs, 0))

    @pl.when(step == steps - 1)
    def _():
        dh = dh_ref[...]
        c, e = c_ref[...].reshape(dh.shape), e_ref[...].reshape(dh.shape)
        s = jax.nn.sigmoid(c)
        silu = c * s
        keep = own_columns(mask_ref[...], c.shape[1])
        ga_ref[...] = jnp.where(keep, dh * e * (s + silu * (1.0 - s)), 0.0).astype(BF16)
        gb_ref[...] = jnp.where(keep, dh * silu, 0.0).astype(BF16)

    @pl.when(step >= steps)
    def _():
        total = contract_last(ga_ref[...], joined(gate_ups, 1, 0))
        total += contract_last(gb_ref[...], joined(gate_ups, 1, 1))
        put_blocks(outs, total)


def backward_call(at, count, mask, scaled_input, part, c, e, downs, gate_ups):
    read, arrays, specs, rows = scaled_input
    width = arrays[0].shape[-1]
    pieces, hid = len(downs), downs[0].shape[0]
    chunk = chunk_of(width, 1024)
    steps = width // chunk
    hidden = pieces * hid
    first = lambda i: jnp.minimum(i, steps - 1)
    second = lambda i: jnp.maximum(i - steps, 0)
    pre_spec = pl.BlockSpec((count, rows, hidden), lambda i, at: (0, part, 0))
    out_spec = pl.BlockSpec((rows, chunk), lambda i, at: (0, second(i)))
    return pl.pallas_call(
        functools.partial(backward_kernel, read, len(arrays), count, pieces, steps),
        grid_spec=pltpu.PrefetchScalarGridSpec(
            num_scalar_prefetch=1,
            grid=(2 * steps,),
            in_specs=[
                pl.BlockSpec((count * rows, 1), lambda i, at: (0, 0)),
                pre_spec,
                pre_spec,
            ]
            + [spec(chunk, first) for spec in specs]
            + [pl.BlockSpec((hid, chunk), lambda i, at: (0, first(i)))] * pieces
            + [pl.BlockSpec((2, chunk, hid), lambda i, at: (0, second(i), 0))] * pieces,
            out_specs=[out_spec] * count,
            scratch_shapes=[
                pltpu.VMEM((count * rows, hidden), F32),
                pltpu.VMEM((count * rows, hidden), BF16),
                pltpu.VMEM((count * rows, hidden), BF16),
            ],
        ),
        out_shape=[jax.ShapeDtypeStruct((rows, width), F32)]
        + [jax.ShapeDtypeStruct((rows, width), BF16)] * (count - 1),
        compiler_params=pltpu.CompilerParams(vmem_limit_bytes=VMEM_LIMIT),
        cost_estimate=pl.CostEstimate(
            flops=6 * count * rows * width * hidden,
            bytes_accessed=4 * count * rows * width + 6 * width * hidden,
            transcendentals=count * rows * hidden,
        ),
    )(at, mask, c, e, *arrays, *downs, *gate_ups)


def forward_kernel(read, inputs, count, pieces, steps, at_ref, mask_ref, *refs):
    xs, refs = refs[:inputs], refs[inputs:]
    gate_ups, downs = refs[:pieces], refs[pieces : 2 * pieces]
    outs = refs[2 * pieces : 2 * pieces + count]
    a_ref, b_ref, hidden_ref = refs[2 * pieces + count :]
    step = pl.program_id(0)

    @pl.when(step == 0)
    def _():
        a_ref[...] = jnp.zeros_like(a_ref)
        b_ref[...] = jnp.zeros_like(b_ref)

    @pl.when(step < steps)
    def _():
        x = read(xs)
        a_ref[...] += jnp.dot(x, joined(gate_ups, 1, 0), preferred_element_type=F32)
        b_ref[...] += jnp.dot(x, joined(gate_ups, 1, 1), preferred_element_type=F32)

    @pl.when(step == steps - 1)
    def _():
        a, b = a_ref[...], b_ref[...]
        keep = own_columns(mask_ref[...], a.shape[1])
        hidden_ref[...] = jnp.where(keep, a * jax.nn.sigmoid(a) * b, 0.0).astype(BF16)

    @pl.when(step >= steps)
    def _():
        total = jnp.dot(hidden_ref[...], joined(downs, 0), preferred_element_type=F32)
        put_blocks(outs, total)


def forward_call(at, count, mask, x_input, gate_ups, downs):
    read, arrays, specs, rows = x_input
    width = arrays[0].shape[-1]
    pieces, hid = len(downs), downs[0].shape[0]
    chunk = chunk_of(width, 1024)
    steps = width // chunk
    hidden = pieces * hid
    first = lambda i: jnp.minimum(i, steps - 1)
    second = lambda i: jnp.maximum(i - steps, 0)
    return pl.pallas_call(
        functools.partial(forward_kernel, read, len(arrays), count, pieces, steps),
        grid_spec=pltpu.PrefetchScalarGridSpec(
            num_scalar_prefetch=1,
            grid=(2 * steps,),
            in_specs=[pl.BlockSpec((count * rows, 1), lambda i, at: (0, 0))]
            + [spec(chunk, first) for spec in specs]
            + [pl.BlockSpec((2, chunk, hid), lambda i, at: (0, first(i), 0))] * pieces
            + [pl.BlockSpec((hid, chunk), lambda i, at: (0, second(i)))] * pieces,
            out_specs=[pl.BlockSpec((rows, chunk), lambda i, at: (0, second(i)))] * count,
            scratch_shapes=[
                pltpu.VMEM((count * rows, hidden), F32),
                pltpu.VMEM((count * rows, hidden), F32),
                pltpu.VMEM((count * rows, hidden), BF16),
            ],
        ),
        out_shape=[jax.ShapeDtypeStruct((rows, width), F32)]
        + [jax.ShapeDtypeStruct((rows, width), BF16)] * (count - 1),
        compiler_params=pltpu.CompilerParams(vmem_limit_bytes=VMEM_LIMIT),
        cost_estimate=pl.CostEstimate(
            flops=6 * count * rows * width * hidden,
            bytes_accessed=6 * count * rows * width + 6 * width * hidden,
            transcendentals=count * rows * hidden,
        ),
    )(at, mask, *arrays, *gate_ups, *downs)


def after(value, *earlier):
    return lax.optimization_barrier((value, earlier))[0]


def hop(below, above, axis, step):
    count = lax.axis_size(axis)
    up = [(i, i + 1) for i in range(step - 1, count - 1)]
    down = [(i, i - 1) for i in range(1, count - step + 1)]
    return lax.ppermute(below, axis, up), lax.ppermute(above, axis, down)


def summands(blocks, step, arrived):
    pair = (blocks[len(blocks) - step], blocks[step])
    if arrived is None:
        return pair
    return tuple(
        (own.astype(F32) + other.astype(F32)).astype(BF16) for own, other in zip(pair, arrived)
    )


def step_home(pair, axis, step):
    count = lax.axis_size(axis)
    up = lax.ppermute(pair[0], axis, [(i, i + 1) for i in range(step)])
    down = lax.ppermute(pair[1], axis, [(i, i - 1) for i in range(count - step, count)])
    return up, down


def summed(block, arrived):
    for part in arrived:
        block = block + part.astype(F32)
    return block


def sent_home(blocks, axis):
    total = blocks[0]
    for away in range(1, len(blocks)):
        total = total + shifted(blocks[away], axis, away).astype(F32)
    return total


def few_experts(
    x_forward,
    route_forward,
    prob_forward,
    x_backward,
    route_backward,
    prob_backward,
    grad_output,
    w_gate,
    w_up,
    w_down,
):
    tokens_here = x_forward.shape[1]
    expert_here = lax.axis_index("expert") // 2
    count = lax.axis_size("dp")
    at = lax.axis_index("dp").reshape(1).astype(jnp.int32)

    last = min(LAST_ROWS, tokens_here // 2)
    early = tokens_here - last
    scaled_grad = (prob_backward[0][:, None] * grad_output[0].astype(F32)).astype(BF16)
    routes = jnp.concatenate([route_forward[0], route_backward[0]], axis=1)
    gate_up, down = jnp.concatenate([w_gate[0], w_up[0]], axis=0), w_down[0, 0]
    bundle = jnp.concatenate([x_backward[0], scaled_grad[:early]], axis=0)
    bundle, routes, scaled_last = lax.optimization_barrier((bundle, routes, scaled_grad[early:]))
    bundle = lax.all_gather(bundle, "dp")
    routes = jnp.stack([routes] + [shifted(routes, "dp", -away) for away in range(1, count)])
    mine = (routes == expert_here).astype(F32)
    mask_fwd, mask_bwd = mine[:, :, 0:1], mine[:, :, 1:2]

    across_gate_up, across_down = flipped(gate_up, "expert", 2), flipped(down, "expert", 2)
    x_sent = jnp.where(jnp.min(routes) >= 0, x_forward[0], jnp.zeros_like(x_forward[0]))
    hops_x = [(x_sent, x_sent)]
    for step in range(1, count):
        hops_x.append(hop(*hops_x[-1], "dp", step))
    gate_ups = [gate_up, flipped(after(gate_up, *hops_x[1]), "expert", 1)]
    gate_ups += [across_gate_up, flipped(across_gate_up, "expert", 1)]
    downs = [down, flipped(down, "expert", 1), across_down, flipped(across_down, "expert", 1)]
    late = after(scaled_last, *hops_x[2])
    hops_last = [(late, late)]
    hops_last.append(hop(*hops_last[-1], "dp", 1))

    from_below, from_above = zip(*hops_x[1:])
    partial_fwd = forward_call(
        at,
        count,
        mask_fwd.reshape(count * tokens_here, 1),
        chained_input(x_forward[0], from_below, from_above),
        gate_ups,
        downs,
    )
    late = [after(rows, partial_fwd[1]) for rows in hops_last[-1]]
    for step in range(2, count):
        hops_last.append(hop(*(late if step == 2 else hops_last[-1]), "dp", step))
    arrived_fwd = step_home(summands(partial_fwd, 1, None), "dp", 1)
    sent_home_fwd = summands(partial_fwd, 2, arrived_fwd)
    arrived_fwd = step_home(sent_home_fwd, "dp", 2)
    bundle = after(bundle, sent_home_fwd, hops_last[-1])
    c, e = gates_call(at, count, gathered_input(bundle, 0, tokens_here), gate_ups)
    mask_early = mask_bwd[:, :early].reshape(count * early, 1)
    scaled_early = gathered_input(bundle, tokens_here, early)
    blocks_early = backward_call(
        at, count, mask_early, scaled_early, 0, c, e, downs, gate_ups
    )

    sent_home_fwd = summands(partial_fwd, 3, after(arrived_fwd, blocks_early[1]))
    arrived_fwd = step_home(sent_home_fwd, "dp", 3)
    arrived_early = step_home(summands(blocks_early, 1, None), "dp", 1)
    from_below, from_above = zip(*hops_last[1:])
    mask_last = after(mask_bwd[:, early:].reshape(count * last, 1), sent_home_fwd)
    scaled_last = chained_input(scaled_last, from_below, from_above)
    blocks_last = backward_call(
        at, count, mask_last, scaled_last, early // last, c, e, downs, gate_ups
    )

    arrived_early, arrived_fwd = after((arrived_early, arrived_fwd), blocks_last[1])
    total_fwd = summed(partial_fwd[0], arrived_fwd)
    layer_out = (x_forward[0].astype(F32) + prob_forward[0][:, None] * total_fwd).astype(BF16)
    sent_fwd = shifted(layer_out, "pipe", 1)
    for step in range(2, count):
        arrived_early = step_home(summands(blocks_early, step, arrived_early), "dp", step)
    total_early = summed(blocks_early[0], arrived_early)
    total_last = sent_home(blocks_last, "dp")
    sent_bwd = []
    for rows, total in ((slice(0, early), total_early), (slice(early, None), total_last)):
        grad_in = (grad_output[0, rows].astype(F32) + total).astype(BF16)
        sent_bwd.append(shifted(grad_in, "pipe", -1))
    return (sent_fwd[None], jnp.concatenate(sent_bwd, axis=0)[None])


def from_partner(block, axis, stride):
    count = lax.axis_size(axis)
    route = []
    for low in range(count):
        high = low | 1 << stride
        if high != low and high < count:
            route += [(low, high), (high, low)]
    return lax.ppermute(block, axis, route)


def silu_parts(pre_gate):
    sigma_gate = jax.nn.sigmoid(pre_gate)
    return (pre_gate * sigma_gate, sigma_gate)


def expert_pass(forward_rows, backward_rows, scaled_rows, gate_weight, up_weight, down_weight):
    gate_fwd = jnp.dot(forward_rows, gate_weight, preferred_element_type=jnp.float32)
    up_fwd = jnp.dot(forward_rows, up_weight, preferred_element_type=jnp.float32)
    silu_fwd, sigma_fwd = silu_parts(gate_fwd)
    hidden_fwd = (silu_fwd * up_fwd).astype(jnp.bfloat16)
    expert_out = jnp.dot(hidden_fwd, down_weight, preferred_element_type=jnp.float32)
    gate_bwd = jnp.dot(backward_rows, gate_weight, preferred_element_type=jnp.float32)
    up_bwd = jnp.dot(backward_rows, up_weight, preferred_element_type=jnp.float32)
    silu_bwd, sigma_bwd = silu_parts(gate_bwd)
    grad_hidden = contract_last(scaled_rows, down_weight)
    grad_gate = (grad_hidden * up_bwd * (sigma_bwd + silu_bwd * (1.0 - sigma_bwd))).astype(
        jnp.bfloat16
    )
    grad_up = (grad_hidden * silu_bwd).astype(jnp.bfloat16)
    grad_rows = contract_last(grad_gate, gate_weight) + contract_last(grad_up, up_weight)
    return (expert_out, grad_rows)


def placing(routes, experts_here, capacity):
    route_hits = (routes[:, None] == jnp.arange(experts_here, dtype=jnp.int32)[None, :]).astype(
        jnp.int32
    )
    before = jnp.cumsum(route_hits, axis=0) - route_hits
    slot_index = jnp.sum(before * route_hits, axis=1)
    position = routes * capacity + slot_index
    selector = (
        position[None, :] == jnp.arange(experts_here * capacity, dtype=jnp.int32)[:, None]
    ).astype(jnp.bfloat16)
    return (position, selector)


def packing(selector, values):
    return jnp.dot(selector, values, preferred_element_type=jnp.float32).astype(jnp.bfloat16)


def many_experts(
    x_forward,
    route_forward,
    prob_forward,
    x_backward,
    route_backward,
    prob_backward,
    grad_output,
    w_gate,
    w_up,
    w_down,
):
    tokens_here = x_forward.shape[1]
    feature_width = x_forward.shape[2]
    groups = lax.axis_size("expert")
    experts_here = groups // 2
    capacity = min(tokens_here, (tokens_here * 5 + 4 * experts_here - 1) // (4 * experts_here))
    pair_side = lax.axis_index("expert") % 2
    gate_full, up_full, down_full = (
        lax.all_gather(w_gate[0, 0], "dp", axis=1, tiled=True),
        lax.all_gather(w_up[0, 0], "dp", axis=1, tiled=True),
        lax.all_gather(w_down[0, 0], "dp", axis=0, tiled=True),
    )
    pos_fwd, select_fwd = placing(route_forward[0, :, 0], experts_here, capacity)
    pos_bwd, select_bwd = placing(route_backward[0, :, 0], experts_here, capacity)
    scaled_grad = (prob_backward[0][:, None] * grad_output[0].astype(jnp.float32)).astype(
        jnp.bfloat16
    )
    stacked = jnp.stack(
        [
            packing(select_fwd, x_forward[0]),
            packing(select_bwd, x_backward[0]),
            packing(select_bwd, scaled_grad),
        ]
    )
    stacked = stacked.reshape(3, experts_here, capacity, feature_width)
    split_rows = stacked.reshape(3, experts_here, capacity, 2, feature_width // 2).transpose(
        0, 1, 3, 2, 4
    )
    split_rows = split_rows.reshape(3, groups, capacity, feature_width // 2)
    own_half = lax.all_to_all(split_rows, "expert", split_axis=1, concat_axis=1, tiled=True)
    partner_half = from_partner(own_half, "expert", 0)
    arrived = jnp.where(
        pair_side == 0,
        jnp.concatenate([own_half, partner_half], axis=3),
        jnp.concatenate([partner_half, own_half], axis=3),
    )
    expert_rows = arrived.reshape(3, groups * capacity, feature_width)
    expert_out, grad_rows = expert_pass(
        expert_rows[0], expert_rows[1], expert_rows[2], gate_full, up_full, down_full
    )
    results = jnp.stack([expert_out, grad_rows]).reshape(2, groups, capacity, feature_width)
    quarters = results.reshape(2, groups, capacity, 2, feature_width // 2)
    keep_part = jnp.where(pair_side == 0, quarters[:, :, :, 0], quarters[:, :, :, 1])
    give_part = jnp.where(pair_side == 0, quarters[:, :, :, 1], quarters[:, :, :, 0])
    finished = keep_part + from_partner(give_part.astype(jnp.bfloat16), "expert", 0).astype(
        give_part.dtype
    )
    returned = lax.all_to_all(finished, "expert", split_axis=1, concat_axis=1, tiled=True)
    combined = returned.reshape(2, experts_here, 2, capacity, feature_width // 2).transpose(
        0, 1, 3, 2, 4
    )
    combined = combined.reshape(2, experts_here, capacity, feature_width)
    flat_out = combined.reshape(2, experts_here * capacity, feature_width)
    moved_fwd = jnp.take(flat_out[0], pos_fwd, axis=0)
    moved_bwd = jnp.take(flat_out[1], pos_bwd, axis=0)
    layer_out = (x_forward[0].astype(jnp.float32) + prob_forward[0][:, None] * moved_fwd).astype(
        jnp.bfloat16
    )
    grad_in = (grad_output[0].astype(jnp.float32) + moved_bwd).astype(jnp.bfloat16)
    sent_fwd = shifted(layer_out, "pipe", 1)
    sent_bwd = shifted(grad_in, "pipe", -1)
    return (sent_fwd[None], sent_bwd[None])


def solution(mesh):
    few = mesh.shape["expert"] == 4
    return jax.shard_map(
        few_experts if few else many_experts,
        mesh=mesh,
        in_specs=(
            P("pipe", ("expert", "dp"), None),
            P("pipe", ("expert", "dp"), None),
            P("pipe", ("expert", "dp")),
            P("pipe", ("expert", "dp"), None),
            P("pipe", ("expert", "dp"), None),
            P("pipe", ("expert", "dp")),
            P("pipe", ("expert", "dp"), None),
            P("pipe", "expert", None, "dp"),
            P("pipe", "expert", None, "dp"),
            P("pipe", "expert", "dp", None),
        ),
        out_specs=(P("pipe", ("expert", "dp"), None), P("pipe", ("expert", "dp"), None)),
        check_vma=False,
    )
```

```python
import functools
import math

import jax
import jax.numpy as jnp
from jax import lax
from jax.experimental import pallas as pl
from jax.experimental.pallas import tpu as pltpu
from jax.sharding import PartitionSpec as P

BF16, F32 = jnp.bfloat16, jnp.float32
VMEM_LIMIT = 56 * 1024 * 1024
LAST_ROWS = 32


def contract_last(left_side, weights):
    return lax.dot_general(
        left_side, weights, (((1,), (1,)), ((), ())), preferred_element_type=F32
    )


def flipped(block, axis, stride):
    route = [(i, i ^ stride) for i in range(lax.axis_size(axis))]
    return lax.ppermute(block, axis, route)


def shifted(block, axis, distance):
    count = lax.axis_size(axis)
    return lax.ppermute(block, axis, [((i - distance) % count, i) for i in range(count)])


def chunk_of(width, most):
    best = 128
    for size in range(128, most + 1, 128):
        if width % size == 0:
            best = size
    return best


def own_columns(mask, hidden):
    column = lax.broadcasted_iota(jnp.int32, (mask.shape[0], hidden), 1)
    return (mask > 0) == (column < hidden // 2)


def joined(refs, axis, index=None):
    pick = (lambda ref: ref[...]) if index is None else (lambda ref: ref[index])
    return jnp.concatenate([pick(ref) for ref in refs], axis=axis)


def gathered_rows(refs):
    return jnp.concatenate([ref[0] for ref in refs], axis=0)


def chained_rows(refs):
    others = len(refs) // 2
    own, below, above = refs[0][...], refs[1 : 1 + others], refs[1 + others :]
    return jnp.concatenate(
        [own] + [above[away][...] + below[others - 1 - away][...] for away in range(others)],
        axis=0,
    )


def put_blocks(out_refs, total):
    rows = out_refs[0].shape[0]
    for index, ref in enumerate(out_refs):
        ref[...] = total[index * rows : (index + 1) * rows].astype(ref.dtype)


def gathered_input(x, begin, rows):
    count, unit = x.shape[0], math.gcd(begin, rows)
    arrays, specs = [], []
    for turn in range(count):
        for piece in range(begin // unit, (begin + rows) // unit):
            arrays.append(x)
            specs.append(
                lambda chunk, column, turn=turn, piece=piece: pl.BlockSpec(
                    (1, unit, chunk),
                    lambda i, at: (lax.rem(at[0] + turn, count), piece, column(i)),
                )
            )
    return gathered_rows, arrays, specs, rows


def chained_input(own, from_below, from_above):
    rows = own.shape[0]
    spec = lambda chunk, column: pl.BlockSpec((rows, chunk), lambda i, at: (0, column(i)))
    arrays = [own, *from_below, *from_above]
    return chained_rows, arrays, [spec] * len(arrays), rows


def gates_kernel(read, inputs, pieces, at_ref, *refs):
    xs, gate_ups = refs[:inputs], refs[inputs : inputs + pieces]
    c_ref, e_ref = refs[inputs + pieces :]

    @pl.when(pl.program_id(0) == 0)
    def _():
        c_ref[...] = jnp.zeros_like(c_ref)
        e_ref[...] = jnp.zeros_like(e_ref)

    x = read(xs)
    c = jnp.dot(x, joined(gate_ups, 1, 0), preferred_element_type=F32)
    e = jnp.dot(x, joined(gate_ups, 1, 1), preferred_element_type=F32)
    c_ref[...] += c.reshape(c_ref.shape)
    e_ref[...] += e.reshape(e_ref.shape)


def gates_call(at, count, x_input, gate_ups):
    read, arrays, specs, rows = x_input
    width = arrays[0].shape[-1]
    pieces, hid = len(gate_ups), gate_ups[0].shape[2]
    chunk = chunk_of(width, 1792)
    hidden = pieces * hid
    weight_spec = pl.BlockSpec((2, chunk, hid), lambda i, at: (0, i, 0))
    return pl.pallas_call(
        functools.partial(gates_kernel, read, len(arrays), pieces),
        grid_spec=pltpu.PrefetchScalarGridSpec(
            num_scalar_prefetch=1,
            grid=(width // chunk,),
            in_specs=[spec(chunk, lambda i: i) for spec in specs] + [weight_spec] * pieces,
            out_specs=[pl.BlockSpec((count, rows, hidden), lambda i, at: (0, 0, 0))] * 2,
        ),
        out_shape=[jax.ShapeDtypeStruct((count, rows, hidden), F32)] * 2,
        compiler_params=pltpu.CompilerParams(vmem_limit_bytes=VMEM_LIMIT),
        cost_estimate=pl.CostEstimate(
            flops=4 * count * rows * width * hidden,
            bytes_accessed=2 * count * rows * width + 4 * width * hidden,
            transcendentals=0,
        ),
    )(at, *arrays, *gate_ups)


def backward_kernel(read, inputs, count, pieces, steps, at_ref, mask_ref, c_ref, e_ref, *refs):
    scaled, refs = refs[:inputs], refs[inputs:]
    downs, gate_ups = refs[:pieces], refs[pieces : 2 * pieces]
    outs = refs[2 * pieces : 2 * pieces + count]
    dh_ref, ga_ref, gb_ref = refs[2 * pieces + count :]
    step = pl.program_id(0)

    @pl.when(step == 0)
    def _():
        dh_ref[...] = jnp.zeros_like(dh_ref)

    @pl.when(step < steps)
    def _():
        dh_ref[...] += contract_last(read(scaled), joined(downs, 0))

    @pl.when(step == steps - 1)
    def _():
        dh = dh_ref[...]
        c, e = c_ref[...].reshape(dh.shape), e_ref[...].reshape(dh.shape)
        s = jax.nn.sigmoid(c)
        silu = c * s
        keep = own_columns(mask_ref[...], c.shape[1])
        ga_ref[...] = jnp.where(keep, dh * e * (s + silu * (1.0 - s)), 0.0).astype(BF16)
        gb_ref[...] = jnp.where(keep, dh * silu, 0.0).astype(BF16)

    @pl.when(step >= steps)
    def _():
        total = contract_last(ga_ref[...], joined(gate_ups, 1, 0))
        total += contract_last(gb_ref[...], joined(gate_ups, 1, 1))
        put_blocks(outs, total)


def backward_call(at, count, mask, scaled_input, part, c, e, downs, gate_ups):
    read, arrays, specs, rows = scaled_input
    width = arrays[0].shape[-1]
    pieces, hid = len(downs), downs[0].shape[0]
    chunk = chunk_of(width, 1792)
    steps = width // chunk
    hidden = pieces * hid
    first = lambda i: jnp.minimum(i, steps - 1)
    second = lambda i: jnp.maximum(i - steps, 0)
    pre_spec = pl.BlockSpec((count, rows, hidden), lambda i, at: (0, part, 0))
    out_spec = pl.BlockSpec((rows, chunk), lambda i, at: (0, second(i)))
    return pl.pallas_call(
        functools.partial(backward_kernel, read, len(arrays), count, pieces, steps),
        grid_spec=pltpu.PrefetchScalarGridSpec(
            num_scalar_prefetch=1,
            grid=(2 * steps,),
            in_specs=[
                pl.BlockSpec((count * rows, 1), lambda i, at: (0, 0)),
                pre_spec,
                pre_spec,
            ]
            + [spec(chunk, first) for spec in specs]
            + [pl.BlockSpec((hid, chunk), lambda i, at: (0, first(i)))] * pieces
            + [pl.BlockSpec((2, chunk, hid), lambda i, at: (0, second(i), 0))] * pieces,
            out_specs=[out_spec] * count,
            scratch_shapes=[
                pltpu.VMEM((count * rows, hidden), F32),
                pltpu.VMEM((count * rows, hidden), BF16),
                pltpu.VMEM((count * rows, hidden), BF16),
            ],
        ),
        out_shape=[jax.ShapeDtypeStruct((rows, width), F32)]
        + [jax.ShapeDtypeStruct((rows, width), BF16)] * (count - 1),
        compiler_params=pltpu.CompilerParams(vmem_limit_bytes=VMEM_LIMIT),
        cost_estimate=pl.CostEstimate(
            flops=6 * count * rows * width * hidden,
            bytes_accessed=4 * count * rows * width + 6 * width * hidden,
            transcendentals=count * rows * hidden,
        ),
    )(at, mask, c, e, *arrays, *downs, *gate_ups)


def forward_kernel(read, inputs, count, pieces, steps, at_ref, mask_ref, *refs):
    xs, refs = refs[:inputs], refs[inputs:]
    gate_ups, downs = refs[:pieces], refs[pieces : 2 * pieces]
    outs = refs[2 * pieces : 2 * pieces + count]
    a_ref, b_ref, hidden_ref = refs[2 * pieces + count :]
    step = pl.program_id(0)

    @pl.when(step == 0)
    def _():
        a_ref[...] = jnp.zeros_like(a_ref)
        b_ref[...] = jnp.zeros_like(b_ref)

    @pl.when(step < steps)
    def _():
        x = read(xs)
        a_ref[...] += jnp.dot(x, joined(gate_ups, 1, 0), preferred_element_type=F32)
        b_ref[...] += jnp.dot(x, joined(gate_ups, 1, 1), preferred_element_type=F32)

    @pl.when(step == steps - 1)
    def _():
        a, b = a_ref[...], b_ref[...]
        keep = own_columns(mask_ref[...], a.shape[1])
        hidden_ref[...] = jnp.where(keep, a * jax.nn.sigmoid(a) * b, 0.0).astype(BF16)

    @pl.when(step >= steps)
    def _():
        total = jnp.dot(hidden_ref[...], joined(downs, 0), preferred_element_type=F32)
        put_blocks(outs, total)


def forward_call(at, count, mask, x_input, gate_ups, downs):
    read, arrays, specs, rows = x_input
    width = arrays[0].shape[-1]
    pieces, hid = len(downs), downs[0].shape[0]
    chunk = chunk_of(width, 1792)
    steps = width // chunk
    hidden = pieces * hid
    first = lambda i: jnp.minimum(i, steps - 1)
    second = lambda i: jnp.maximum(i - steps, 0)
    return pl.pallas_call(
        functools.partial(forward_kernel, read, len(arrays), count, pieces, steps),
        grid_spec=pltpu.PrefetchScalarGridSpec(
            num_scalar_prefetch=1,
            grid=(2 * steps,),
            in_specs=[pl.BlockSpec((count * rows, 1), lambda i, at: (0, 0))]
            + [spec(chunk, first) for spec in specs]
            + [pl.BlockSpec((2, chunk, hid), lambda i, at: (0, first(i), 0))] * pieces
            + [pl.BlockSpec((hid, chunk), lambda i, at: (0, second(i)))] * pieces,
            out_specs=[pl.BlockSpec((rows, chunk), lambda i, at: (0, second(i)))] * count,
            scratch_shapes=[
                pltpu.VMEM((count * rows, hidden), F32),
                pltpu.VMEM((count * rows, hidden), F32),
                pltpu.VMEM((count * rows, hidden), BF16),
            ],
        ),
        out_shape=[jax.ShapeDtypeStruct((rows, width), F32)]
        + [jax.ShapeDtypeStruct((rows, width), BF16)] * (count - 1),
        compiler_params=pltpu.CompilerParams(vmem_limit_bytes=VMEM_LIMIT),
        cost_estimate=pl.CostEstimate(
            flops=6 * count * rows * width * hidden,
            bytes_accessed=6 * count * rows * width + 6 * width * hidden,
            transcendentals=count * rows * hidden,
        ),
    )(at, mask, *arrays, *gate_ups, *downs)


def after(value, *earlier):
    return lax.optimization_barrier((value, earlier))[0]


def hop(below, above, axis, step):
    count = lax.axis_size(axis)
    up = [(i, i + 1) for i in range(step - 1, count - 1)]
    down = [(i, i - 1) for i in range(1, count - step + 1)]
    return lax.ppermute(below, axis, up), lax.ppermute(above, axis, down)


def summands(blocks, step, arrived):
    pair = (blocks[len(blocks) - step], blocks[step])
    if arrived is None:
        return pair
    return tuple(
        (own.astype(F32) + other.astype(F32)).astype(BF16) for own, other in zip(pair, arrived)
    )


def step_home(pair, axis, step):
    count = lax.axis_size(axis)
    up = lax.ppermute(pair[0], axis, [(i, i + 1) for i in range(step)])
    down = lax.ppermute(pair[1], axis, [(i, i - 1) for i in range(count - step, count)])
    return up, down


def summed(block, arrived):
    for part in arrived:
        block = block + part.astype(F32)
    return block


def few_experts(
    x_forward,
    route_forward,
    prob_forward,
    x_backward,
    route_backward,
    prob_backward,
    grad_output,
    w_gate,
    w_up,
    w_down,
):
    tokens_here = x_forward.shape[1]
    expert_here = lax.axis_index("expert") // 2
    count = lax.axis_size("dp")
    at = lax.axis_index("dp").reshape(1).astype(jnp.int32)

    last = min(LAST_ROWS, tokens_here // 2)
    early = tokens_here - last
    scaled_grad = (prob_backward[0][:, None] * grad_output[0].astype(F32)).astype(BF16)
    routes = jnp.concatenate([route_forward[0], route_backward[0]], axis=1)
    gate_up, down = jnp.concatenate([w_gate[0], w_up[0]], axis=0), w_down[0, 0]
    bundle = jnp.concatenate([x_backward[0], scaled_grad[:early]], axis=0)
    bundle, routes, scaled_last = lax.optimization_barrier((bundle, routes, scaled_grad[early:]))
    x_gathered = lax.all_gather(x_forward[0], "dp")
    bundle = lax.all_gather(after(bundle, x_gathered), "dp")
    other_routes = [shifted(routes, "dp", -away) for away in range(1, count)]
    mine = (jnp.stack([routes] + other_routes) == expert_here).astype(F32)
    mask_fwd, mask_bwd = mine[:, :, 0:1], mine[:, :, 1:2]

    own = [after(gate_up, other_routes), down]
    own_flips = [flipped(weight, "expert", 1) for weight in own]
    across = [flipped(weight, "expert", 2) for weight in (gate_up, down)]
    across_first = after(across[0], x_gathered, own_flips, other_routes)
    across_flips = [flipped(weight, "expert", 1) for weight in (across_first, across[1])]
    gate_ups, downs = zip((gate_up, down), own_flips, across, across_flips)
    hops_last = [(scaled_last, scaled_last)]
    hops_last.append(hop(*hops_last[0], "dp", 1))

    partial_fwd = forward_call(
        at,
        count,
        after(mask_fwd.reshape(count * tokens_here, 1), hops_last[1]),
        gathered_input(x_gathered, 0, tokens_here),
        gate_ups,
        downs,
    )
    hops_last[1] = after(hops_last[1], partial_fwd[1])
    for step in range(2, count):
        hops_last.append(hop(*hops_last[-1], "dp", step))
    arrived_fwd = step_home(summands(partial_fwd, 1, None), "dp", 1)
    sends_fwd = summands(partial_fwd, 2, arrived_fwd)
    arrived_fwd = step_home(sends_fwd, "dp", 2)
    bundle = after(bundle, sends_fwd, hops_last[-1])
    c, e = gates_call(at, count, gathered_input(bundle, 0, tokens_here), gate_ups)

    sends_fwd = summands(partial_fwd, 3, after(arrived_fwd, c))
    arrived_fwd = step_home(sends_fwd, "dp", 3)
    mask_early = after(mask_bwd[:, :early].reshape(count * early, 1), sends_fwd)
    scaled_early = gathered_input(bundle, tokens_here, early)
    blocks_early = backward_call(
        at, count, mask_early, scaled_early, 0, c, e, downs, gate_ups
    )

    arrived_early = step_home(summands(blocks_early, 1, None), "dp", 1)
    total_fwd = summed(partial_fwd[0], after(arrived_fwd, blocks_early[1]))
    layer_out = (x_forward[0].astype(F32) + prob_forward[0][:, None] * total_fwd).astype(BF16)
    sent_fwd = shifted(layer_out, "pipe", 1)
    from_below, from_above = zip(*hops_last[1:])
    mask_last = after(mask_bwd[:, early:].reshape(count * last, 1), layer_out)
    scaled_last = chained_input(scaled_last, from_below, from_above)
    blocks_last = backward_call(
        at, count, mask_last, scaled_last, early // last, c, e, downs, gate_ups
    )

    arrived_early, arrived_last = after(arrived_early, blocks_last[1]), None
    for step in range(2, count):
        if step > 2:
            arrived_early = after(arrived_early, sent_fwd)
        arrived_early = step_home(summands(blocks_early, step, arrived_early), "dp", step)
        arrived_last = step_home(summands(blocks_last, step - 1, arrived_last), "dp", step - 1)

    def sent_back(rows, block, arrived):
        grad_in = (grad_output[0, rows].astype(F32) + summed(block, arrived)).astype(BF16)
        return shifted(grad_in, "pipe", -1)

    sent_early = sent_back(slice(0, early), blocks_early[0], arrived_early)
    arrived_last = step_home(summands(blocks_last, count - 1, arrived_last), "dp", count - 1)
    sent_last = sent_back(slice(early, None), blocks_last[0], after(arrived_last, sent_early))
    return (sent_fwd[None], jnp.concatenate([sent_early, sent_last], axis=0)[None])


def from_partner(block, axis, stride):
    count = lax.axis_size(axis)
    route = []
    for low in range(count):
        high = low | 1 << stride
        if high != low and high < count:
            route += [(low, high), (high, low)]
    return lax.ppermute(block, axis, route)


def silu_parts(pre_gate):
    sigma_gate = jax.nn.sigmoid(pre_gate)
    return (pre_gate * sigma_gate, sigma_gate)


def expert_pass(forward_rows, backward_rows, scaled_rows, gate_weight, up_weight, down_weight):
    gate_fwd = jnp.dot(forward_rows, gate_weight, preferred_element_type=jnp.float32)
    up_fwd = jnp.dot(forward_rows, up_weight, preferred_element_type=jnp.float32)
    silu_fwd, sigma_fwd = silu_parts(gate_fwd)
    hidden_fwd = (silu_fwd * up_fwd).astype(jnp.bfloat16)
    expert_out = jnp.dot(hidden_fwd, down_weight, preferred_element_type=jnp.float32)
    gate_bwd = jnp.dot(backward_rows, gate_weight, preferred_element_type=jnp.float32)
    up_bwd = jnp.dot(backward_rows, up_weight, preferred_element_type=jnp.float32)
    silu_bwd, sigma_bwd = silu_parts(gate_bwd)
    grad_hidden = contract_last(scaled_rows, down_weight)
    grad_gate = (grad_hidden * up_bwd * (sigma_bwd + silu_bwd * (1.0 - sigma_bwd))).astype(
        jnp.bfloat16
    )
    grad_up = (grad_hidden * silu_bwd).astype(jnp.bfloat16)
    grad_rows = contract_last(grad_gate, gate_weight) + contract_last(grad_up, up_weight)
    return (expert_out, grad_rows)


def placing(routes, experts_here, capacity):
    route_hits = (routes[:, None] == jnp.arange(experts_here, dtype=jnp.int32)[None, :]).astype(
        jnp.int32
    )
    before = jnp.cumsum(route_hits, axis=0) - route_hits
    slot_index = jnp.sum(before * route_hits, axis=1)
    position = routes * capacity + slot_index
    selector = (
        position[None, :] == jnp.arange(experts_here * capacity, dtype=jnp.int32)[:, None]
    ).astype(jnp.bfloat16)
    return (position, selector)


def packing(selector, values):
    return jnp.dot(selector, values, preferred_element_type=jnp.float32).astype(jnp.bfloat16)


def many_experts(
    x_forward,
    route_forward,
    prob_forward,
    x_backward,
    route_backward,
    prob_backward,
    grad_output,
    w_gate,
    w_up,
    w_down,
):
    tokens_here = x_forward.shape[1]
    feature_width = x_forward.shape[2]
    groups = lax.axis_size("expert")
    experts_here = groups // 2
    capacity = min(tokens_here, (tokens_here * 5 + 4 * experts_here - 1) // (4 * experts_here))
    pair_side = lax.axis_index("expert") % 2
    gate_full, up_full, down_full = (
        lax.all_gather(w_gate[0, 0], "dp", axis=1, tiled=True),
        lax.all_gather(w_up[0, 0], "dp", axis=1, tiled=True),
        lax.all_gather(w_down[0, 0], "dp", axis=0, tiled=True),
    )
    pos_fwd, select_fwd = placing(route_forward[0, :, 0], experts_here, capacity)
    pos_bwd, select_bwd = placing(route_backward[0, :, 0], experts_here, capacity)
    scaled_grad = (prob_backward[0][:, None] * grad_output[0].astype(jnp.float32)).astype(
        jnp.bfloat16
    )
    stacked = jnp.stack(
        [
            packing(select_fwd, x_forward[0]),
            packing(select_bwd, x_backward[0]),
            packing(select_bwd, scaled_grad),
        ]
    )
    stacked = stacked.reshape(3, experts_here, capacity, feature_width)
    split_rows = stacked.reshape(3, experts_here, capacity, 2, feature_width // 2).transpose(
        0, 1, 3, 2, 4
    )
    split_rows = split_rows.reshape(3, groups, capacity, feature_width // 2)
    own_half = lax.all_to_all(split_rows, "expert", split_axis=1, concat_axis=1, tiled=True)
    partner_half = from_partner(own_half, "expert", 0)
    arrived = jnp.where(
        pair_side == 0,
        jnp.concatenate([own_half, partner_half], axis=3),
        jnp.concatenate([partner_half, own_half], axis=3),
    )
    expert_rows = arrived.reshape(3, groups * capacity, feature_width)
    expert_out, grad_rows = expert_pass(
        expert_rows[0], expert_rows[1], expert_rows[2], gate_full, up_full, down_full
    )
    results = jnp.stack([expert_out, grad_rows]).reshape(2, groups, capacity, feature_width)
    quarters = results.reshape(2, groups, capacity, 2, feature_width // 2)
    keep_part = jnp.where(pair_side == 0, quarters[:, :, :, 0], quarters[:, :, :, 1])
    give_part = jnp.where(pair_side == 0, quarters[:, :, :, 1], quarters[:, :, :, 0])
    finished = keep_part + from_partner(give_part.astype(jnp.bfloat16), "expert", 0).astype(
        give_part.dtype
    )
    returned = lax.all_to_all(finished, "expert", split_axis=1, concat_axis=1, tiled=True)
    combined = returned.reshape(2, experts_here, 2, capacity, feature_width // 2).transpose(
        0, 1, 3, 2, 4
    )
    combined = combined.reshape(2, experts_here, capacity, feature_width)
    flat_out = combined.reshape(2, experts_here * capacity, feature_width)
    moved_fwd = jnp.take(flat_out[0], pos_fwd, axis=0)
    moved_bwd = jnp.take(flat_out[1], pos_bwd, axis=0)
    layer_out = (x_forward[0].astype(jnp.float32) + prob_forward[0][:, None] * moved_fwd).astype(
        jnp.bfloat16
    )
    grad_in = (grad_output[0].astype(jnp.float32) + moved_bwd).astype(jnp.bfloat16)
    sent_fwd = shifted(layer_out, "pipe", 1)
    sent_bwd = shifted(grad_in, "pipe", -1)
    return (sent_fwd[None], sent_bwd[None])


def solution(mesh):
    few = mesh.shape["expert"] == 4
    return jax.shard_map(
        few_experts if few else many_experts,
        mesh=mesh,
        in_specs=(
            P("pipe", ("expert", "dp"), None),
            P("pipe", ("expert", "dp"), None),
            P("pipe", ("expert", "dp")),
            P("pipe", ("expert", "dp"), None),
            P("pipe", ("expert", "dp"), None),
            P("pipe", ("expert", "dp")),
            P("pipe", ("expert", "dp"), None),
            P("pipe", "expert", None, "dp"),
            P("pipe", "expert", None, "dp"),
            P("pipe", "expert", "dp", None),
        ),
        out_specs=(P("pipe", ("expert", "dp"), None), P("pipe", ("expert", "dp"), None)),
        check_vma=False,
    )
```

```python
import functools
import math

import jax
import jax.numpy as jnp
from jax import lax
from jax.experimental import pallas as pl
from jax.experimental.pallas import tpu as pltpu
from jax.sharding import PartitionSpec as P

BF16, F32 = jnp.bfloat16, jnp.float32
VMEM_LIMIT = 56 * 1024 * 1024
LEAD_ROWS = 16
TAG_COLUMNS = 128


def contract_last(left_side, weights):
    return lax.dot_general(
        left_side, weights, (((1,), (1,)), ((), ())), preferred_element_type=F32
    )


def flipped(block, axis, stride):
    route = [(i, i ^ stride) for i in range(lax.axis_size(axis))]
    return lax.ppermute(block, axis, route)


def shifted(block, axis, distance):
    count = lax.axis_size(axis)
    return lax.ppermute(block, axis, [((i - distance) % count, i) for i in range(count)])


def chunk_of(width, most):
    best = 128
    for size in range(128, most + 1, 128):
        if width % size == 0:
            best = size
    return best


def gathered_rows(refs):
    return jnp.concatenate([ref[0] for ref in refs], axis=0)


def chained_rows(refs):
    others = len(refs) // 2
    own, below, above = refs[0][...], refs[1 : 1 + others], refs[1 + others :]
    return jnp.concatenate(
        [own] + [above[away][...] + below[others - 1 - away][...] for away in range(others)],
        axis=0,
    )


def gathered_input(x, begin, rows):
    count, unit = x.shape[0], math.gcd(begin, rows)
    arrays, specs = [], []
    for turn in range(count):
        for piece in range(begin // unit, (begin + rows) // unit):
            arrays.append(x)
            specs.append(
                lambda chunk, column, turn=turn, piece=piece: pl.BlockSpec(
                    (1, unit, chunk),
                    lambda i, at: (lax.rem(at[0] + turn, count), piece, column(i)),
                )
            )
    return gathered_rows, arrays, specs


def chained_input(hops, begin, rows):
    (own, _), *others = hops
    from_below, from_above = zip(*others)
    spec = lambda chunk, column: pl.BlockSpec(
        (rows, chunk), lambda i, at: (begin // rows, column(i))
    )
    arrays = [own, *from_below, *from_above]
    return chained_rows, arrays, [spec] * len(arrays)


def weight_copies(chunk, steps, gate_ups, downs, gate_up_held, down_held, sems):
    by_chunk = []
    for step in range(steps):
        part = pl.ds(step * chunk, chunk)
        by_chunk.append(
            (
                [
                    pltpu.make_async_copy(
                        ref.at[:, part, :], gate_up_held.at[i, :, part, :], sems.at[0, step, i]
                    )
                    for i, ref in enumerate(gate_ups)
                ],
                [
                    pltpu.make_async_copy(
                        ref.at[:, part], down_held.at[i, :, part], sems.at[1, step, i]
                    )
                    for i, ref in enumerate(downs)
                ],
            )
        )
    return by_chunk


def own_hidden(at_ref, tags, column, hidden):
    mine = tags[:, column : column + 1].astype(jnp.int32) == at_ref[1]
    unit = lax.broadcasted_iota(jnp.int32, (tags.shape[0], hidden), 1)
    return mine == (unit < hidden // 2)


def expert_kernel(backward, reads, inputs, count, pieces, chunk, steps, at_ref, *refs):
    groups = []
    for number in (*inputs, pieces, pieces, count):
        groups.append(refs[:number])
        refs = refs[number:]
    *rows_in, gate_ups, downs, outs = groups
    (*totals, hidden_refs, gate_up_held, down_held, sems) = (
        refs[: 3 if backward else 2] + (refs[3 if backward else 2 : -3],) + refs[-3:]
    )
    step = pl.program_id(0)
    hidden = totals[0].shape[1]
    copies = weight_copies(chunk, steps, gate_ups, downs, gate_up_held, down_held, sems)

    @pl.when(step == 0)
    def _():
        for kind in range(2):
            for by_kind in copies:
                for copy in by_kind[kind]:
                    copy.start()
        for total in totals:
            total[...] = jnp.zeros_like(total)

    for number in range(steps):

        @pl.when(step == number)
        def _(number=number):
            for copy in copies[number][0] + (copies[number][1] if backward else []):
                copy.wait()

        if not backward:

            @pl.when(step == steps + number)
            def _(number=number):
                for copy in copies[number][1]:
                    copy.wait()

    at_chunk = pl.ds(pl.multiple_of(lax.rem(step, steps) * chunk, chunk), chunk)

    def gate_or_up(which):
        return jnp.concatenate(
            [gate_up_held[i, which, at_chunk, :] for i in range(pieces)], axis=1
        )

    def down():
        return jnp.concatenate([down_held[i, :, at_chunk] for i in range(pieces)], axis=0)

    @pl.when(step < steps)
    def _():
        x = reads[1](rows_in[1])
        totals[0][...] += jnp.dot(x, gate_or_up(0), preferred_element_type=F32)
        totals[1][...] += jnp.dot(x, gate_or_up(1), preferred_element_type=F32)
        if backward:
            totals[2][...] += contract_last(reads[2](rows_in[2]), down())

    @pl.when(step == steps - 1)
    def _():
        tags = reads[0](rows_in[0])
        keep = own_hidden(at_ref, tags, TAG_COLUMNS // 2 if backward else 0, hidden)
        gate, up = totals[0][...], totals[1][...]
        s = jax.nn.sigmoid(gate)
        silu = gate * s
        if backward:
            grad = totals[2][...]
            grad_gate = grad * up * (s + silu * (1.0 - s))
            hidden_refs[0][...] = jnp.where(keep, grad_gate, 0.0).astype(BF16)
            hidden_refs[1][...] = jnp.where(keep, grad * silu, 0.0).astype(BF16)
        else:
            hidden_refs[0][...] = jnp.where(keep, silu * up, 0.0).astype(BF16)

    @pl.when(step >= steps)
    def _():
        if backward:
            total = contract_last(hidden_refs[0][...], gate_or_up(0))
            total += contract_last(hidden_refs[1][...], gate_or_up(1))
        else:
            total = jnp.dot(hidden_refs[0][...], down(), preferred_element_type=F32)
        rows = outs[0].shape[0]
        for index, ref in enumerate(outs):
            ref[...] = total[index * rows : (index + 1) * rows].astype(ref.dtype)


def expert_call(at, count, rows, width, tags, inputs, gate_ups, downs):
    backward = len(inputs) == 2
    pieces, hid = len(downs), downs[0].shape[0]
    chunk = chunk_of(width, 1792)
    steps, hidden, many = width // chunk, pieces * hid, count * rows
    first = lambda i: jnp.minimum(i, steps - 1)
    second = lambda i: jnp.maximum(i - steps, 0)
    all_inputs = [tags, *inputs]
    arrays = [array for _, some, _ in all_inputs for array in some]
    in_specs = [spec(TAG_COLUMNS, lambda i: width // TAG_COLUMNS) for spec in tags[2]]
    in_specs += [spec(chunk, first) for _, _, specs in inputs for spec in specs]
    in_specs += [pl.BlockSpec(memory_space=pl.ANY)] * (2 * pieces)
    kernel = functools.partial(
        expert_kernel,
        backward,
        [read for read, _, _ in all_inputs],
        [len(some) for _, some, _ in all_inputs],
        count,
        pieces,
        chunk,
        steps,
    )
    return pl.pallas_call(
        kernel,
        grid_spec=pltpu.PrefetchScalarGridSpec(
            num_scalar_prefetch=1,
            grid=(2 * steps,),
            in_specs=in_specs,
            out_specs=[pl.BlockSpec((rows, chunk), lambda i, at: (0, second(i)))] * count,
            scratch_shapes=[pltpu.VMEM((many, hidden), F32)] * (3 if backward else 2)
            + [pltpu.VMEM((many, hidden), BF16)] * (2 if backward else 1)
            + [
                pltpu.VMEM((pieces, 2, width, hid), BF16),
                pltpu.VMEM((pieces, hid, width), BF16),
                pltpu.SemaphoreType.DMA((2, steps, pieces)),
            ],
        ),
        out_shape=[jax.ShapeDtypeStruct((rows, width), F32)]
        + [jax.ShapeDtypeStruct((rows, width), BF16)] * (count - 1),
        compiler_params=pltpu.CompilerParams(vmem_limit_bytes=VMEM_LIMIT),
        cost_estimate=pl.CostEstimate(
            flops=(10 if backward else 6) * many * width * hidden,
            bytes_accessed=6 * many * width + 6 * width * hidden,
            transcendentals=many * hidden,
        ),
    )(at, *arrays, *gate_ups, *downs)


def after(value, *earlier):
    return lax.optimization_barrier((value, earlier))[0]


def hop(below, above, axis, step):
    count = lax.axis_size(axis)
    up = [(i, i + 1) for i in range(step - 1, count - 1)]
    down = [(i, i - 1) for i in range(1, count - step + 1)]
    return lax.ppermute(below, axis, up), lax.ppermute(above, axis, down)


def summands(blocks, step, arrived):
    pair = (blocks[len(blocks) - step], blocks[step])
    if arrived is None:
        return pair
    return tuple(
        (own.astype(F32) + other.astype(F32)).astype(BF16) for own, other in zip(pair, arrived)
    )


def step_home(pair, axis, step):
    count = lax.axis_size(axis)
    up = lax.ppermute(pair[0], axis, [(i, i + 1) for i in range(step)])
    down = lax.ppermute(pair[1], axis, [(i, i - 1) for i in range(count - step, count)])
    return up, down


def summed(block, arrived):
    for part in arrived:
        block = block + part.astype(F32)
    return block


def few_experts(
    x_forward,
    route_forward,
    prob_forward,
    x_backward,
    route_backward,
    prob_backward,
    grad_output,
    w_gate,
    w_up,
    w_down,
):
    tokens_here, width = x_forward.shape[1:]
    expert_here = lax.axis_index("expert") // 2
    count = lax.axis_size("dp")
    at = jnp.stack([lax.axis_index("dp"), expert_here]).astype(jnp.int32)
    lead = min(LEAD_ROWS, tokens_here // 2)
    main = tokens_here - lead
    ends = (slice(0, main), slice(main, tokens_here))

    half_tag = (tokens_here, TAG_COLUMNS // 2)
    tagged = jnp.concatenate(
        [x_forward[0]]
        + [jnp.broadcast_to(r[0].astype(BF16), half_tag) for r in (route_forward, route_backward)],
        axis=1,
    )
    scaled_grad = (prob_backward[0][:, None] * grad_output[0].astype(F32)).astype(BF16)
    main_rows, lead_rows = (
        jnp.concatenate([x_backward[0, rows], scaled_grad[rows]], axis=0) for rows in ends
    )
    gate_up, down = jnp.concatenate([w_gate[0], w_up[0]], axis=0), w_down[0, 0]

    x_gathered = lax.all_gather(tagged, "dp")
    main_gathered = lax.all_gather(after(main_rows, x_gathered), "dp")
    across_down = flipped(down, "expert", 2)
    across_gate_up = flipped(gate_up, "expert", 2)
    hops = [(lead_rows, lead_rows)]
    hops.append(hop(*hops[-1], "dp", 1))
    hops[1] = after(hops[1], x_gathered)
    for step in range(2, count):
        hops.append(hop(*hops[-1], "dp", step))
    gate_ups = [gate_up, flipped(gate_up, "expert", 1), across_gate_up]
    downs = [down, flipped(down, "expert", 1), across_down, flipped(across_down, "expert", 1)]
    gate_ups.append(flipped(after(across_gate_up, hops[-1], gate_ups[1], downs[3]), "expert", 1))

    def call(tags_from, rows, inputs):
        tags = gathered_input(x_gathered, tags_from, rows)
        return expert_call(at, count, rows, width, tags, inputs, gate_ups, downs)

    partial_fwd = call(0, tokens_here, [gathered_input(x_gathered, 0, tokens_here)])

    arrived_fwd = step_home(summands(partial_fwd, 1, None), "dp", 1)
    hops[0] = after(hops[0], partial_fwd[1])
    partial_lead = call(main, lead, [chained_input(hops, begin, lead) for begin in (0, lead)])

    arrived_fwd = step_home(summands(partial_fwd, 2, after(arrived_fwd, partial_lead[1])), "dp", 2)
    arrived_lead = step_home(summands(partial_lead, 1, None), "dp", 1)
    sends_fwd = summands(partial_fwd, 3, arrived_fwd)
    sends_lead = summands(partial_lead, 2, arrived_lead)
    arrived_fwd = step_home(sends_fwd, "dp", 3)
    arrived_lead = step_home(sends_lead, "dp", 2)
    main_gathered = after(main_gathered, sends_fwd, sends_lead)
    partial_main = call(0, main, [gathered_input(main_gathered, b, main) for b in (0, main)])

    arrived_fwd, arrived_lead = after((arrived_fwd, arrived_lead), partial_main[1])
    sends_main = after(summands(partial_main, 1, None), arrived_fwd, arrived_lead)
    arrived_main = step_home(sends_main, "dp", 1)
    total_fwd = summed(partial_fwd[0], arrived_fwd)
    layer_out = (x_forward[0].astype(F32) + prob_forward[0][:, None] * total_fwd).astype(BF16)
    sent_fwd = shifted(layer_out, "pipe", 1)
    arrived_lead = step_home(summands(partial_lead, 3, arrived_lead), "dp", 3)

    def sent_back(rows, block, arrived):
        grad_in = (grad_output[0, rows].astype(F32) + summed(block, arrived)).astype(BF16)
        return shifted(grad_in, "pipe", -1)

    arrived_main = step_home(summands(partial_main, 2, arrived_main), "dp", 2)
    sent_lead = sent_back(ends[1], partial_lead[0], arrived_lead)
    arrived_main = after(arrived_main, sent_fwd, sent_lead)
    arrived_main = step_home(summands(partial_main, 3, arrived_main), "dp", 3)
    sent_main = sent_back(ends[0], partial_main[0], arrived_main)
    return (sent_fwd[None], jnp.concatenate([sent_main, sent_lead], axis=0)[None])


def from_partner(block, axis, stride):
    count = lax.axis_size(axis)
    route = []
    for low in range(count):
        high = low | 1 << stride
        if high != low and high < count:
            route += [(low, high), (high, low)]
    return lax.ppermute(block, axis, route)


def silu_parts(pre_gate):
    sigma_gate = jax.nn.sigmoid(pre_gate)
    return (pre_gate * sigma_gate, sigma_gate)


def expert_pass(forward_rows, backward_rows, scaled_rows, gate_weight, up_weight, down_weight):
    gate_fwd = jnp.dot(forward_rows, gate_weight, preferred_element_type=jnp.float32)
    up_fwd = jnp.dot(forward_rows, up_weight, preferred_element_type=jnp.float32)
    silu_fwd, sigma_fwd = silu_parts(gate_fwd)
    hidden_fwd = (silu_fwd * up_fwd).astype(jnp.bfloat16)
    expert_out = jnp.dot(hidden_fwd, down_weight, preferred_element_type=jnp.float32)
    gate_bwd = jnp.dot(backward_rows, gate_weight, preferred_element_type=jnp.float32)
    up_bwd = jnp.dot(backward_rows, up_weight, preferred_element_type=jnp.float32)
    silu_bwd, sigma_bwd = silu_parts(gate_bwd)
    grad_hidden = contract_last(scaled_rows, down_weight)
    grad_gate = (grad_hidden * up_bwd * (sigma_bwd + silu_bwd * (1.0 - sigma_bwd))).astype(
        jnp.bfloat16
    )
    grad_up = (grad_hidden * silu_bwd).astype(jnp.bfloat16)
    grad_rows = contract_last(grad_gate, gate_weight) + contract_last(grad_up, up_weight)
    return (expert_out, grad_rows)


def placing(routes, experts_here, capacity):
    route_hits = (routes[:, None] == jnp.arange(experts_here, dtype=jnp.int32)[None, :]).astype(
        jnp.int32
    )
    before = jnp.cumsum(route_hits, axis=0) - route_hits
    slot_index = jnp.sum(before * route_hits, axis=1)
    position = routes * capacity + slot_index
    selector = (
        position[None, :] == jnp.arange(experts_here * capacity, dtype=jnp.int32)[:, None]
    ).astype(jnp.bfloat16)
    return (position, selector)


def packing(selector, values):
    return jnp.dot(selector, values, preferred_element_type=jnp.float32).astype(jnp.bfloat16)


def many_experts(
    x_forward,
    route_forward,
    prob_forward,
    x_backward,
    route_backward,
    prob_backward,
    grad_output,
    w_gate,
    w_up,
    w_down,
):
    tokens_here = x_forward.shape[1]
    feature_width = x_forward.shape[2]
    groups = lax.axis_size("expert")
    experts_here = groups // 2
    capacity = min(tokens_here, (tokens_here * 5 + 4 * experts_here - 1) // (4 * experts_here))
    pair_side = lax.axis_index("expert") % 2
    gate_full, up_full, down_full = (
        lax.all_gather(w_gate[0, 0], "dp", axis=1, tiled=True),
        lax.all_gather(w_up[0, 0], "dp", axis=1, tiled=True),
        lax.all_gather(w_down[0, 0], "dp", axis=0, tiled=True),
    )
    pos_fwd, select_fwd = placing(route_forward[0, :, 0], experts_here, capacity)
    pos_bwd, select_bwd = placing(route_backward[0, :, 0], experts_here, capacity)
    scaled_grad = (prob_backward[0][:, None] * grad_output[0].astype(jnp.float32)).astype(
        jnp.bfloat16
    )
    stacked = jnp.stack(
        [
            packing(select_fwd, x_forward[0]),
            packing(select_bwd, x_backward[0]),
            packing(select_bwd, scaled_grad),
        ]
    )
    stacked = stacked.reshape(3, experts_here, capacity, feature_width)
    split_rows = stacked.reshape(3, experts_here, capacity, 2, feature_width // 2).transpose(
        0, 1, 3, 2, 4
    )
    split_rows = split_rows.reshape(3, groups, capacity, feature_width // 2)
    own_half = lax.all_to_all(split_rows, "expert", split_axis=1, concat_axis=1, tiled=True)
    partner_half = from_partner(own_half, "expert", 0)
    arrived = jnp.where(
        pair_side == 0,
        jnp.concatenate([own_half, partner_half], axis=3),
        jnp.concatenate([partner_half, own_half], axis=3),
    )
    expert_rows = arrived.reshape(3, groups * capacity, feature_width)
    expert_out, grad_rows = expert_pass(
        expert_rows[0], expert_rows[1], expert_rows[2], gate_full, up_full, down_full
    )
    results = jnp.stack([expert_out, grad_rows]).reshape(2, groups, capacity, feature_width)
    quarters = results.reshape(2, groups, capacity, 2, feature_width // 2)
    keep_part = jnp.where(pair_side == 0, quarters[:, :, :, 0], quarters[:, :, :, 1])
    give_part = jnp.where(pair_side == 0, quarters[:, :, :, 1], quarters[:, :, :, 0])
    finished = keep_part + from_partner(give_part.astype(jnp.bfloat16), "expert", 0).astype(
        give_part.dtype
    )
    returned = lax.all_to_all(finished, "expert", split_axis=1, concat_axis=1, tiled=True)
    combined = returned.reshape(2, experts_here, 2, capacity, feature_width // 2).transpose(
        0, 1, 3, 2, 4
    )
    combined = combined.reshape(2, experts_here, capacity, feature_width)
    flat_out = combined.reshape(2, experts_here * capacity, feature_width)
    moved_fwd = jnp.take(flat_out[0], pos_fwd, axis=0)
    moved_bwd = jnp.take(flat_out[1], pos_bwd, axis=0)
    layer_out = (x_forward[0].astype(jnp.float32) + prob_forward[0][:, None] * moved_fwd).astype(
        jnp.bfloat16
    )
    grad_in = (grad_output[0].astype(jnp.float32) + moved_bwd).astype(jnp.bfloat16)
    sent_fwd = shifted(layer_out, "pipe", 1)
    sent_bwd = shifted(grad_in, "pipe", -1)
    return (sent_fwd[None], sent_bwd[None])


def solution(mesh):
    few = mesh.shape["expert"] == 4
    return jax.shard_map(
        few_experts if few else many_experts,
        mesh=mesh,
        in_specs=(
            P("pipe", ("expert", "dp"), None),
            P("pipe", ("expert", "dp"), None),
            P("pipe", ("expert", "dp")),
            P("pipe", ("expert", "dp"), None),
            P("pipe", ("expert", "dp"), None),
            P("pipe", ("expert", "dp")),
            P("pipe", ("expert", "dp"), None),
            P("pipe", "expert", None, "dp"),
            P("pipe", "expert", None, "dp"),
            P("pipe", "expert", "dp", None),
        ),
        out_specs=(P("pipe", ("expert", "dp"), None), P("pipe", ("expert", "dp"), None)),
        check_vma=False,
    )
```

```python
import functools
import math

import jax
import jax.numpy as jnp
from jax import lax
from jax.experimental import pallas as pl
from jax.experimental.pallas import tpu as pltpu
from jax.sharding import PartitionSpec as P

BF16, F32 = jnp.bfloat16, jnp.float32
VMEM_LIMIT = 56 * 1024 * 1024
LEAD_ROWS = 16
TAG_COLUMNS = 128


def contract_last(left_side, weights):
    return lax.dot_general(
        left_side, weights, (((1,), (1,)), ((), ())), preferred_element_type=F32
    )


def flipped(block, axis, stride):
    route = [(i, i ^ stride) for i in range(lax.axis_size(axis))]
    return lax.ppermute(block, axis, route)


def shifted(block, axis, distance):
    count = lax.axis_size(axis)
    return lax.ppermute(block, axis, [((i - distance) % count, i) for i in range(count)])


def chunk_of(width, most):
    best = 128
    for size in range(128, most + 1, 128):
        if width % size == 0:
            best = size
    return best


def gathered_rows(refs):
    return jnp.concatenate([ref[0] for ref in refs], axis=0)


def chained_rows(refs):
    others = len(refs) // 2
    own, below, above = refs[0][...], refs[1 : 1 + others], refs[1 + others :]
    return jnp.concatenate(
        [own] + [above[away][...] + below[others - 1 - away][...] for away in range(others)],
        axis=0,
    )


def gathered_input(x, begin, rows):
    count, unit = x.shape[0], math.gcd(begin, rows)
    arrays, specs = [], []
    for turn in range(count):
        for piece in range(begin // unit, (begin + rows) // unit):
            arrays.append(x)
            specs.append(
                lambda chunk, column, turn=turn, piece=piece: pl.BlockSpec(
                    (1, unit, chunk),
                    lambda i, at: (lax.rem(at[0] + turn, count), piece, column(i)),
                )
            )
    return gathered_rows, arrays, specs


def chained_input(hops, begin, rows):
    (own, _), *others = hops
    from_below, from_above = zip(*others)
    spec = lambda chunk, column: pl.BlockSpec(
        (rows, chunk), lambda i, at: (begin // rows, column(i))
    )
    arrays = [own, *from_below, *from_above]
    return chained_rows, arrays, [spec] * len(arrays)


def weight_copies(chunk, steps, gate_ups, downs, gate_up_held, down_held, sems):
    by_chunk = []
    for step in range(steps):
        part = pl.ds(step * chunk, chunk)
        by_chunk.append(
            (
                [
                    pltpu.make_async_copy(
                        ref.at[:, part, :], gate_up_held.at[i, :, part, :], sems.at[0, step, i]
                    )
                    for i, ref in enumerate(gate_ups)
                ],
                [
                    pltpu.make_async_copy(
                        ref.at[:, part], down_held.at[i, :, part], sems.at[1, step, i]
                    )
                    for i, ref in enumerate(downs)
                ],
            )
        )
    return by_chunk


def own_hidden(at_ref, tags, column, hidden):
    mine = tags[:, column : column + 1].astype(jnp.int32) == at_ref[1]
    unit = lax.broadcasted_iota(jnp.int32, (tags.shape[0], hidden), 1)
    return mine == (unit < hidden // 2)


def joined(refs, axis, index=None):
    pick = (lambda ref: ref[...]) if index is None else (lambda ref: ref[index])
    return jnp.concatenate([pick(ref) for ref in refs], axis=axis)


def put_blocks(outs, total):
    rows = outs[0].shape[0]
    for index, ref in enumerate(outs):
        ref[...] = total[index * rows : (index + 1) * rows].astype(ref.dtype)


def compiler_params():
    return pltpu.CompilerParams(vmem_limit_bytes=VMEM_LIMIT)


def small_cost(many, hidden):
    return pl.CostEstimate(flops=many * hidden, bytes_accessed=many, transcendentals=0)


def home_shapes(count, rows, width):
    own, others = (jax.ShapeDtypeStruct((rows, width), kind) for kind in (F32, BF16))
    return [own] + [others] * (count - 1)


def hidden_kernel(count, pieces, steps, at_ref, *refs):
    tags, rows_in, gate_ups = refs[:count], refs[count : 2 * count], refs[2 * count : -3]
    out_ref, gate_ref, up_ref = refs[-3:]
    step = pl.program_id(0)

    @pl.when(step == 0)
    def _():
        gate_ref[...] = jnp.zeros_like(gate_ref)
        up_ref[...] = jnp.zeros_like(up_ref)

    x = gathered_rows(rows_in)
    gate_ref[...] += jnp.dot(x, joined(gate_ups, 1, 0), preferred_element_type=F32)
    up_ref[...] += jnp.dot(x, joined(gate_ups, 1, 1), preferred_element_type=F32)

    @pl.when(step == steps - 1)
    def _():
        gate, up = gate_ref[...], up_ref[...]
        keep = own_hidden(at_ref, gathered_rows(tags), 0, gate.shape[1])
        out_ref[...] = jnp.where(keep, gate * jax.nn.sigmoid(gate) * up, 0.0).astype(BF16)


def hidden_call(at, x_gathered, rows, width, gate_ups):
    count, pieces, hid = x_gathered.shape[0], len(gate_ups), gate_ups[0].shape[2]
    chunk = chunk_of(width, 1792)
    steps, hidden, many = width // chunk, pieces * hid, count * rows
    _, arrays, specs = gathered_input(x_gathered, 0, rows)
    return pl.pallas_call(
        functools.partial(hidden_kernel, count, pieces, steps),
        grid_spec=pltpu.PrefetchScalarGridSpec(
            num_scalar_prefetch=1,
            grid=(steps,),
            in_specs=[spec(TAG_COLUMNS, lambda i: width // TAG_COLUMNS) for spec in specs]
            + [spec(chunk, lambda i: i) for spec in specs]
            + [pl.BlockSpec((2, chunk, hid), lambda i, at: (0, i, 0))] * pieces,
            out_specs=pl.BlockSpec((many, hidden), lambda i, at: (0, 0)),
            scratch_shapes=[pltpu.VMEM((many, hidden), F32)] * 2,
        ),
        out_shape=jax.ShapeDtypeStruct((many, hidden), BF16),
        compiler_params=compiler_params(),
        cost_estimate=small_cost(many, hidden),
    )(at, *arrays, *arrays, *gate_ups)


def down_kernel(pieces, hidden_ref, *refs):
    downs, outs = refs[:pieces], refs[pieces:]
    total = jnp.dot(hidden_ref[...], joined(downs, 0), preferred_element_type=F32)
    put_blocks(outs, total)


def down_call(hidden_rows, count, downs):
    many, hidden = hidden_rows.shape
    pieces, (hid, width), rows = len(downs), downs[0].shape, many // count
    chunk = chunk_of(width, 1792)
    return pl.pallas_call(
        functools.partial(down_kernel, pieces),
        grid=(width // chunk,),
        in_specs=[pl.BlockSpec((many, hidden), lambda i: (0, 0))]
        + [pl.BlockSpec((hid, chunk), lambda i: (0, i))] * pieces,
        out_specs=[pl.BlockSpec((rows, chunk), lambda i: (0, i))] * count,
        out_shape=home_shapes(count, rows, width),
        compiler_params=compiler_params(),
        cost_estimate=small_cost(many, hidden),
    )(hidden_rows, *downs)


def backward_kernel(inputs, count, pieces, chunk, steps, at_ref, *refs):
    tags, refs = refs[:count], refs[count:]
    rows_in, scaled_in, refs = refs[:inputs], refs[inputs : 2 * inputs], refs[2 * inputs :]
    gate_ups, downs, outs = refs[:pieces], refs[pieces : 2 * pieces], refs[2 * pieces : -8]
    gate_ref, up_ref, grad_ref, grad_gate_ref, grad_up_ref = refs[-8:-3]
    gate_up_held, down_held, sems = refs[-3:]
    step = pl.program_id(0)
    copies = weight_copies(chunk, steps, gate_ups, downs, gate_up_held, down_held, sems)

    @pl.when(step == 0)
    def _():
        for of_gate_up, of_down in copies:
            for copy in of_gate_up + of_down:
                copy.start()
        for total in (gate_ref, up_ref, grad_ref):
            total[...] = jnp.zeros_like(total)

    for number, (of_gate_up, of_down) in enumerate(copies):

        @pl.when(step == number)
        def _(waited=of_gate_up + of_down):
            for copy in waited:
                copy.wait()

    at_chunk = pl.ds(pl.multiple_of(lax.rem(step, steps) * chunk, chunk), chunk)

    def gate_or_up(which):
        return jnp.concatenate(
            [gate_up_held[i, which, at_chunk, :] for i in range(pieces)], axis=1
        )

    @pl.when(step < steps)
    def _():
        x = chained_rows(rows_in)
        gate_ref[...] += jnp.dot(x, gate_or_up(0), preferred_element_type=F32)
        up_ref[...] += jnp.dot(x, gate_or_up(1), preferred_element_type=F32)
        down = jnp.concatenate([down_held[i, :, at_chunk] for i in range(pieces)], axis=0)
        grad_ref[...] += contract_last(chained_rows(scaled_in), down)

    @pl.when(step == steps - 1)
    def _():
        gate, up, grad = gate_ref[...], up_ref[...], grad_ref[...]
        keep = own_hidden(at_ref, gathered_rows(tags), TAG_COLUMNS // 2, gate.shape[1])
        s = jax.nn.sigmoid(gate)
        silu = gate * s
        grad_gate = grad * up * (s + silu * (1.0 - s))
        grad_gate_ref[...] = jnp.where(keep, grad_gate, 0.0).astype(BF16)
        grad_up_ref[...] = jnp.where(keep, grad * silu, 0.0).astype(BF16)

    @pl.when(step >= steps)
    def _():
        total = contract_last(grad_gate_ref[...], gate_or_up(0))
        total += contract_last(grad_up_ref[...], gate_or_up(1))
        put_blocks(outs, total)


def backward_call(at, x_gathered, begin, rows, hops, gate_ups, downs):
    count, width = x_gathered.shape[0], hops[0][0].shape[1]
    pieces, hid = len(downs), downs[0].shape[0]
    chunk = chunk_of(width, 1792)
    steps, hidden, many = width // chunk, pieces * hid, count * rows
    first = lambda i: jnp.minimum(i, steps - 1)
    second = lambda i: jnp.maximum(i - steps, 0)
    _, tags, tag_specs = gathered_input(x_gathered, begin, rows)
    _, rows_in, row_specs = chained_input(hops, 0, rows)
    _, _, scaled_specs = chained_input(hops, rows, rows)
    return pl.pallas_call(
        functools.partial(backward_kernel, len(rows_in), count, pieces, chunk, steps),
        grid_spec=pltpu.PrefetchScalarGridSpec(
            num_scalar_prefetch=1,
            grid=(2 * steps,),
            in_specs=[spec(TAG_COLUMNS, lambda i: width // TAG_COLUMNS) for spec in tag_specs]
            + [spec(chunk, first) for spec in row_specs + scaled_specs]
            + [pl.BlockSpec(memory_space=pl.ANY)] * (2 * pieces),
            out_specs=[pl.BlockSpec((rows, chunk), lambda i, at: (0, second(i)))] * count,
            scratch_shapes=[pltpu.VMEM((many, hidden), F32)] * 3
            + [pltpu.VMEM((many, hidden), BF16)] * 2
            + [
                pltpu.VMEM((pieces, 2, width, hid), BF16),
                pltpu.VMEM((pieces, hid, width), BF16),
                pltpu.SemaphoreType.DMA((2, steps, pieces)),
            ],
        ),
        out_shape=home_shapes(count, rows, width),
        compiler_params=compiler_params(),
        cost_estimate=small_cost(many, hidden),
    )(at, *tags, *rows_in, *rows_in, *gate_ups, *downs)


def after(value, *earlier):
    return lax.optimization_barrier((value, earlier))[0]


def hop(below, above, axis, step):
    count = lax.axis_size(axis)
    up = [(i, i + 1) for i in range(step - 1, count - 1)]
    down = [(i, i - 1) for i in range(1, count - step + 1)]
    return lax.ppermute(below, axis, up), lax.ppermute(above, axis, down)


def summands(blocks, step, arrived):
    pair = (blocks[len(blocks) - step], blocks[step])
    if arrived is None:
        return pair
    return tuple(
        (own.astype(F32) + other.astype(F32)).astype(BF16) for own, other in zip(pair, arrived)
    )


def step_home(pair, axis, step):
    count = lax.axis_size(axis)
    up = lax.ppermute(pair[0], axis, [(i, i + 1) for i in range(step)])
    down = lax.ppermute(pair[1], axis, [(i, i - 1) for i in range(count - step, count)])
    return up, down


def summed(block, arrived):
    for part in arrived:
        block = block + part.astype(F32)
    return block


def few_experts(
    x_forward,
    route_forward,
    prob_forward,
    x_backward,
    route_backward,
    prob_backward,
    grad_output,
    w_gate,
    w_up,
    w_down,
):
    tokens_here, width = x_forward.shape[1:]
    expert_here = lax.axis_index("expert") // 2
    count = lax.axis_size("dp")
    at = jnp.stack([lax.axis_index("dp"), expert_here]).astype(jnp.int32)
    lead = min(LEAD_ROWS, tokens_here // 2)
    main = tokens_here - lead
    ends = (slice(0, main), slice(main, tokens_here))

    half_tag = (tokens_here, TAG_COLUMNS // 2)
    tagged = jnp.concatenate(
        [x_forward[0]]
        + [jnp.broadcast_to(r[0].astype(BF16), half_tag) for r in (route_forward, route_backward)],
        axis=1,
    )
    scaled_grad = (prob_backward[0][:, None] * grad_output[0].astype(F32)).astype(BF16)
    main_rows, lead_rows = (
        jnp.concatenate([x_backward[0, rows], scaled_grad[rows]], axis=0) for rows in ends
    )
    gate_up, down = jnp.concatenate([w_gate[0], w_up[0]], axis=0), w_down[0, 0]

    x_gathered = lax.all_gather(tagged, "dp")
    across_gate_up = flipped(gate_up, "expert", 2)
    across_down = flipped(down, "expert", 2)
    hops_main = [(main_rows, main_rows)]
    for step in range(1, count):
        hops_main.append(hop(*hops_main[-1], "dp", step))
    gate_ups = [gate_up, flipped(gate_up, "expert", 1), across_gate_up]
    downs = [down, flipped(down, "expert", 1), across_down]
    waits = (x_gathered, hops_main[1], gate_ups[1], downs[1])
    gate_ups.append(flipped(after(across_gate_up, waits), "expert", 1))
    hidden_fwd = hidden_call(at, x_gathered, tokens_here, width, gate_ups)
    downs.append(flipped(after(across_down, hops_main[2], hidden_fwd), "expert", 1))
    partial_fwd = down_call(hidden_fwd, count, downs)

    arrived_fwd = step_home(summands(partial_fwd, 1, None), "dp", 1)
    lead_rows = after(lead_rows, hops_main[3])
    hops_lead = [(lead_rows, lead_rows)]
    hops_lead.append(hop(*hops_lead[-1], "dp", 1))
    sends_fwd = summands(partial_fwd, 2, arrived_fwd)
    arrived_fwd = step_home(sends_fwd, "dp", 2)
    main_in = after(hops_main[:1], sends_fwd) + hops_main[1:]
    partial_main = backward_call(at, x_gathered, 0, main, main_in, gate_ups, downs)

    arrived_fwd, hops_lead[1] = after((arrived_fwd, hops_lead[1]), partial_main[1])
    arrived_fwd = step_home(summands(partial_fwd, 3, arrived_fwd), "dp", 3)
    arrived_main = step_home(summands(partial_main, 1, None), "dp", 1)
    for step in range(2, count):
        hops_lead.append(hop(*hops_lead[-1], "dp", step))
    partial_lead = backward_call(at, x_gathered, main, lead, hops_lead, gate_ups, downs)

    arrived_fwd, arrived_main = after((arrived_fwd, arrived_main), partial_lead[1])
    arrived_main = step_home(summands(partial_main, 2, arrived_main), "dp", 2)
    arrived_lead = step_home(summands(partial_lead, 1, None), "dp", 1)
    total_fwd = summed(partial_fwd[0], arrived_fwd)
    layer_out = (x_forward[0].astype(F32) + prob_forward[0][:, None] * total_fwd).astype(BF16)
    sent_fwd = shifted(layer_out, "pipe", 1)

    def sent_back(rows, block, arrived):
        grad_in = (grad_output[0, rows].astype(F32) + summed(block, arrived)).astype(BF16)
        return shifted(grad_in, "pipe", -1)

    arrived_main = after(arrived_main, sent_fwd)
    arrived_main = step_home(summands(partial_main, 3, arrived_main), "dp", 3)
    arrived_lead = step_home(summands(partial_lead, 2, arrived_lead), "dp", 2)
    sent_main = sent_back(ends[0], partial_main[0], arrived_main)
    arrived_lead = step_home(summands(partial_lead, 3, arrived_lead), "dp", 3)
    sent_lead = sent_back(ends[1], partial_lead[0], after(arrived_lead, sent_main))
    return (sent_fwd[None], jnp.concatenate([sent_main, sent_lead], axis=0)[None])


def from_partner(block, axis, stride):
    count = lax.axis_size(axis)
    route = []
    for low in range(count):
        high = low | 1 << stride
        if high != low and high < count:
            route += [(low, high), (high, low)]
    return lax.ppermute(block, axis, route)


def silu_parts(pre_gate):
    sigma_gate = jax.nn.sigmoid(pre_gate)
    return (pre_gate * sigma_gate, sigma_gate)


def expert_pass(forward_rows, backward_rows, scaled_rows, gate_weight, up_weight, down_weight):
    gate_fwd = jnp.dot(forward_rows, gate_weight, preferred_element_type=jnp.float32)
    up_fwd = jnp.dot(forward_rows, up_weight, preferred_element_type=jnp.float32)
    silu_fwd, sigma_fwd = silu_parts(gate_fwd)
    hidden_fwd = (silu_fwd * up_fwd).astype(jnp.bfloat16)
    expert_out = jnp.dot(hidden_fwd, down_weight, preferred_element_type=jnp.float32)
    gate_bwd = jnp.dot(backward_rows, gate_weight, preferred_element_type=jnp.float32)
    up_bwd = jnp.dot(backward_rows, up_weight, preferred_element_type=jnp.float32)
    silu_bwd, sigma_bwd = silu_parts(gate_bwd)
    grad_hidden = contract_last(scaled_rows, down_weight)
    grad_gate = (grad_hidden * up_bwd * (sigma_bwd + silu_bwd * (1.0 - sigma_bwd))).astype(
        jnp.bfloat16
    )
    grad_up = (grad_hidden * silu_bwd).astype(jnp.bfloat16)
    grad_rows = contract_last(grad_gate, gate_weight) + contract_last(grad_up, up_weight)
    return (expert_out, grad_rows)


def placing(routes, experts_here, capacity):
    route_hits = (routes[:, None] == jnp.arange(experts_here, dtype=jnp.int32)[None, :]).astype(
        jnp.int32
    )
    before = jnp.cumsum(route_hits, axis=0) - route_hits
    slot_index = jnp.sum(before * route_hits, axis=1)
    position = routes * capacity + slot_index
    selector = (
        position[None, :] == jnp.arange(experts_here * capacity, dtype=jnp.int32)[:, None]
    ).astype(jnp.bfloat16)
    return (position, selector)


def packing(selector, values):
    return jnp.dot(selector, values, preferred_element_type=jnp.float32).astype(jnp.bfloat16)


def many_experts(
    x_forward,
    route_forward,
    prob_forward,
    x_backward,
    route_backward,
    prob_backward,
    grad_output,
    w_gate,
    w_up,
    w_down,
):
    tokens_here = x_forward.shape[1]
    feature_width = x_forward.shape[2]
    groups = lax.axis_size("expert")
    experts_here = groups // 2
    capacity = min(tokens_here, (tokens_here * 5 + 4 * experts_here - 1) // (4 * experts_here))
    pair_side = lax.axis_index("expert") % 2
    gate_full, up_full, down_full = (
        lax.all_gather(w_gate[0, 0], "dp", axis=1, tiled=True),
        lax.all_gather(w_up[0, 0], "dp", axis=1, tiled=True),
        lax.all_gather(w_down[0, 0], "dp", axis=0, tiled=True),
    )
    pos_fwd, select_fwd = placing(route_forward[0, :, 0], experts_here, capacity)
    pos_bwd, select_bwd = placing(route_backward[0, :, 0], experts_here, capacity)
    scaled_grad = (prob_backward[0][:, None] * grad_output[0].astype(jnp.float32)).astype(
        jnp.bfloat16
    )
    stacked = jnp.stack(
        [
            packing(select_fwd, x_forward[0]),
            packing(select_bwd, x_backward[0]),
            packing(select_bwd, scaled_grad),
        ]
    )
    stacked = stacked.reshape(3, experts_here, capacity, feature_width)
    split_rows = stacked.reshape(3, experts_here, capacity, 2, feature_width // 2).transpose(
        0, 1, 3, 2, 4
    )
    split_rows = split_rows.reshape(3, groups, capacity, feature_width // 2)
    own_half = lax.all_to_all(split_rows, "expert", split_axis=1, concat_axis=1, tiled=True)
    partner_half = from_partner(own_half, "expert", 0)
    arrived = jnp.where(
        pair_side == 0,
        jnp.concatenate([own_half, partner_half], axis=3),
        jnp.concatenate([partner_half, own_half], axis=3),
    )
    expert_rows = arrived.reshape(3, groups * capacity, feature_width)
    expert_out, grad_rows = expert_pass(
        expert_rows[0], expert_rows[1], expert_rows[2], gate_full, up_full, down_full
    )
    results = jnp.stack([expert_out, grad_rows]).reshape(2, groups, capacity, feature_width)
    quarters = results.reshape(2, groups, capacity, 2, feature_width // 2)
    keep_part = jnp.where(pair_side == 0, quarters[:, :, :, 0], quarters[:, :, :, 1])
    give_part = jnp.where(pair_side == 0, quarters[:, :, :, 1], quarters[:, :, :, 0])
    finished = keep_part + from_partner(give_part.astype(jnp.bfloat16), "expert", 0).astype(
        give_part.dtype
    )
    returned = lax.all_to_all(finished, "expert", split_axis=1, concat_axis=1, tiled=True)
    combined = returned.reshape(2, experts_here, 2, capacity, feature_width // 2).transpose(
        0, 1, 3, 2, 4
    )
    combined = combined.reshape(2, experts_here, capacity, feature_width)
    flat_out = combined.reshape(2, experts_here * capacity, feature_width)
    moved_fwd = jnp.take(flat_out[0], pos_fwd, axis=0)
    moved_bwd = jnp.take(flat_out[1], pos_bwd, axis=0)
    layer_out = (x_forward[0].astype(jnp.float32) + prob_forward[0][:, None] * moved_fwd).astype(
        jnp.bfloat16
    )
    grad_in = (grad_output[0].astype(jnp.float32) + moved_bwd).astype(jnp.bfloat16)
    sent_fwd = shifted(layer_out, "pipe", 1)
    sent_bwd = shifted(grad_in, "pipe", -1)
    return (sent_fwd[None], sent_bwd[None])


def solution(mesh):
    few = mesh.shape["expert"] == 4
    return jax.shard_map(
        few_experts if few else many_experts,
        mesh=mesh,
        in_specs=(
            P("pipe", ("expert", "dp"), None),
            P("pipe", ("expert", "dp"), None),
            P("pipe", ("expert", "dp")),
            P("pipe", ("expert", "dp"), None),
            P("pipe", ("expert", "dp"), None),
            P("pipe", ("expert", "dp")),
            P("pipe", ("expert", "dp"), None),
            P("pipe", "expert", None, "dp"),
            P("pipe", "expert", None, "dp"),
            P("pipe", "expert", "dp", None),
        ),
        out_specs=(P("pipe", ("expert", "dp"), None), P("pipe", ("expert", "dp"), None)),
        check_vma=False,
    )
```

```python
import functools
import math

import jax
import jax.numpy as jnp
from jax import lax
from jax.experimental import pallas as pl
from jax.experimental.pallas import tpu as pltpu
from jax.sharding import PartitionSpec as P

BF16, F32 = jnp.bfloat16, jnp.float32
VMEM_LIMIT = 56 * 1024 * 1024
ROW_PARTS = 2
TAG_COLUMNS = 128


def contract_last(left_side, weights):
    return lax.dot_general(
        left_side, weights, (((1,), (1,)), ((), ())), preferred_element_type=F32
    )


def flipped(block, axis, stride):
    route = [(i, i ^ stride) for i in range(lax.axis_size(axis))]
    return lax.ppermute(block, axis, route)


def shifted(block, axis, distance):
    count = lax.axis_size(axis)
    return lax.ppermute(block, axis, [((i - distance) % count, i) for i in range(count)])


def chunk_of(width, most):
    best = 128
    for size in range(128, most + 1, 128):
        if width % size == 0:
            best = size
    return best


def gathered_rows(refs):
    return jnp.concatenate([ref[0] for ref in refs], axis=0)


def chained_rows(refs):
    others = len(refs) // 2
    own, below, above = refs[0][...], refs[1 : 1 + others], refs[1 + others :]
    return jnp.concatenate(
        [own] + [above[away][...] + below[others - 1 - away][...] for away in range(others)],
        axis=0,
    )


def gathered_input(x, begin, rows):
    count, unit = x.shape[0], math.gcd(begin, rows)
    arrays, specs = [], []
    for turn in range(count):
        for piece in range(begin // unit, (begin + rows) // unit):
            arrays.append(x)
            specs.append(
                lambda chunk, column, turn=turn, piece=piece: pl.BlockSpec(
                    (1, unit, chunk),
                    lambda i, at: (lax.rem(at[0] + turn, count), piece, column(i)),
                )
            )
    return gathered_rows, arrays, specs


def chained_input(hops, begin, rows):
    (own, _), *others = hops
    from_below, from_above = zip(*others)
    spec = lambda chunk, column: pl.BlockSpec(
        (rows, chunk), lambda i, at: (begin // rows, column(i))
    )
    arrays = [own, *from_below, *from_above]
    return chained_rows, arrays, [spec] * len(arrays)


def weight_copies(chunk, steps, gate_ups, downs, gate_up_held, down_held, sems):
    by_chunk = []
    for step in range(steps):
        part = pl.ds(step * chunk, chunk)
        by_chunk.append(
            (
                [
                    pltpu.make_async_copy(
                        ref.at[:, part, :], gate_up_held.at[i, :, part, :], sems.at[0, step, i]
                    )
                    for i, ref in enumerate(gate_ups)
                ],
                [
                    pltpu.make_async_copy(
                        ref.at[:, part], down_held.at[i, :, part], sems.at[1, step, i]
                    )
                    for i, ref in enumerate(downs)
                ],
            )
        )
    return by_chunk


def own_hidden(at_ref, tags, column, hidden):
    mine = tags[:, column : column + 1].astype(jnp.int32) == at_ref[1]
    unit = lax.broadcasted_iota(jnp.int32, (tags.shape[0], hidden), 1)
    return mine == (unit < hidden // 2)


def joined(refs, axis, index=None):
    pick = (lambda ref: ref[...]) if index is None else (lambda ref: ref[index])
    return jnp.concatenate([pick(ref) for ref in refs], axis=axis)


def put_blocks(outs, total):
    rows = outs[0].shape[0]
    for index, ref in enumerate(outs):
        ref[...] = total[index * rows : (index + 1) * rows].astype(ref.dtype)


def compiler_params():
    return pltpu.CompilerParams(vmem_limit_bytes=VMEM_LIMIT)


def small_cost(many, hidden):
    return pl.CostEstimate(flops=many * hidden, bytes_accessed=many, transcendentals=0)


def home_shapes(count, rows, width, parts=1):
    own, others = (jax.ShapeDtypeStruct((rows // parts, width), kind) for kind in (F32, BF16))
    return [own] * parts + [others] * (parts * (count - 1))


def hidden_kernel(count, pieces, steps, at_ref, *refs):
    tags, rows_in, gate_ups = refs[:count], refs[count : 2 * count], refs[2 * count : -3]
    out_ref, gate_ref, up_ref = refs[-3:]
    step = pl.program_id(0)

    @pl.when(step == 0)
    def _():
        gate_ref[...] = jnp.zeros_like(gate_ref)
        up_ref[...] = jnp.zeros_like(up_ref)

    x = gathered_rows(rows_in)
    gate_ref[...] += jnp.dot(x, joined(gate_ups, 1, 0), preferred_element_type=F32)
    up_ref[...] += jnp.dot(x, joined(gate_ups, 1, 1), preferred_element_type=F32)

    @pl.when(step == steps - 1)
    def _():
        gate, up = gate_ref[...], up_ref[...]
        keep = own_hidden(at_ref, gathered_rows(tags), 0, gate.shape[1])
        out_ref[...] = jnp.where(keep, gate * jax.nn.sigmoid(gate) * up, 0.0).astype(BF16)


def hidden_call(at, x_gathered, rows, width, gate_ups):
    count, pieces, hid = x_gathered.shape[0], len(gate_ups), gate_ups[0].shape[2]
    chunk = chunk_of(width, 1792)
    steps, hidden, many = width // chunk, pieces * hid, count * rows
    _, arrays, specs = gathered_input(x_gathered, 0, rows)
    return pl.pallas_call(
        functools.partial(hidden_kernel, count, pieces, steps),
        grid_spec=pltpu.PrefetchScalarGridSpec(
            num_scalar_prefetch=1,
            grid=(steps,),
            in_specs=[spec(TAG_COLUMNS, lambda i: width // TAG_COLUMNS) for spec in specs]
            + [spec(chunk, lambda i: i) for spec in specs]
            + [pl.BlockSpec((2, chunk, hid), lambda i, at: (0, i, 0))] * pieces,
            out_specs=pl.BlockSpec((many, hidden), lambda i, at: (0, 0)),
            scratch_shapes=[pltpu.VMEM((many, hidden), F32)] * 2,
        ),
        out_shape=jax.ShapeDtypeStruct((many, hidden), BF16),
        compiler_params=compiler_params(),
        cost_estimate=small_cost(many, hidden),
    )(at, *arrays, *arrays, *gate_ups)


def down_kernel(pieces, hidden_ref, *refs):
    downs, outs = refs[:pieces], refs[pieces:]
    total = jnp.dot(hidden_ref[...], joined(downs, 0), preferred_element_type=F32)
    put_blocks(outs, total)


def down_call(hidden_rows, count, downs):
    many, hidden = hidden_rows.shape
    pieces, (hid, width), rows = len(downs), downs[0].shape, many // count
    chunk = chunk_of(width, 1792)
    return pl.pallas_call(
        functools.partial(down_kernel, pieces),
        grid=(width // chunk,),
        in_specs=[pl.BlockSpec((many, hidden), lambda i: (0, 0))]
        + [pl.BlockSpec((hid, chunk), lambda i: (0, i))] * pieces,
        out_specs=[pl.BlockSpec((rows, chunk), lambda i: (0, i))] * count,
        out_shape=home_shapes(count, rows, width),
        compiler_params=compiler_params(),
        cost_estimate=small_cost(many, hidden),
    )(hidden_rows, *downs)


def backward_kernel(inputs, count, pieces, chunk, steps, at_ref, *refs):
    tags, refs = refs[:count], refs[count:]
    rows_in, scaled_in, refs = refs[:inputs], refs[inputs : 2 * inputs], refs[2 * inputs :]
    gate_ups, downs, outs = refs[:pieces], refs[pieces : 2 * pieces], refs[2 * pieces : -8]
    gate_ref, up_ref, grad_ref, grad_gate_ref, grad_up_ref = refs[-8:-3]
    gate_up_held, down_held, sems = refs[-3:]
    step = pl.program_id(0)
    copies = weight_copies(chunk, steps, gate_ups, downs, gate_up_held, down_held, sems)

    @pl.when(step == 0)
    def _():
        for of_gate_up, of_down in copies:
            for copy in of_gate_up + of_down:
                copy.start()
        for total in (gate_ref, up_ref, grad_ref):
            total[...] = jnp.zeros_like(total)

    for number, (of_gate_up, of_down) in enumerate(copies):

        @pl.when(step == number)
        def _(waited=of_gate_up + of_down):
            for copy in waited:
                copy.wait()

    at_chunk = pl.ds(pl.multiple_of(lax.rem(step, steps) * chunk, chunk), chunk)

    def gate_or_up(which):
        return jnp.concatenate(
            [gate_up_held[i, which, at_chunk, :] for i in range(pieces)], axis=1
        )

    @pl.when(step < steps)
    def _():
        x = chained_rows(rows_in)
        gate_ref[...] += jnp.dot(x, gate_or_up(0), preferred_element_type=F32)
        up_ref[...] += jnp.dot(x, gate_or_up(1), preferred_element_type=F32)
        down = jnp.concatenate([down_held[i, :, at_chunk] for i in range(pieces)], axis=0)
        grad_ref[...] += contract_last(chained_rows(scaled_in), down)

    @pl.when(step == steps - 1)
    def _():
        gate, up, grad = gate_ref[...], up_ref[...], grad_ref[...]
        keep = own_hidden(at_ref, gathered_rows(tags), TAG_COLUMNS // 2, gate.shape[1])
        s = jax.nn.sigmoid(gate)
        silu = gate * s
        grad_gate = grad * up * (s + silu * (1.0 - s))
        grad_gate_ref[...] = jnp.where(keep, grad_gate, 0.0).astype(BF16)
        grad_up_ref[...] = jnp.where(keep, grad * silu, 0.0).astype(BF16)

    @pl.when(step >= steps)
    def _():
        total = contract_last(grad_gate_ref[...], gate_or_up(0))
        total += contract_last(grad_up_ref[...], gate_or_up(1))
        put_blocks(outs, total)


def backward_call(at, x_gathered, rows, parts, hops, gate_ups, downs):
    count, width = x_gathered.shape[0], hops[0][0].shape[1]
    pieces, hid = len(downs), downs[0].shape[0]
    chunk = chunk_of(width, 1792)
    steps, hidden, many = width // chunk, pieces * hid, count * rows
    first = lambda i: jnp.minimum(i, steps - 1)
    second = lambda i: jnp.maximum(i - steps, 0)
    _, tags, tag_specs = gathered_input(x_gathered, 0, rows)
    _, rows_in, row_specs = chained_input(hops, 0, rows)
    _, _, scaled_specs = chained_input(hops, rows, rows)
    return pl.pallas_call(
        functools.partial(backward_kernel, len(rows_in), count, pieces, chunk, steps),
        grid_spec=pltpu.PrefetchScalarGridSpec(
            num_scalar_prefetch=1,
            grid=(2 * steps,),
            in_specs=[spec(TAG_COLUMNS, lambda i: width // TAG_COLUMNS) for spec in tag_specs]
            + [spec(chunk, first) for spec in row_specs + scaled_specs]
            + [pl.BlockSpec(memory_space=pl.ANY)] * (2 * pieces),
            out_specs=[pl.BlockSpec((rows // parts, chunk), lambda i, at: (0, second(i)))]
            * (parts * count),
            scratch_shapes=[pltpu.VMEM((many, hidden), F32)] * 3
            + [pltpu.VMEM((many, hidden), BF16)] * 2
            + [
                pltpu.VMEM((pieces, 2, width, hid), BF16),
                pltpu.VMEM((pieces, hid, width), BF16),
                pltpu.SemaphoreType.DMA((2, steps, pieces)),
            ],
        ),
        out_shape=home_shapes(count, rows, width, parts),
        compiler_params=compiler_params(),
        cost_estimate=small_cost(many, hidden),
    )(at, *tags, *rows_in, *rows_in, *gate_ups, *downs)


def after(value, *earlier):
    return lax.optimization_barrier((value, earlier))[0]


def hop(below, above, axis, step):
    count = lax.axis_size(axis)
    up = [(i, i + 1) for i in range(step - 1, count - 1)]
    down = [(i, i - 1) for i in range(1, count - step + 1)]
    return lax.ppermute(below, axis, up), lax.ppermute(above, axis, down)


def summands(blocks, step, arrived):
    pair = (blocks[len(blocks) - step], blocks[step])
    if arrived is None:
        return pair
    return tuple(
        (own.astype(F32) + other.astype(F32)).astype(BF16) for own, other in zip(pair, arrived)
    )


def step_home(pair, axis, step):
    count = lax.axis_size(axis)
    up = lax.ppermute(pair[0], axis, [(i, i + 1) for i in range(step)])
    down = lax.ppermute(pair[1], axis, [(i, i - 1) for i in range(count - step, count)])
    return up, down


def summed(block, arrived):
    for part in arrived:
        block = block + part.astype(F32)
    return block


def few_experts(
    x_forward,
    route_forward,
    prob_forward,
    x_backward,
    route_backward,
    prob_backward,
    grad_output,
    w_gate,
    w_up,
    w_down,
):
    tokens_here, width = x_forward.shape[1:]
    expert_here = lax.axis_index("expert") // 2
    count = lax.axis_size("dp")
    at = jnp.stack([lax.axis_index("dp"), expert_here]).astype(jnp.int32)
    half_tag = (tokens_here, TAG_COLUMNS // 2)
    tagged = jnp.concatenate(
        [x_forward[0]]
        + [jnp.broadcast_to(r[0].astype(BF16), half_tag) for r in (route_forward, route_backward)],
        axis=1,
    )
    scaled_grad = (prob_backward[0][:, None] * grad_output[0].astype(F32)).astype(BF16)
    back_rows = jnp.concatenate([x_backward[0], scaled_grad], axis=0)
    gate_up, down = jnp.concatenate([w_gate[0], w_up[0]], axis=0), w_down[0, 0]

    x_gathered = lax.all_gather(tagged, "dp")
    across_down = flipped(down, "expert", 2)
    gate_up, back_rows = after((gate_up, back_rows), across_down)
    across_gate_up = flipped(gate_up, "expert", 2)
    hops = [(back_rows, back_rows)]
    for step in range(1, count):
        hops.append(hop(*hops[-1], "dp", step))
    gate_ups = [gate_up, flipped(after(gate_up, hops[1]), "expert", 1), across_gate_up]
    downs = [down, flipped(down, "expert", 1), across_down, flipped(across_down, "expert", 1)]
    gate_ups.append(flipped(after(across_gate_up, x_gathered, hops[1], downs[1:]), "expert", 1))
    hidden_fwd = hidden_call(at, x_gathered, tokens_here, width, gate_ups)
    partial_fwd = down_call(hidden_fwd, count, downs)

    arrived_fwd = step_home(summands(partial_fwd, 1, None), "dp", 1)
    arrived_fwd = after(arrived_fwd, hops[2])
    arrived_fwd = step_home(summands(partial_fwd, 2, arrived_fwd), "dp", 2)
    sends_fwd = summands(partial_fwd, 3, arrived_fwd)
    arrived_fwd = step_home(sends_fwd, "dp", 3)
    hops[0] = after(hops[0], sends_fwd)
    partial_bwd = backward_call(at, x_gathered, tokens_here, ROW_PARTS, hops, gate_ups, downs)

    arrived_fwd = after(arrived_fwd, partial_bwd[-1])
    total_fwd = summed(partial_fwd[0], arrived_fwd)
    layer_out = (x_forward[0].astype(F32) + prob_forward[0][:, None] * total_fwd).astype(BF16)
    sent_fwd = shifted(layer_out, "pipe", 1)
    size = tokens_here // ROW_PARTS
    partial_bwd = after(tuple(partial_bwd), arrived_fwd)
    blocks = [partial_bwd[part::ROW_PARTS] for part in range(ROW_PARTS)]
    arrived = [None] * ROW_PARTS
    for step in range(1, count):
        for part in range(ROW_PARTS):
            if step == 3 and part == 0:
                arrived[0] = after(arrived[0], sent_fwd)
            arrived[part] = step_home(summands(blocks[part], step, arrived[part]), "dp", step)
    sent_bwd = []
    for part in range(ROW_PARTS):
        rows = slice(part * size, (part + 1) * size)
        total = summed(blocks[part][0], after(arrived[part], sent_bwd))
        grad_in = (grad_output[0, rows].astype(F32) + total).astype(BF16)
        sent_bwd.append(shifted(grad_in, "pipe", -1))
    return (sent_fwd[None], jnp.concatenate(sent_bwd, axis=0)[None])


def from_partner(block, axis, stride):
    count = lax.axis_size(axis)
    route = []
    for low in range(count):
        high = low | 1 << stride
        if high != low and high < count:
            route += [(low, high), (high, low)]
    return lax.ppermute(block, axis, route)


def silu_parts(pre_gate):
    sigma_gate = jax.nn.sigmoid(pre_gate)
    return (pre_gate * sigma_gate, sigma_gate)


def expert_pass(forward_rows, backward_rows, scaled_rows, gate_weight, up_weight, down_weight):
    gate_fwd = jnp.dot(forward_rows, gate_weight, preferred_element_type=jnp.float32)
    up_fwd = jnp.dot(forward_rows, up_weight, preferred_element_type=jnp.float32)
    silu_fwd, sigma_fwd = silu_parts(gate_fwd)
    hidden_fwd = (silu_fwd * up_fwd).astype(jnp.bfloat16)
    expert_out = jnp.dot(hidden_fwd, down_weight, preferred_element_type=jnp.float32)
    gate_bwd = jnp.dot(backward_rows, gate_weight, preferred_element_type=jnp.float32)
    up_bwd = jnp.dot(backward_rows, up_weight, preferred_element_type=jnp.float32)
    silu_bwd, sigma_bwd = silu_parts(gate_bwd)
    grad_hidden = contract_last(scaled_rows, down_weight)
    grad_gate = (grad_hidden * up_bwd * (sigma_bwd + silu_bwd * (1.0 - sigma_bwd))).astype(
        jnp.bfloat16
    )
    grad_up = (grad_hidden * silu_bwd).astype(jnp.bfloat16)
    grad_rows = contract_last(grad_gate, gate_weight) + contract_last(grad_up, up_weight)
    return (expert_out, grad_rows)


def placing(routes, experts_here, capacity):
    route_hits = (routes[:, None] == jnp.arange(experts_here, dtype=jnp.int32)[None, :]).astype(
        jnp.int32
    )
    before = jnp.cumsum(route_hits, axis=0) - route_hits
    slot_index = jnp.sum(before * route_hits, axis=1)
    position = routes * capacity + slot_index
    selector = (
        position[None, :] == jnp.arange(experts_here * capacity, dtype=jnp.int32)[:, None]
    ).astype(jnp.bfloat16)
    return (position, selector)


def packing(selector, values):
    return jnp.dot(selector, values, preferred_element_type=jnp.float32).astype(jnp.bfloat16)


def many_experts(
    x_forward,
    route_forward,
    prob_forward,
    x_backward,
    route_backward,
    prob_backward,
    grad_output,
    w_gate,
    w_up,
    w_down,
):
    tokens_here = x_forward.shape[1]
    feature_width = x_forward.shape[2]
    groups = lax.axis_size("expert")
    experts_here = groups // 2
    capacity = min(tokens_here, (tokens_here * 5 + 4 * experts_here - 1) // (4 * experts_here))
    pair_side = lax.axis_index("expert") % 2
    gate_full, up_full, down_full = (
        lax.all_gather(w_gate[0, 0], "dp", axis=1, tiled=True),
        lax.all_gather(w_up[0, 0], "dp", axis=1, tiled=True),
        lax.all_gather(w_down[0, 0], "dp", axis=0, tiled=True),
    )
    pos_fwd, select_fwd = placing(route_forward[0, :, 0], experts_here, capacity)
    pos_bwd, select_bwd = placing(route_backward[0, :, 0], experts_here, capacity)
    scaled_grad = (prob_backward[0][:, None] * grad_output[0].astype(jnp.float32)).astype(
        jnp.bfloat16
    )
    stacked = jnp.stack(
        [
            packing(select_fwd, x_forward[0]),
            packing(select_bwd, x_backward[0]),
            packing(select_bwd, scaled_grad),
        ]
    )
    stacked = stacked.reshape(3, experts_here, capacity, feature_width)
    split_rows = stacked.reshape(3, experts_here, capacity, 2, feature_width // 2).transpose(
        0, 1, 3, 2, 4
    )
    split_rows = split_rows.reshape(3, groups, capacity, feature_width // 2)
    own_half = lax.all_to_all(split_rows, "expert", split_axis=1, concat_axis=1, tiled=True)
    partner_half = from_partner(own_half, "expert", 0)
    arrived = jnp.where(
        pair_side == 0,
        jnp.concatenate([own_half, partner_half], axis=3),
        jnp.concatenate([partner_half, own_half], axis=3),
    )
    expert_rows = arrived.reshape(3, groups * capacity, feature_width)
    expert_out, grad_rows = expert_pass(
        expert_rows[0], expert_rows[1], expert_rows[2], gate_full, up_full, down_full
    )
    results = jnp.stack([expert_out, grad_rows]).reshape(2, groups, capacity, feature_width)
    quarters = results.reshape(2, groups, capacity, 2, feature_width // 2)
    keep_part = jnp.where(pair_side == 0, quarters[:, :, :, 0], quarters[:, :, :, 1])
    give_part = jnp.where(pair_side == 0, quarters[:, :, :, 1], quarters[:, :, :, 0])
    finished = keep_part + from_partner(give_part.astype(jnp.bfloat16), "expert", 0).astype(
        give_part.dtype
    )
    returned = lax.all_to_all(finished, "expert", split_axis=1, concat_axis=1, tiled=True)
    combined = returned.reshape(2, experts_here, 2, capacity, feature_width // 2).transpose(
        0, 1, 3, 2, 4
    )
    combined = combined.reshape(2, experts_here, capacity, feature_width)
    flat_out = combined.reshape(2, experts_here * capacity, feature_width)
    moved_fwd = jnp.take(flat_out[0], pos_fwd, axis=0)
    moved_bwd = jnp.take(flat_out[1], pos_bwd, axis=0)
    layer_out = (x_forward[0].astype(jnp.float32) + prob_forward[0][:, None] * moved_fwd).astype(
        jnp.bfloat16
    )
    grad_in = (grad_output[0].astype(jnp.float32) + moved_bwd).astype(jnp.bfloat16)
    sent_fwd = shifted(layer_out, "pipe", 1)
    sent_bwd = shifted(grad_in, "pipe", -1)
    return (sent_fwd[None], sent_bwd[None])


def solution(mesh):
    few = mesh.shape["expert"] == 4
    return jax.shard_map(
        few_experts if few else many_experts,
        mesh=mesh,
        in_specs=(
            P("pipe", ("expert", "dp"), None),
            P("pipe", ("expert", "dp"), None),
            P("pipe", ("expert", "dp")),
            P("pipe", ("expert", "dp"), None),
            P("pipe", ("expert", "dp"), None),
            P("pipe", ("expert", "dp")),
            P("pipe", ("expert", "dp"), None),
            P("pipe", "expert", None, "dp"),
            P("pipe", "expert", None, "dp"),
            P("pipe", "expert", "dp", None),
        ),
        out_specs=(P("pipe", ("expert", "dp"), None), P("pipe", ("expert", "dp"), None)),
        check_vma=False,
    )
```

```python
import functools
import math

import jax
import jax.numpy as jnp
from jax import lax
from jax.experimental import pallas as pl
from jax.experimental.pallas import tpu as pltpu
from jax.sharding import PartitionSpec as P

BF16, F32 = jnp.bfloat16, jnp.float32
VMEM_LIMIT = 56 * 1024 * 1024
ROW_PARTS = 2
TAG_COLUMNS = 128


def contract_last(left_side, weights):
    return lax.dot_general(
        left_side, weights, (((1,), (1,)), ((), ())), preferred_element_type=F32
    )


def flipped(block, axis, stride):
    route = [(i, i ^ stride) for i in range(lax.axis_size(axis))]
    return lax.ppermute(block, axis, route)


def shifted(block, axis, distance):
    count = lax.axis_size(axis)
    return lax.ppermute(block, axis, [((i - distance) % count, i) for i in range(count)])


def chunk_of(width, most):
    best = 128
    for size in range(128, most + 1, 128):
        if width % size == 0:
            best = size
    return best


def gathered_rows(refs):
    return jnp.concatenate([ref[0] for ref in refs], axis=0)


def chained_rows(refs):
    others = len(refs) // 2
    own, below, above = refs[0][...], refs[1 : 1 + others], refs[1 + others :]
    return jnp.concatenate(
        [own] + [above[away][...] + below[others - 1 - away][...] for away in range(others)],
        axis=0,
    )


def gathered_input(x, begin, rows):
    count, unit = x.shape[0], math.gcd(begin, rows)
    arrays, specs = [], []
    for turn in range(count):
        for piece in range(begin // unit, (begin + rows) // unit):
            arrays.append(x)
            specs.append(
                lambda chunk, column, turn=turn, piece=piece: pl.BlockSpec(
                    (1, unit, chunk),
                    lambda i, at: (lax.rem(at[0] + turn, count), piece, column(i)),
                )
            )
    return gathered_rows, arrays, specs


def chained_input(hops, begin, rows):
    (own, _), *others = hops
    from_below, from_above = zip(*others)
    spec = lambda chunk, column: pl.BlockSpec(
        (rows, chunk), lambda i, at: (begin // rows, column(i))
    )
    arrays = [own, *from_below, *from_above]
    return chained_rows, arrays, [spec] * len(arrays)


def weight_copies(chunk, steps, gate_ups, downs, gate_up_held, down_held, sems):
    by_chunk = []
    for step in range(steps):
        part = pl.ds(step * chunk, chunk)
        by_chunk.append(
            (
                [
                    pltpu.make_async_copy(
                        ref.at[:, part, :], gate_up_held.at[i, :, part, :], sems.at[0, step, i]
                    )
                    for i, ref in enumerate(gate_ups)
                ],
                [
                    pltpu.make_async_copy(
                        ref.at[:, part], down_held.at[i, :, part], sems.at[1, step, i]
                    )
                    for i, ref in enumerate(downs)
                ],
            )
        )
    return by_chunk


def own_hidden(at_ref, tags, column, hidden):
    mine = tags[:, column : column + 1].astype(jnp.int32) == at_ref[1]
    unit = lax.broadcasted_iota(jnp.int32, (tags.shape[0], hidden), 1)
    return mine == (unit < hidden // 2)


def joined(refs, axis, index=None):
    pick = (lambda ref: ref[...]) if index is None else (lambda ref: ref[index])
    return jnp.concatenate([pick(ref) for ref in refs], axis=axis)


def put_blocks(outs, total):
    rows = outs[0].shape[0]
    for index, ref in enumerate(outs):
        ref[...] = total[index * rows : (index + 1) * rows].astype(ref.dtype)


def compiler_params():
    return pltpu.CompilerParams(vmem_limit_bytes=VMEM_LIMIT)


def small_cost(many, hidden):
    return pl.CostEstimate(flops=many * hidden, bytes_accessed=many, transcendentals=0)


def home_shapes(count, rows, width, parts=1):
    own, others = (jax.ShapeDtypeStruct((rows // parts, width), kind) for kind in (F32, BF16))
    return [own] * parts + [others] * (parts * (count - 1))


def hidden_kernel(count, pieces, steps, at_ref, *refs):
    tags, rows_in, gate_ups = refs[:count], refs[count : 2 * count], refs[2 * count : -3]
    out_ref, gate_ref, up_ref = refs[-3:]
    step = pl.program_id(0)

    @pl.when(step == 0)
    def _():
        gate_ref[...] = jnp.zeros_like(gate_ref)
        up_ref[...] = jnp.zeros_like(up_ref)

    x = gathered_rows(rows_in)
    gate_ref[...] += jnp.dot(x, joined(gate_ups, 1, 0), preferred_element_type=F32)
    up_ref[...] += jnp.dot(x, joined(gate_ups, 1, 1), preferred_element_type=F32)

    @pl.when(step == steps - 1)
    def _():
        gate, up = gate_ref[...], up_ref[...]
        keep = own_hidden(at_ref, gathered_rows(tags), 0, gate.shape[1])
        out_ref[...] = jnp.where(keep, gate * jax.nn.sigmoid(gate) * up, 0.0).astype(BF16)


def hidden_call(at, x_gathered, rows, width, gate_ups):
    count, pieces, hid = x_gathered.shape[0], len(gate_ups), gate_ups[0].shape[2]
    chunk = chunk_of(width, 1792)
    steps, hidden, many = width // chunk, pieces * hid, count * rows
    _, arrays, specs = gathered_input(x_gathered, 0, rows)
    return pl.pallas_call(
        functools.partial(hidden_kernel, count, pieces, steps),
        grid_spec=pltpu.PrefetchScalarGridSpec(
            num_scalar_prefetch=1,
            grid=(steps,),
            in_specs=[spec(TAG_COLUMNS, lambda i: width // TAG_COLUMNS) for spec in specs]
            + [spec(chunk, lambda i: i) for spec in specs]
            + [pl.BlockSpec((2, chunk, hid), lambda i, at: (0, i, 0))] * pieces,
            out_specs=pl.BlockSpec((many, hidden), lambda i, at: (0, 0)),
            scratch_shapes=[pltpu.VMEM((many, hidden), F32)] * 2,
        ),
        out_shape=jax.ShapeDtypeStruct((many, hidden), BF16),
        compiler_params=compiler_params(),
        cost_estimate=small_cost(many, hidden),
    )(at, *arrays, *arrays, *gate_ups)


def down_kernel(pieces, hidden_ref, *refs):
    downs, outs = refs[:pieces], refs[pieces:]
    total = jnp.dot(hidden_ref[...], joined(downs, 0), preferred_element_type=F32)
    put_blocks(outs, total)


def down_call(hidden_rows, count, downs):
    many, hidden = hidden_rows.shape
    pieces, (hid, width), rows = len(downs), downs[0].shape, many // count
    chunk = chunk_of(width, 1792)
    return pl.pallas_call(
        functools.partial(down_kernel, pieces),
        grid=(width // chunk,),
        in_specs=[pl.BlockSpec((many, hidden), lambda i: (0, 0))]
        + [pl.BlockSpec((hid, chunk), lambda i: (0, i))] * pieces,
        out_specs=[pl.BlockSpec((rows, chunk), lambda i: (0, i))] * count,
        out_shape=home_shapes(count, rows, width),
        compiler_params=compiler_params(),
        cost_estimate=small_cost(many, hidden),
    )(hidden_rows, *downs)


def backward_kernel(inputs, count, pieces, chunk, steps, at_ref, *refs):
    tags, refs = refs[:count], refs[count:]
    rows_in, scaled_in, refs = refs[:inputs], refs[inputs : 2 * inputs], refs[2 * inputs :]
    gate_ups, downs, outs = refs[:pieces], refs[pieces : 2 * pieces], refs[2 * pieces : -8]
    gate_ref, up_ref, grad_ref, grad_gate_ref, grad_up_ref = refs[-8:-3]
    gate_up_held, down_held, sems = refs[-3:]
    step = pl.program_id(0)
    copies = weight_copies(chunk, steps, gate_ups, downs, gate_up_held, down_held, sems)

    @pl.when(step == 0)
    def _():
        for of_gate_up, of_down in copies:
            for copy in of_gate_up + of_down:
                copy.start()
        for total in (gate_ref, up_ref, grad_ref):
            total[...] = jnp.zeros_like(total)

    for number, (of_gate_up, of_down) in enumerate(copies):

        @pl.when(step == number)
        def _(waited=of_gate_up + of_down):
            for copy in waited:
                copy.wait()

    at_chunk = pl.ds(pl.multiple_of(lax.rem(step, steps) * chunk, chunk), chunk)

    def gate_or_up(which):
        return jnp.concatenate(
            [gate_up_held[i, which, at_chunk, :] for i in range(pieces)], axis=1
        )

    @pl.when(step < steps)
    def _():
        x = chained_rows(rows_in)
        gate_ref[...] += jnp.dot(x, gate_or_up(0), preferred_element_type=F32)
        up_ref[...] += jnp.dot(x, gate_or_up(1), preferred_element_type=F32)
        down = jnp.concatenate([down_held[i, :, at_chunk] for i in range(pieces)], axis=0)
        grad_ref[...] += contract_last(chained_rows(scaled_in), down)

    @pl.when(step == steps - 1)
    def _():
        gate, up, grad = gate_ref[...], up_ref[...], grad_ref[...]
        keep = own_hidden(at_ref, gathered_rows(tags), TAG_COLUMNS // 2, gate.shape[1])
        s = jax.nn.sigmoid(gate)
        silu = gate * s
        grad_gate = grad * up * (s + silu * (1.0 - s))
        grad_gate_ref[...] = jnp.where(keep, grad_gate, 0.0).astype(BF16)
        grad_up_ref[...] = jnp.where(keep, grad * silu, 0.0).astype(BF16)

    @pl.when(step >= steps)
    def _():
        total = contract_last(grad_gate_ref[...], gate_or_up(0))
        total += contract_last(grad_up_ref[...], gate_or_up(1))
        put_blocks(outs, total)


def backward_call(at, x_gathered, rows, parts, hops_x, hops_scaled, gate_ups, downs):
    count, width = x_gathered.shape[0], hops_x[0][0].shape[1]
    pieces, hid = len(downs), downs[0].shape[0]
    chunk = chunk_of(width, 1792)
    steps, hidden, many = width // chunk, pieces * hid, count * rows
    first = lambda i: jnp.minimum(i, steps - 1)
    second = lambda i: jnp.maximum(i - steps, 0)
    _, tags, tag_specs = gathered_input(x_gathered, 0, rows)
    _, rows_in, row_specs = chained_input(hops_x, 0, rows)
    _, scaled_in, scaled_specs = chained_input(hops_scaled, 0, rows)
    return pl.pallas_call(
        functools.partial(backward_kernel, len(rows_in), count, pieces, chunk, steps),
        grid_spec=pltpu.PrefetchScalarGridSpec(
            num_scalar_prefetch=1,
            grid=(2 * steps,),
            in_specs=[spec(TAG_COLUMNS, lambda i: width // TAG_COLUMNS) for spec in tag_specs]
            + [spec(chunk, first) for spec in row_specs + scaled_specs]
            + [pl.BlockSpec(memory_space=pl.ANY)] * (2 * pieces),
            out_specs=[pl.BlockSpec((rows // parts, chunk), lambda i, at: (0, second(i)))]
            * (parts * count),
            scratch_shapes=[pltpu.VMEM((many, hidden), F32)] * 3
            + [pltpu.VMEM((many, hidden), BF16)] * 2
            + [
                pltpu.VMEM((pieces, 2, width, hid), BF16),
                pltpu.VMEM((pieces, hid, width), BF16),
                pltpu.SemaphoreType.DMA((2, steps, pieces)),
            ],
        ),
        out_shape=home_shapes(count, rows, width, parts),
        compiler_params=compiler_params(),
        cost_estimate=small_cost(many, hidden),
    )(at, *tags, *rows_in, *scaled_in, *gate_ups, *downs)


def after(value, *earlier):
    return lax.optimization_barrier((value, earlier))[0]


def hop(below, above, axis, step):
    count = lax.axis_size(axis)
    up = [(i, i + 1) for i in range(step - 1, count - 1)]
    down = [(i, i - 1) for i in range(1, count - step + 1)]
    return lax.ppermute(below, axis, up), lax.ppermute(above, axis, down)


def summands(blocks, step, arrived):
    pair = (blocks[len(blocks) - step], blocks[step])
    if arrived is None:
        return pair
    return tuple(
        (own.astype(F32) + other.astype(F32)).astype(BF16) for own, other in zip(pair, arrived)
    )


def step_home(pair, axis, step):
    count = lax.axis_size(axis)
    up = lax.ppermute(pair[0], axis, [(i, i + 1) for i in range(step)])
    down = lax.ppermute(pair[1], axis, [(i, i - 1) for i in range(count - step, count)])
    return up, down


def summed(block, arrived):
    for part in arrived:
        block = block + part.astype(F32)
    return block


def few_experts(
    x_forward,
    route_forward,
    prob_forward,
    x_backward,
    route_backward,
    prob_backward,
    grad_output,
    w_gate,
    w_up,
    w_down,
):
    tokens_here, width = x_forward.shape[1:]
    expert_here = lax.axis_index("expert") // 2
    count = lax.axis_size("dp")
    at = jnp.stack([lax.axis_index("dp"), expert_here]).astype(jnp.int32)
    half_tag = (tokens_here, TAG_COLUMNS // 2)
    tagged = jnp.concatenate(
        [x_forward[0]]
        + [jnp.broadcast_to(r[0].astype(BF16), half_tag) for r in (route_forward, route_backward)],
        axis=1,
    )
    scaled_grad = (prob_backward[0][:, None] * grad_output[0].astype(F32)).astype(BF16)
    gate_up, down = jnp.concatenate([w_gate[0], w_up[0]], axis=0), w_down[0, 0]

    x_gathered = lax.all_gather(tagged, "dp")
    across_down = flipped(down, "expert", 2)
    first_scaled = after(scaled_grad, across_down)
    hops_scaled = [(first_scaled, first_scaled)]
    own_flip = flipped(gate_up, "expert", 1)
    across_gate_up = flipped(after(gate_up, across_down, own_flip), "expert", 2)
    hops_x = [(x_backward[0], x_backward[0])]
    for hops in (hops_x, hops_scaled):
        for step in range(1, count):
            hops.append(hop(*hops[-1], "dp", step))
    gate_ups = [gate_up, own_flip, across_gate_up]
    downs = [down, flipped(down, "expert", 1), across_down, flipped(across_down, "expert", 1)]
    gate_ups.append(flipped(after(across_gate_up, x_gathered, hops_x[2], hops_scaled[1]), "expert", 1))
    hidden_fwd = hidden_call(at, x_gathered, tokens_here, width, gate_ups)
    partial_fwd = down_call(hidden_fwd, count, downs)

    arrived_fwd = step_home(summands(partial_fwd, 1, None), "dp", 1)
    arrived_fwd = after(arrived_fwd, hops_x[3], hops_scaled[2])
    arrived_fwd = step_home(summands(partial_fwd, 2, arrived_fwd), "dp", 2)
    sends_fwd = summands(partial_fwd, 3, arrived_fwd)
    arrived_fwd = step_home(sends_fwd, "dp", 3)
    hops_scaled[0] = (after(scaled_grad, sends_fwd),) * 2
    partial_bwd = backward_call(
        at, x_gathered, tokens_here, ROW_PARTS, hops_x, hops_scaled, gate_ups, downs
    )

    arrived_fwd = after(arrived_fwd, partial_bwd[-1])
    total_fwd = summed(partial_fwd[0], arrived_fwd)
    layer_out = (x_forward[0].astype(F32) + prob_forward[0][:, None] * total_fwd).astype(BF16)
    sent_fwd = shifted(layer_out, "pipe", 1)
    size = tokens_here // ROW_PARTS
    partial_bwd = after(tuple(partial_bwd), arrived_fwd)
    blocks = [partial_bwd[part::ROW_PARTS] for part in range(ROW_PARTS)]
    arrived = [None] * ROW_PARTS
    for step in range(1, count):
        for part in range(ROW_PARTS):
            if step == 3 and part == 0:
                arrived[0] = after(arrived[0], sent_fwd)
            arrived[part] = step_home(summands(blocks[part], step, arrived[part]), "dp", step)
    sent_bwd = []
    for part in range(ROW_PARTS):
        rows = slice(part * size, (part + 1) * size)
        total = summed(blocks[part][0], after(arrived[part], sent_bwd))
        grad_in = (grad_output[0, rows].astype(F32) + total).astype(BF16)
        sent_bwd.append(shifted(grad_in, "pipe", -1))
    return (sent_fwd[None], jnp.concatenate(sent_bwd, axis=0)[None])


def from_partner(block, axis, stride):
    count = lax.axis_size(axis)
    route = []
    for low in range(count):
        high = low | 1 << stride
        if high != low and high < count:
            route += [(low, high), (high, low)]
    return lax.ppermute(block, axis, route)


def silu_parts(pre_gate):
    sigma_gate = jax.nn.sigmoid(pre_gate)
    return (pre_gate * sigma_gate, sigma_gate)


def expert_pass(forward_rows, backward_rows, scaled_rows, gate_weight, up_weight, down_weight):
    gate_fwd = jnp.dot(forward_rows, gate_weight, preferred_element_type=jnp.float32)
    up_fwd = jnp.dot(forward_rows, up_weight, preferred_element_type=jnp.float32)
    silu_fwd, sigma_fwd = silu_parts(gate_fwd)
    hidden_fwd = (silu_fwd * up_fwd).astype(jnp.bfloat16)
    expert_out = jnp.dot(hidden_fwd, down_weight, preferred_element_type=jnp.float32)
    gate_bwd = jnp.dot(backward_rows, gate_weight, preferred_element_type=jnp.float32)
    up_bwd = jnp.dot(backward_rows, up_weight, preferred_element_type=jnp.float32)
    silu_bwd, sigma_bwd = silu_parts(gate_bwd)
    grad_hidden = contract_last(scaled_rows, down_weight)
    grad_gate = (grad_hidden * up_bwd * (sigma_bwd + silu_bwd * (1.0 - sigma_bwd))).astype(
        jnp.bfloat16
    )
    grad_up = (grad_hidden * silu_bwd).astype(jnp.bfloat16)
    grad_rows = contract_last(grad_gate, gate_weight) + contract_last(grad_up, up_weight)
    return (expert_out, grad_rows)


def placing(routes, experts_here, capacity):
    route_hits = (routes[:, None] == jnp.arange(experts_here, dtype=jnp.int32)[None, :]).astype(
        jnp.int32
    )
    before = jnp.cumsum(route_hits, axis=0) - route_hits
    slot_index = jnp.sum(before * route_hits, axis=1)
    position = routes * capacity + slot_index
    selector = (
        position[None, :] == jnp.arange(experts_here * capacity, dtype=jnp.int32)[:, None]
    ).astype(jnp.bfloat16)
    return (position, selector)


def packing(selector, values):
    return jnp.dot(selector, values, preferred_element_type=jnp.float32).astype(jnp.bfloat16)


def many_experts(
    x_forward,
    route_forward,
    prob_forward,
    x_backward,
    route_backward,
    prob_backward,
    grad_output,
    w_gate,
    w_up,
    w_down,
):
    tokens_here = x_forward.shape[1]
    feature_width = x_forward.shape[2]
    groups = lax.axis_size("expert")
    experts_here = groups // 2
    capacity = min(tokens_here, (tokens_here * 5 + 4 * experts_here - 1) // (4 * experts_here))
    pair_side = lax.axis_index("expert") % 2
    gate_full, up_full, down_full = (
        lax.all_gather(w_gate[0, 0], "dp", axis=1, tiled=True),
        lax.all_gather(w_up[0, 0], "dp", axis=1, tiled=True),
        lax.all_gather(w_down[0, 0], "dp", axis=0, tiled=True),
    )
    pos_fwd, select_fwd = placing(route_forward[0, :, 0], experts_here, capacity)
    pos_bwd, select_bwd = placing(route_backward[0, :, 0], experts_here, capacity)
    scaled_grad = (prob_backward[0][:, None] * grad_output[0].astype(jnp.float32)).astype(
        jnp.bfloat16
    )
    stacked = jnp.stack(
        [
            packing(select_fwd, x_forward[0]),
            packing(select_bwd, x_backward[0]),
            packing(select_bwd, scaled_grad),
        ]
    )
    stacked = stacked.reshape(3, experts_here, capacity, feature_width)
    split_rows = stacked.reshape(3, experts_here, capacity, 2, feature_width // 2).transpose(
        0, 1, 3, 2, 4
    )
    split_rows = split_rows.reshape(3, groups, capacity, feature_width // 2)
    own_half = lax.all_to_all(split_rows, "expert", split_axis=1, concat_axis=1, tiled=True)
    partner_half = from_partner(own_half, "expert", 0)
    arrived = jnp.where(
        pair_side == 0,
        jnp.concatenate([own_half, partner_half], axis=3),
        jnp.concatenate([partner_half, own_half], axis=3),
    )
    expert_rows = arrived.reshape(3, groups * capacity, feature_width)
    expert_out, grad_rows = expert_pass(
        expert_rows[0], expert_rows[1], expert_rows[2], gate_full, up_full, down_full
    )
    results = jnp.stack([expert_out, grad_rows]).reshape(2, groups, capacity, feature_width)
    quarters = results.reshape(2, groups, capacity, 2, feature_width // 2)
    keep_part = jnp.where(pair_side == 0, quarters[:, :, :, 0], quarters[:, :, :, 1])
    give_part = jnp.where(pair_side == 0, quarters[:, :, :, 1], quarters[:, :, :, 0])
    finished = keep_part + from_partner(give_part.astype(jnp.bfloat16), "expert", 0).astype(
        give_part.dtype
    )
    returned = lax.all_to_all(finished, "expert", split_axis=1, concat_axis=1, tiled=True)
    combined = returned.reshape(2, experts_here, 2, capacity, feature_width // 2).transpose(
        0, 1, 3, 2, 4
    )
    combined = combined.reshape(2, experts_here, capacity, feature_width)
    flat_out = combined.reshape(2, experts_here * capacity, feature_width)
    moved_fwd = jnp.take(flat_out[0], pos_fwd, axis=0)
    moved_bwd = jnp.take(flat_out[1], pos_bwd, axis=0)
    layer_out = (x_forward[0].astype(jnp.float32) + prob_forward[0][:, None] * moved_fwd).astype(
        jnp.bfloat16
    )
    grad_in = (grad_output[0].astype(jnp.float32) + moved_bwd).astype(jnp.bfloat16)
    sent_fwd = shifted(layer_out, "pipe", 1)
    sent_bwd = shifted(grad_in, "pipe", -1)
    return (sent_fwd[None], sent_bwd[None])


def solution(mesh):
    few = mesh.shape["expert"] == 4
    return jax.shard_map(
        few_experts if few else many_experts,
        mesh=mesh,
        in_specs=(
            P("pipe", ("expert", "dp"), None),
            P("pipe", ("expert", "dp"), None),
            P("pipe", ("expert", "dp")),
            P("pipe", ("expert", "dp"), None),
            P("pipe", ("expert", "dp"), None),
            P("pipe", ("expert", "dp")),
            P("pipe", ("expert", "dp"), None),
            P("pipe", "expert", None, "dp"),
            P("pipe", "expert", None, "dp"),
            P("pipe", "expert", "dp", None),
        ),
        out_specs=(P("pipe", ("expert", "dp"), None), P("pipe", ("expert", "dp"), None)),
        check_vma=False,
    )
```

```python
import functools
import math

import jax
import jax.numpy as jnp
from jax import lax
from jax.experimental import pallas as pl
from jax.experimental.pallas import tpu as pltpu
from jax.sharding import PartitionSpec as P

BF16, F32 = jnp.bfloat16, jnp.float32
VMEM_LIMIT = 56 * 1024 * 1024
ROW_PARTS = 2
TAG_COLUMNS = 128


def contract_last(left_side, weights):
    return lax.dot_general(
        left_side, weights, (((1,), (1,)), ((), ())), preferred_element_type=F32
    )


def flipped(block, axis, stride):
    route = [(i, i ^ stride) for i in range(lax.axis_size(axis))]
    return lax.ppermute(block, axis, route)


def shifted(block, axis, distance):
    count = lax.axis_size(axis)
    return lax.ppermute(block, axis, [((i - distance) % count, i) for i in range(count)])


def chunk_of(width, most):
    best = 128
    for size in range(128, most + 1, 128):
        if width % size == 0:
            best = size
    return best


def gathered_rows(refs):
    return jnp.concatenate([ref[0] for ref in refs], axis=0)


def chained_rows(refs):
    others = len(refs) // 2
    own, below, above = refs[0][...], refs[1 : 1 + others], refs[1 + others :]
    return jnp.concatenate(
        [own] + [above[away][...] + below[others - 1 - away][...] for away in range(others)],
        axis=0,
    )


def gathered_input(x, begin, rows):
    count, unit = x.shape[0], math.gcd(begin, rows)
    arrays, specs = [], []
    for turn in range(count):
        for piece in range(begin // unit, (begin + rows) // unit):
            arrays.append(x)
            specs.append(
                lambda chunk, column, turn=turn, piece=piece: pl.BlockSpec(
                    (1, unit, chunk),
                    lambda i, at: (lax.rem(at[0] + turn, count), piece, column(i)),
                )
            )
    return gathered_rows, arrays, specs


def chained_input(hops, begin, rows):
    (own, _), *others = hops
    from_below, from_above = zip(*others)
    spec = lambda chunk, column: pl.BlockSpec(
        (rows, chunk), lambda i, at: (begin // rows, column(i))
    )
    arrays = [own, *from_below, *from_above]
    return chained_rows, arrays, [spec] * len(arrays)


def weight_copies(chunk, steps, gate_ups, downs, gate_up_held, down_held, sems):
    by_chunk = []
    for step in range(steps):
        part = pl.ds(step * chunk, chunk)
        by_chunk.append(
            (
                [
                    pltpu.make_async_copy(
                        ref.at[:, part, :], gate_up_held.at[i, :, part, :], sems.at[0, step, i]
                    )
                    for i, ref in enumerate(gate_ups)
                ],
                [
                    pltpu.make_async_copy(
                        ref.at[:, part], down_held.at[i, :, part], sems.at[1, step, i]
                    )
                    for i, ref in enumerate(downs)
                ],
            )
        )
    return by_chunk


def own_hidden(at_ref, tags, column, hidden):
    mine = tags[:, column : column + 1].astype(jnp.int32) == at_ref[1]
    unit = lax.broadcasted_iota(jnp.int32, (tags.shape[0], hidden), 1)
    return mine == (unit < hidden // 2)


def joined(refs, axis, index=None):
    pick = (lambda ref: ref[...]) if index is None else (lambda ref: ref[index])
    return jnp.concatenate([pick(ref) for ref in refs], axis=axis)


def put_blocks(outs, total):
    rows = outs[0].shape[0]
    for index, ref in enumerate(outs):
        ref[...] = total[index * rows : (index + 1) * rows].astype(ref.dtype)


def compiler_params():
    return pltpu.CompilerParams(vmem_limit_bytes=VMEM_LIMIT)


def small_cost(many, hidden):
    return pl.CostEstimate(flops=many * hidden, bytes_accessed=many, transcendentals=0)


def home_shapes(count, rows, width, parts=1):
    own, others = (jax.ShapeDtypeStruct((rows // parts, width), kind) for kind in (F32, BF16))
    return [own] * parts + [others] * (parts * (count - 1))


def hidden_kernel(count, pieces, steps, at_ref, *refs):
    tags, rows_in, gate_ups = refs[:count], refs[count : 2 * count], refs[2 * count : -3]
    out_ref, gate_ref, up_ref = refs[-3:]
    step = pl.program_id(0)

    @pl.when(step == 0)
    def _():
        gate_ref[...] = jnp.zeros_like(gate_ref)
        up_ref[...] = jnp.zeros_like(up_ref)

    x = gathered_rows(rows_in)
    gate_ref[...] += jnp.dot(x, joined(gate_ups, 1, 0), preferred_element_type=F32)
    up_ref[...] += jnp.dot(x, joined(gate_ups, 1, 1), preferred_element_type=F32)

    @pl.when(step == steps - 1)
    def _():
        gate, up = gate_ref[...], up_ref[...]
        keep = own_hidden(at_ref, gathered_rows(tags), 0, gate.shape[1])
        out_ref[...] = jnp.where(keep, gate * jax.nn.sigmoid(gate) * up, 0.0).astype(BF16)


def hidden_call(at, x_gathered, rows, width, gate_ups):
    count, pieces, hid = x_gathered.shape[0], len(gate_ups), gate_ups[0].shape[2]
    chunk = chunk_of(width, 1792)
    steps, hidden, many = width // chunk, pieces * hid, count * rows
    _, arrays, specs = gathered_input(x_gathered, 0, rows)
    return pl.pallas_call(
        functools.partial(hidden_kernel, count, pieces, steps),
        grid_spec=pltpu.PrefetchScalarGridSpec(
            num_scalar_prefetch=1,
            grid=(steps,),
            in_specs=[spec(TAG_COLUMNS, lambda i: width // TAG_COLUMNS) for spec in specs]
            + [spec(chunk, lambda i: i) for spec in specs]
            + [pl.BlockSpec((2, chunk, hid), lambda i, at: (0, i, 0))] * pieces,
            out_specs=pl.BlockSpec((many, hidden), lambda i, at: (0, 0)),
            scratch_shapes=[pltpu.VMEM((many, hidden), F32)] * 2,
        ),
        out_shape=jax.ShapeDtypeStruct((many, hidden), BF16),
        compiler_params=compiler_params(),
        cost_estimate=small_cost(many, hidden),
    )(at, *arrays, *arrays, *gate_ups)


def down_kernel(pieces, hidden_ref, *refs):
    downs, outs = refs[:pieces], refs[pieces:]
    total = jnp.dot(hidden_ref[...], joined(downs, 0), preferred_element_type=F32)
    put_blocks(outs, total)


def down_call(hidden_rows, count, downs):
    many, hidden = hidden_rows.shape
    pieces, (hid, width), rows = len(downs), downs[0].shape, many // count
    chunk = chunk_of(width, 1792)
    return pl.pallas_call(
        functools.partial(down_kernel, pieces),
        grid=(width // chunk,),
        in_specs=[pl.BlockSpec((many, hidden), lambda i: (0, 0))]
        + [pl.BlockSpec((hid, chunk), lambda i: (0, i))] * pieces,
        out_specs=[pl.BlockSpec((rows, chunk), lambda i: (0, i))] * count,
        out_shape=home_shapes(count, rows, width),
        compiler_params=compiler_params(),
        cost_estimate=small_cost(many, hidden),
    )(hidden_rows, *downs)


def backward_kernel(inputs, count, pieces, chunk, steps, at_ref, *refs):
    tags, refs = refs[:count], refs[count:]
    rows_in, scaled_in, refs = refs[:inputs], refs[inputs : 2 * inputs], refs[2 * inputs :]
    gate_ups, downs, outs = refs[:pieces], refs[pieces : 2 * pieces], refs[2 * pieces : -8]
    gate_ref, up_ref, grad_ref, grad_gate_ref, grad_up_ref = refs[-8:-3]
    gate_up_held, down_held, sems = refs[-3:]
    step = pl.program_id(0)
    copies = weight_copies(chunk, steps, gate_ups, downs, gate_up_held, down_held, sems)

    @pl.when(step == 0)
    def _():
        for of_gate_up, of_down in copies:
            for copy in of_gate_up + of_down:
                copy.start()
        for total in (gate_ref, up_ref, grad_ref):
            total[...] = jnp.zeros_like(total)

    for number, (of_gate_up, of_down) in enumerate(copies):

        @pl.when(step == number)
        def _(waited=of_gate_up + of_down):
            for copy in waited:
                copy.wait()

    at_chunk = pl.ds(pl.multiple_of(lax.rem(step, steps) * chunk, chunk), chunk)

    def gate_or_up(which):
        return jnp.concatenate(
            [gate_up_held[i, which, at_chunk, :] for i in range(pieces)], axis=1
        )

    @pl.when(step < steps)
    def _():
        x = chained_rows(rows_in)
        gate_ref[...] += jnp.dot(x, gate_or_up(0), preferred_element_type=F32)
        up_ref[...] += jnp.dot(x, gate_or_up(1), preferred_element_type=F32)
        down = jnp.concatenate([down_held[i, :, at_chunk] for i in range(pieces)], axis=0)
        grad_ref[...] += contract_last(down, chained_rows(scaled_in))

    @pl.when(step == steps - 1)
    def _():
        gate, up, grad = gate_ref[...], up_ref[...], grad_ref[...].T
        keep = own_hidden(at_ref, gathered_rows(tags), TAG_COLUMNS // 2, gate.shape[1])
        s = jax.nn.sigmoid(gate)
        silu = gate * s
        grad_gate = grad * up * (s + silu * (1.0 - s))
        grad_gate_ref[...] = jnp.where(keep, grad_gate, 0.0).astype(BF16)
        grad_up_ref[...] = jnp.where(keep, grad * silu, 0.0).astype(BF16)

    @pl.when(step >= steps)
    def _():
        total = contract_last(gate_or_up(0), grad_gate_ref[...])
        total += contract_last(gate_or_up(1), grad_up_ref[...])
        put_blocks(outs, total.T)


def backward_call(at, x_gathered, rows, parts, hops, gate_ups, downs):
    count, width = x_gathered.shape[0], hops[0][0].shape[1]
    pieces, hid = len(downs), downs[0].shape[0]
    chunk = chunk_of(width, 1792)
    steps, hidden, many = width // chunk, pieces * hid, count * rows
    first = lambda i: jnp.minimum(i, steps - 1)
    second = lambda i: jnp.maximum(i - steps, 0)
    _, tags, tag_specs = gathered_input(x_gathered, 0, rows)
    _, rows_in, row_specs = chained_input(hops, 0, rows)
    _, _, scaled_specs = chained_input(hops, rows, rows)
    return pl.pallas_call(
        functools.partial(backward_kernel, len(rows_in), count, pieces, chunk, steps),
        grid_spec=pltpu.PrefetchScalarGridSpec(
            num_scalar_prefetch=1,
            grid=(2 * steps,),
            in_specs=[spec(TAG_COLUMNS, lambda i: width // TAG_COLUMNS) for spec in tag_specs]
            + [spec(chunk, first) for spec in row_specs + scaled_specs]
            + [pl.BlockSpec(memory_space=pl.ANY)] * (2 * pieces),
            out_specs=[pl.BlockSpec((rows // parts, chunk), lambda i, at: (0, second(i)))]
            * (parts * count),
            scratch_shapes=[pltpu.VMEM((many, hidden), F32)] * 2
            + [pltpu.VMEM((hidden, many), F32)]
            + [pltpu.VMEM((many, hidden), BF16)] * 2
            + [
                pltpu.VMEM((pieces, 2, width, hid), BF16),
                pltpu.VMEM((pieces, hid, width), BF16),
                pltpu.SemaphoreType.DMA((2, steps, pieces)),
            ],
        ),
        out_shape=home_shapes(count, rows, width, parts),
        compiler_params=compiler_params(),
        cost_estimate=small_cost(many, hidden),
    )(at, *tags, *rows_in, *rows_in, *gate_ups, *downs)


def after(value, *earlier):
    return lax.optimization_barrier((value, earlier))[0]


def hop(below, above, axis, step):
    count = lax.axis_size(axis)
    up = [(i, i + 1) for i in range(step - 1, count - 1)]
    down = [(i, i - 1) for i in range(1, count - step + 1)]
    return lax.ppermute(below, axis, up), lax.ppermute(above, axis, down)


def summands(blocks, step, arrived):
    pair = (blocks[len(blocks) - step], blocks[step])
    if arrived is None:
        return pair
    return tuple(
        (own.astype(F32) + other.astype(F32)).astype(BF16) for own, other in zip(pair, arrived)
    )


def step_home(pair, axis, step):
    count = lax.axis_size(axis)
    up = lax.ppermute(pair[0], axis, [(i, i + 1) for i in range(step)])
    down = lax.ppermute(pair[1], axis, [(i, i - 1) for i in range(count - step, count)])
    return up, down


def summed(block, arrived):
    for part in arrived:
        block = block + part.astype(F32)
    return block


def few_experts(
    x_forward,
    route_forward,
    prob_forward,
    x_backward,
    route_backward,
    prob_backward,
    grad_output,
    w_gate,
    w_up,
    w_down,
):
    tokens_here, width = x_forward.shape[1:]
    expert_here = lax.axis_index("expert") // 2
    count = lax.axis_size("dp")
    at = jnp.stack([lax.axis_index("dp"), expert_here]).astype(jnp.int32)
    half_tag = (tokens_here, TAG_COLUMNS // 2)
    tagged = jnp.concatenate(
        [x_forward[0]]
        + [jnp.broadcast_to(r[0].astype(BF16), half_tag) for r in (route_forward, route_backward)],
        axis=1,
    )
    scaled_grad = (prob_backward[0][:, None] * grad_output[0].astype(F32)).astype(BF16)
    back_rows = jnp.concatenate([x_backward[0], scaled_grad], axis=0)
    gate_up, down = jnp.concatenate([w_gate[0], w_up[0]], axis=0), w_down[0, 0]

    x_gathered = lax.all_gather(tagged, "dp")
    across_down = flipped(down, "expert", 2)
    gate_up, back_rows = after((gate_up, back_rows), across_down)
    across_gate_up = flipped(gate_up, "expert", 2)
    hops = [(back_rows, back_rows)]
    for step in range(1, count):
        hops.append(hop(*hops[-1], "dp", step))
    gate_ups = [gate_up, flipped(after(gate_up, hops[1]), "expert", 1), across_gate_up]
    downs = [down, flipped(down, "expert", 1), across_down, flipped(across_down, "expert", 1)]
    gate_ups.append(flipped(after(across_gate_up, x_gathered, hops[1], downs[1:]), "expert", 1))
    hidden_fwd = hidden_call(at, x_gathered, tokens_here, width, gate_ups)
    partial_fwd = down_call(hidden_fwd, count, downs)

    arrived_fwd = step_home(summands(partial_fwd, 1, None), "dp", 1)
    arrived_fwd = after(arrived_fwd, hops[2])
    arrived_fwd = step_home(summands(partial_fwd, 2, arrived_fwd), "dp", 2)
    sends_fwd = summands(partial_fwd, 3, arrived_fwd)
    arrived_fwd = step_home(sends_fwd, "dp", 3)
    hops[0] = after(hops[0], sends_fwd)
    partial_bwd = backward_call(at, x_gathered, tokens_here, ROW_PARTS, hops, gate_ups, downs)

    arrived_fwd = after(arrived_fwd, partial_bwd[-1])
    total_fwd = summed(partial_fwd[0], arrived_fwd)
    layer_out = (x_forward[0].astype(F32) + prob_forward[0][:, None] * total_fwd).astype(BF16)
    sent_fwd = shifted(layer_out, "pipe", 1)
    size = tokens_here // ROW_PARTS
    partial_bwd = after(tuple(partial_bwd), arrived_fwd)
    blocks = [partial_bwd[part::ROW_PARTS] for part in range(ROW_PARTS)]
    arrived = [None] * ROW_PARTS
    for step in range(1, count):
        for part in range(ROW_PARTS):
            if step == 3 and part == 0:
                arrived[0] = after(arrived[0], sent_fwd)
            arrived[part] = step_home(summands(blocks[part], step, arrived[part]), "dp", step)
    sent_bwd = []
    for part in range(ROW_PARTS):
        rows = slice(part * size, (part + 1) * size)
        total = summed(blocks[part][0], after(arrived[part], sent_bwd))
        grad_in = (grad_output[0, rows].astype(F32) + total).astype(BF16)
        sent_bwd.append(shifted(grad_in, "pipe", -1))
    return (sent_fwd[None], jnp.concatenate(sent_bwd, axis=0)[None])


def from_partner(block, axis, stride):
    count = lax.axis_size(axis)
    route = []
    for low in range(count):
        high = low | 1 << stride
        if high != low and high < count:
            route += [(low, high), (high, low)]
    return lax.ppermute(block, axis, route)


def silu_parts(pre_gate):
    sigma_gate = jax.nn.sigmoid(pre_gate)
    return (pre_gate * sigma_gate, sigma_gate)


def expert_pass(forward_rows, backward_rows, scaled_rows, gate_weight, up_weight, down_weight):
    gate_fwd = jnp.dot(forward_rows, gate_weight, preferred_element_type=jnp.float32)
    up_fwd = jnp.dot(forward_rows, up_weight, preferred_element_type=jnp.float32)
    silu_fwd, sigma_fwd = silu_parts(gate_fwd)
    hidden_fwd = (silu_fwd * up_fwd).astype(jnp.bfloat16)
    expert_out = jnp.dot(hidden_fwd, down_weight, preferred_element_type=jnp.float32)
    gate_bwd = jnp.dot(backward_rows, gate_weight, preferred_element_type=jnp.float32)
    up_bwd = jnp.dot(backward_rows, up_weight, preferred_element_type=jnp.float32)
    silu_bwd, sigma_bwd = silu_parts(gate_bwd)
    grad_hidden = contract_last(scaled_rows, down_weight)
    grad_gate = (grad_hidden * up_bwd * (sigma_bwd + silu_bwd * (1.0 - sigma_bwd))).astype(
        jnp.bfloat16
    )
    grad_up = (grad_hidden * silu_bwd).astype(jnp.bfloat16)
    grad_rows = contract_last(grad_gate, gate_weight) + contract_last(grad_up, up_weight)
    return (expert_out, grad_rows)


def placing(routes, experts_here, capacity):
    route_hits = (routes[:, None] == jnp.arange(experts_here, dtype=jnp.int32)[None, :]).astype(
        jnp.int32
    )
    before = jnp.cumsum(route_hits, axis=0) - route_hits
    slot_index = jnp.sum(before * route_hits, axis=1)
    position = routes * capacity + slot_index
    selector = (
        position[None, :] == jnp.arange(experts_here * capacity, dtype=jnp.int32)[:, None]
    ).astype(jnp.bfloat16)
    return (position, selector)


def packing(selector, values):
    return jnp.dot(selector, values, preferred_element_type=jnp.float32).astype(jnp.bfloat16)


def many_experts(
    x_forward,
    route_forward,
    prob_forward,
    x_backward,
    route_backward,
    prob_backward,
    grad_output,
    w_gate,
    w_up,
    w_down,
):
    tokens_here = x_forward.shape[1]
    feature_width = x_forward.shape[2]
    groups = lax.axis_size("expert")
    experts_here = groups // 2
    capacity = min(tokens_here, (tokens_here * 5 + 4 * experts_here - 1) // (4 * experts_here))
    pair_side = lax.axis_index("expert") % 2
    gate_full, up_full, down_full = (
        lax.all_gather(w_gate[0, 0], "dp", axis=1, tiled=True),
        lax.all_gather(w_up[0, 0], "dp", axis=1, tiled=True),
        lax.all_gather(w_down[0, 0], "dp", axis=0, tiled=True),
    )
    pos_fwd, select_fwd = placing(route_forward[0, :, 0], experts_here, capacity)
    pos_bwd, select_bwd = placing(route_backward[0, :, 0], experts_here, capacity)
    scaled_grad = (prob_backward[0][:, None] * grad_output[0].astype(jnp.float32)).astype(
        jnp.bfloat16
    )
    stacked = jnp.stack(
        [
            packing(select_fwd, x_forward[0]),
            packing(select_bwd, x_backward[0]),
            packing(select_bwd, scaled_grad),
        ]
    )
    stacked = stacked.reshape(3, experts_here, capacity, feature_width)
    split_rows = stacked.reshape(3, experts_here, capacity, 2, feature_width // 2).transpose(
        0, 1, 3, 2, 4
    )
    split_rows = split_rows.reshape(3, groups, capacity, feature_width // 2)
    own_half = lax.all_to_all(split_rows, "expert", split_axis=1, concat_axis=1, tiled=True)
    partner_half = from_partner(own_half, "expert", 0)
    arrived = jnp.where(
        pair_side == 0,
        jnp.concatenate([own_half, partner_half], axis=3),
        jnp.concatenate([partner_half, own_half], axis=3),
    )
    expert_rows = arrived.reshape(3, groups * capacity, feature_width)
    expert_out, grad_rows = expert_pass(
        expert_rows[0], expert_rows[1], expert_rows[2], gate_full, up_full, down_full
    )
    results = jnp.stack([expert_out, grad_rows]).reshape(2, groups, capacity, feature_width)
    quarters = results.reshape(2, groups, capacity, 2, feature_width // 2)
    keep_part = jnp.where(pair_side == 0, quarters[:, :, :, 0], quarters[:, :, :, 1])
    give_part = jnp.where(pair_side == 0, quarters[:, :, :, 1], quarters[:, :, :, 0])
    finished = keep_part + from_partner(give_part.astype(jnp.bfloat16), "expert", 0).astype(
        give_part.dtype
    )
    returned = lax.all_to_all(finished, "expert", split_axis=1, concat_axis=1, tiled=True)
    combined = returned.reshape(2, experts_here, 2, capacity, feature_width // 2).transpose(
        0, 1, 3, 2, 4
    )
    combined = combined.reshape(2, experts_here, capacity, feature_width)
    flat_out = combined.reshape(2, experts_here * capacity, feature_width)
    moved_fwd = jnp.take(flat_out[0], pos_fwd, axis=0)
    moved_bwd = jnp.take(flat_out[1], pos_bwd, axis=0)
    layer_out = (x_forward[0].astype(jnp.float32) + prob_forward[0][:, None] * moved_fwd).astype(
        jnp.bfloat16
    )
    grad_in = (grad_output[0].astype(jnp.float32) + moved_bwd).astype(jnp.bfloat16)
    sent_fwd = shifted(layer_out, "pipe", 1)
    sent_bwd = shifted(grad_in, "pipe", -1)
    return (sent_fwd[None], sent_bwd[None])


def solution(mesh):
    few = mesh.shape["expert"] == 4
    return jax.shard_map(
        few_experts if few else many_experts,
        mesh=mesh,
        in_specs=(
            P("pipe", ("expert", "dp"), None),
            P("pipe", ("expert", "dp"), None),
            P("pipe", ("expert", "dp")),
            P("pipe", ("expert", "dp"), None),
            P("pipe", ("expert", "dp"), None),
            P("pipe", ("expert", "dp")),
            P("pipe", ("expert", "dp"), None),
            P("pipe", "expert", None, "dp"),
            P("pipe", "expert", None, "dp"),
            P("pipe", "expert", "dp", None),
        ),
        out_specs=(P("pipe", ("expert", "dp"), None), P("pipe", ("expert", "dp"), None)),
        check_vma=False,
    )
```

```python
import functools
import math

import jax
import jax.numpy as jnp
from jax import lax
from jax.experimental import pallas as pl
from jax.experimental.pallas import tpu as pltpu
from jax.sharding import PartitionSpec as P

BF16, F32 = jnp.bfloat16, jnp.float32
VMEM_LIMIT = 56 * 1024 * 1024
ROW_PARTS = 2
TAG_COLUMNS = 128


def contract_last(left_side, weights):
    return lax.dot_general(
        left_side, weights, (((1,), (1,)), ((), ())), preferred_element_type=F32
    )


def flipped(block, axis, stride):
    route = [(i, i ^ stride) for i in range(lax.axis_size(axis))]
    return lax.ppermute(block, axis, route)


def shifted(block, axis, distance):
    count = lax.axis_size(axis)
    return lax.ppermute(block, axis, [((i - distance) % count, i) for i in range(count)])


def chunk_of(width, most):
    best = 128
    for size in range(128, most + 1, 128):
        if width % size == 0:
            best = size
    return best


def gathered_rows(refs):
    return jnp.concatenate([ref[0] for ref in refs], axis=0)


def chained_rows(refs):
    others = len(refs) // 2
    own, below, above = refs[0][...], refs[1 : 1 + others], refs[1 + others :]
    return jnp.concatenate(
        [own] + [above[away][...] + below[others - 1 - away][...] for away in range(others)],
        axis=0,
    )


def gathered_input(x, begin, rows):
    count, unit = x.shape[0], math.gcd(begin, rows)
    arrays, specs = [], []
    for turn in range(count):
        for piece in range(begin // unit, (begin + rows) // unit):
            arrays.append(x)
            specs.append(
                lambda chunk, column, turn=turn, piece=piece: pl.BlockSpec(
                    (1, unit, chunk),
                    lambda i, at: (lax.rem(at[0] + turn, count), piece, column(i)),
                )
            )
    return gathered_rows, arrays, specs


def chained_input(hops, begin, rows):
    (own, _), *others = hops
    from_below, from_above = zip(*others)
    arrays = [own, *from_below, *from_above]
    specs = []
    for array in arrays:
        block = begin // rows if array.shape[0] > rows else 0
        specs.append(
            lambda chunk, column, block=block: pl.BlockSpec(
                (rows, chunk), lambda i, at: (block, column(i))
            )
        )
    return chained_rows, arrays, specs


def weight_copies(chunk, steps, gate_ups, downs, gate_up_held, down_held, sems):
    by_chunk = []
    for step in range(steps):
        part = pl.ds(step * chunk, chunk)
        by_chunk.append(
            (
                [
                    pltpu.make_async_copy(
                        ref.at[:, part, :], gate_up_held.at[i, :, part, :], sems.at[0, step, i]
                    )
                    for i, ref in enumerate(gate_ups)
                ],
                [
                    pltpu.make_async_copy(
                        ref.at[:, part], down_held.at[i, :, part], sems.at[1, step, i]
                    )
                    for i, ref in enumerate(downs)
                ],
            )
        )
    return by_chunk


def own_hidden(at_ref, tags, column, hidden):
    mine = tags[:, column : column + 1].astype(jnp.int32) == at_ref[1]
    unit = lax.broadcasted_iota(jnp.int32, (tags.shape[0], hidden), 1)
    return mine == (unit < hidden // 2)


def joined(refs, axis, index=None):
    pick = (lambda ref: ref[...]) if index is None else (lambda ref: ref[index])
    return jnp.concatenate([pick(ref) for ref in refs], axis=axis)


def put_blocks(outs, total):
    rows = outs[0].shape[0]
    for index, ref in enumerate(outs):
        ref[...] = total[index * rows : (index + 1) * rows].astype(ref.dtype)


def compiler_params():
    return pltpu.CompilerParams(vmem_limit_bytes=VMEM_LIMIT)


def small_cost(many, hidden):
    return pl.CostEstimate(flops=many * hidden, bytes_accessed=many, transcendentals=0)


def home_shapes(count, rows, width, parts=1):
    own, others = (jax.ShapeDtypeStruct((rows // parts, width), kind) for kind in (F32, BF16))
    return [own] * parts + [others] * (parts * (count - 1))


def hidden_kernel(count, pieces, steps, at_ref, *refs):
    tags, rows_in, gate_ups = refs[:count], refs[count : 2 * count], refs[2 * count : -3]
    out_ref, gate_ref, up_ref = refs[-3:]
    step = pl.program_id(0)

    @pl.when(step == 0)
    def _():
        gate_ref[...] = jnp.zeros_like(gate_ref)
        up_ref[...] = jnp.zeros_like(up_ref)

    x = gathered_rows(rows_in)
    gate_ref[...] += jnp.dot(x, joined(gate_ups, 1, 0), preferred_element_type=F32)
    up_ref[...] += jnp.dot(x, joined(gate_ups, 1, 1), preferred_element_type=F32)

    @pl.when(step == steps - 1)
    def _():
        gate, up = gate_ref[...], up_ref[...]
        keep = own_hidden(at_ref, gathered_rows(tags), 0, gate.shape[1])
        out_ref[...] = jnp.where(keep, gate * jax.nn.sigmoid(gate) * up, 0.0).astype(BF16)


def hidden_call(at, x_gathered, rows, width, gate_ups):
    count, pieces, hid = x_gathered.shape[0], len(gate_ups), gate_ups[0].shape[2]
    chunk = chunk_of(width, 1792)
    steps, hidden, many = width // chunk, pieces * hid, count * rows
    _, arrays, specs = gathered_input(x_gathered, 0, rows)
    return pl.pallas_call(
        functools.partial(hidden_kernel, count, pieces, steps),
        grid_spec=pltpu.PrefetchScalarGridSpec(
            num_scalar_prefetch=1,
            grid=(steps,),
            in_specs=[spec(TAG_COLUMNS, lambda i: width // TAG_COLUMNS) for spec in specs]
            + [spec(chunk, lambda i: i) for spec in specs]
            + [pl.BlockSpec((2, chunk, hid), lambda i, at: (0, i, 0))] * pieces,
            out_specs=pl.BlockSpec((many, hidden), lambda i, at: (0, 0)),
            scratch_shapes=[pltpu.VMEM((many, hidden), F32)] * 2,
        ),
        out_shape=jax.ShapeDtypeStruct((many, hidden), BF16),
        compiler_params=compiler_params(),
        cost_estimate=small_cost(many, hidden),
    )(at, *arrays, *arrays, *gate_ups)


def down_kernel(pieces, hidden_ref, *refs):
    downs, outs = refs[:pieces], refs[pieces:]
    total = jnp.dot(hidden_ref[...], joined(downs, 0), preferred_element_type=F32)
    put_blocks(outs, total)


def down_call(hidden_rows, count, downs):
    many, hidden = hidden_rows.shape
    pieces, (hid, width), rows = len(downs), downs[0].shape, many // count
    chunk = chunk_of(width, 1792)
    return pl.pallas_call(
        functools.partial(down_kernel, pieces),
        grid=(width // chunk,),
        in_specs=[pl.BlockSpec((many, hidden), lambda i: (0, 0))]
        + [pl.BlockSpec((hid, chunk), lambda i: (0, i))] * pieces,
        out_specs=[pl.BlockSpec((rows, chunk), lambda i: (0, i))] * count,
        out_shape=home_shapes(count, rows, width),
        compiler_params=compiler_params(),
        cost_estimate=small_cost(many, hidden),
    )(hidden_rows, *downs)


def backward_kernel(inputs, count, pieces, chunk, steps, at_ref, *refs):
    tags, refs = refs[:count], refs[count:]
    rows_in, scaled_in, refs = refs[:inputs], refs[inputs : 2 * inputs], refs[2 * inputs :]
    gate_ups, downs, outs = refs[:pieces], refs[pieces : 2 * pieces], refs[2 * pieces : -8]
    gate_ref, up_ref, grad_ref, grad_gate_ref, grad_up_ref = refs[-8:-3]
    gate_up_held, down_held, sems = refs[-3:]
    step = pl.program_id(0)
    copies = weight_copies(chunk, steps, gate_ups, downs, gate_up_held, down_held, sems)

    @pl.when(step == 0)
    def _():
        for of_gate_up, of_down in copies:
            for copy in of_gate_up + of_down:
                copy.start()
        for total in (gate_ref, up_ref, grad_ref):
            total[...] = jnp.zeros_like(total)

    for number, (of_gate_up, of_down) in enumerate(copies):

        @pl.when(step == number)
        def _(waited=of_gate_up + of_down):
            for copy in waited:
                copy.wait()

    at_chunk = pl.ds(pl.multiple_of(lax.rem(step, steps) * chunk, chunk), chunk)

    def gate_or_up(which):
        return jnp.concatenate(
            [gate_up_held[i, which, at_chunk, :] for i in range(pieces)], axis=1
        )

    @pl.when(step < steps)
    def _():
        x = chained_rows(rows_in)
        gate_ref[...] += jnp.dot(x, gate_or_up(0), preferred_element_type=F32)
        up_ref[...] += jnp.dot(x, gate_or_up(1), preferred_element_type=F32)
        down = jnp.concatenate([down_held[i, :, at_chunk] for i in range(pieces)], axis=0)
        grad_ref[...] += contract_last(chained_rows(scaled_in), down)

    @pl.when(step == steps - 1)
    def _():
        gate, up, grad = gate_ref[...], up_ref[...], grad_ref[...]
        keep = own_hidden(at_ref, gathered_rows(tags), TAG_COLUMNS // 2, gate.shape[1])
        s = jax.nn.sigmoid(gate)
        silu = gate * s
        grad_gate = grad * up * (s + silu * (1.0 - s))
        grad_gate_ref[...] = jnp.where(keep, grad_gate, 0.0).astype(BF16)
        grad_up_ref[...] = jnp.where(keep, grad * silu, 0.0).astype(BF16)

    @pl.when(step >= steps)
    def _():
        total = contract_last(grad_gate_ref[...], gate_or_up(0))
        total += contract_last(grad_up_ref[...], gate_or_up(1))
        put_blocks(outs, total)


def backward_call(at, x_gathered, rows, parts, hops, last_hops, gate_ups, downs):
    count, width = x_gathered.shape[0], hops[0][0].shape[1]
    pieces, hid = len(downs), downs[0].shape[0]
    chunk = chunk_of(width, 1792)
    steps, hidden, many = width // chunk, pieces * hid, count * rows
    first = lambda i: jnp.minimum(i, steps - 1)
    second = lambda i: jnp.maximum(i - steps, 0)
    _, tags, tag_specs = gathered_input(x_gathered, 0, rows)
    _, rows_in, row_specs = chained_input([*hops, last_hops[0]], 0, rows)
    _, scaled_in, scaled_specs = chained_input([*hops, last_hops[1]], rows, rows)
    return pl.pallas_call(
        functools.partial(backward_kernel, len(rows_in), count, pieces, chunk, steps),
        grid_spec=pltpu.PrefetchScalarGridSpec(
            num_scalar_prefetch=1,
            grid=(2 * steps,),
            in_specs=[spec(TAG_COLUMNS, lambda i: width // TAG_COLUMNS) for spec in tag_specs]
            + [spec(chunk, first) for spec in row_specs + scaled_specs]
            + [pl.BlockSpec(memory_space=pl.ANY)] * (2 * pieces),
            out_specs=[pl.BlockSpec((rows // parts, chunk), lambda i, at: (0, second(i)))]
            * (parts * count),
            scratch_shapes=[pltpu.VMEM((many, hidden), F32)] * 3
            + [pltpu.VMEM((many, hidden), BF16)] * 2
            + [
                pltpu.VMEM((pieces, 2, width, hid), BF16),
                pltpu.VMEM((pieces, hid, width), BF16),
                pltpu.SemaphoreType.DMA((2, steps, pieces)),
            ],
        ),
        out_shape=home_shapes(count, rows, width, parts),
        compiler_params=compiler_params(),
        cost_estimate=small_cost(many, hidden),
    )(at, *tags, *rows_in, *scaled_in, *gate_ups, *downs)


def after(value, *earlier):
    return lax.optimization_barrier((value, earlier))[0]


def hop(below, above, axis, step):
    count = lax.axis_size(axis)
    up = [(i, i + 1) for i in range(step - 1, count - 1)]
    down = [(i, i - 1) for i in range(1, count - step + 1)]
    return lax.ppermute(below, axis, up), lax.ppermute(above, axis, down)


def summands(blocks, step, arrived):
    pair = (blocks[len(blocks) - step], blocks[step])
    if arrived is None:
        return pair
    return tuple(
        (own.astype(F32) + other.astype(F32)).astype(BF16) for own, other in zip(pair, arrived)
    )


def step_home(pair, axis, step):
    count = lax.axis_size(axis)
    up = lax.ppermute(pair[0], axis, [(i, i + 1) for i in range(step)])
    down = lax.ppermute(pair[1], axis, [(i, i - 1) for i in range(count - step, count)])
    return up, down


def summed(block, arrived):
    for part in arrived:
        block = block + part.astype(F32)
    return block


def few_experts(
    x_forward,
    route_forward,
    prob_forward,
    x_backward,
    route_backward,
    prob_backward,
    grad_output,
    w_gate,
    w_up,
    w_down,
):
    tokens_here, width = x_forward.shape[1:]
    expert_here = lax.axis_index("expert") // 2
    count = lax.axis_size("dp")
    at = jnp.stack([lax.axis_index("dp"), expert_here]).astype(jnp.int32)
    half_tag = (tokens_here, TAG_COLUMNS // 2)
    tagged = jnp.concatenate(
        [x_forward[0]]
        + [jnp.broadcast_to(r[0].astype(BF16), half_tag) for r in (route_forward, route_backward)],
        axis=1,
    )
    scaled_grad = (prob_backward[0][:, None] * grad_output[0].astype(F32)).astype(BF16)
    back_rows = jnp.concatenate([x_backward[0], scaled_grad], axis=0)
    gate_up, down = jnp.concatenate([w_gate[0], w_up[0]], axis=0), w_down[0, 0]

    x_gathered = lax.all_gather(tagged, "dp")
    across_down = flipped(down, "expert", 2)
    gate_up, back_rows = after((gate_up, back_rows), across_down)
    across_gate_up = flipped(gate_up, "expert", 2)
    hops = [(back_rows, back_rows)]
    for step in range(1, count - 1):
        hops.append(hop(*hops[-1], "dp", step))
    downs = [down, flipped(down, "expert", 1), across_down, flipped(across_down, "expert", 1)]
    own_flip = flipped(after(gate_up, hops[1], downs[1], downs[3]), "expert", 1)
    gate_ups = [gate_up, own_flip, across_gate_up]
    gate_ups.append(flipped(after(across_gate_up, x_gathered, own_flip), "expert", 1))
    hidden_fwd = hidden_call(at, x_gathered, tokens_here, width, gate_ups)
    partial_fwd = down_call(hidden_fwd, count, downs)
    last_hops, arrived_rows = [], after(hops[-1], partial_fwd[-1])
    for part in (slice(0, tokens_here), slice(tokens_here, None)):
        below, above = (rows[part] for rows in arrived_rows)
        last_hops.append(hop(below, above, "dp", count - 1))

    arrived_fwd = step_home(summands(partial_fwd, 1, None), "dp", 1)
    arrived_fwd = after(arrived_fwd, last_hops[0])
    arrived_fwd = step_home(summands(partial_fwd, 2, arrived_fwd), "dp", 2)
    sends_fwd = summands(partial_fwd, 3, arrived_fwd)
    arrived_fwd = step_home(sends_fwd, "dp", 3)
    hops[0] = after(hops[0], sends_fwd)
    partial_bwd = backward_call(
        at, x_gathered, tokens_here, ROW_PARTS, hops, last_hops, gate_ups, downs
    )

    arrived_fwd = after(arrived_fwd, partial_bwd[-1])
    total_fwd = summed(partial_fwd[0], arrived_fwd)
    layer_out = (x_forward[0].astype(F32) + prob_forward[0][:, None] * total_fwd).astype(BF16)
    sent_fwd = shifted(layer_out, "pipe", 1)
    size = tokens_here // ROW_PARTS
    partial_bwd = after(tuple(partial_bwd), arrived_fwd)
    blocks = [partial_bwd[part::ROW_PARTS] for part in range(ROW_PARTS)]
    arrived = [None] * ROW_PARTS
    for step in range(1, count):
        for part in range(ROW_PARTS):
            if step == 3 and part == 0:
                arrived[0] = after(arrived[0], sent_fwd)
            arrived[part] = step_home(summands(blocks[part], step, arrived[part]), "dp", step)
    sent_bwd = []
    for part in range(ROW_PARTS):
        rows = slice(part * size, (part + 1) * size)
        total = summed(blocks[part][0], after(arrived[part], sent_bwd))
        grad_in = (grad_output[0, rows].astype(F32) + total).astype(BF16)
        sent_bwd.append(shifted(grad_in, "pipe", -1))
    return (sent_fwd[None], jnp.concatenate(sent_bwd, axis=0)[None])


def from_partner(block, axis, stride):
    count = lax.axis_size(axis)
    route = []
    for low in range(count):
        high = low | 1 << stride
        if high != low and high < count:
            route += [(low, high), (high, low)]
    return lax.ppermute(block, axis, route)


def silu_parts(pre_gate):
    sigma_gate = jax.nn.sigmoid(pre_gate)
    return (pre_gate * sigma_gate, sigma_gate)


def expert_pass(forward_rows, backward_rows, scaled_rows, gate_weight, up_weight, down_weight):
    gate_fwd = jnp.dot(forward_rows, gate_weight, preferred_element_type=jnp.float32)
    up_fwd = jnp.dot(forward_rows, up_weight, preferred_element_type=jnp.float32)
    silu_fwd, sigma_fwd = silu_parts(gate_fwd)
    hidden_fwd = (silu_fwd * up_fwd).astype(jnp.bfloat16)
    expert_out = jnp.dot(hidden_fwd, down_weight, preferred_element_type=jnp.float32)
    gate_bwd = jnp.dot(backward_rows, gate_weight, preferred_element_type=jnp.float32)
    up_bwd = jnp.dot(backward_rows, up_weight, preferred_element_type=jnp.float32)
    silu_bwd, sigma_bwd = silu_parts(gate_bwd)
    grad_hidden = contract_last(scaled_rows, down_weight)
    grad_gate = (grad_hidden * up_bwd * (sigma_bwd + silu_bwd * (1.0 - sigma_bwd))).astype(
        jnp.bfloat16
    )
    grad_up = (grad_hidden * silu_bwd).astype(jnp.bfloat16)
    grad_rows = contract_last(grad_gate, gate_weight) + contract_last(grad_up, up_weight)
    return (expert_out, grad_rows)


def placing(routes, experts_here, capacity):
    route_hits = (routes[:, None] == jnp.arange(experts_here, dtype=jnp.int32)[None, :]).astype(
        jnp.int32
    )
    before = jnp.cumsum(route_hits, axis=0) - route_hits
    slot_index = jnp.sum(before * route_hits, axis=1)
    position = routes * capacity + slot_index
    selector = (
        position[None, :] == jnp.arange(experts_here * capacity, dtype=jnp.int32)[:, None]
    ).astype(jnp.bfloat16)
    return (position, selector)


def packing(selector, values):
    return jnp.dot(selector, values, preferred_element_type=jnp.float32).astype(jnp.bfloat16)


def many_experts(
    x_forward,
    route_forward,
    prob_forward,
    x_backward,
    route_backward,
    prob_backward,
    grad_output,
    w_gate,
    w_up,
    w_down,
):
    tokens_here = x_forward.shape[1]
    feature_width = x_forward.shape[2]
    groups = lax.axis_size("expert")
    experts_here = groups // 2
    capacity = min(tokens_here, (tokens_here * 5 + 4 * experts_here - 1) // (4 * experts_here))
    pair_side = lax.axis_index("expert") % 2
    gate_full, up_full, down_full = (
        lax.all_gather(w_gate[0, 0], "dp", axis=1, tiled=True),
        lax.all_gather(w_up[0, 0], "dp", axis=1, tiled=True),
        lax.all_gather(w_down[0, 0], "dp", axis=0, tiled=True),
    )
    pos_fwd, select_fwd = placing(route_forward[0, :, 0], experts_here, capacity)
    pos_bwd, select_bwd = placing(route_backward[0, :, 0], experts_here, capacity)
    scaled_grad = (prob_backward[0][:, None] * grad_output[0].astype(jnp.float32)).astype(
        jnp.bfloat16
    )
    stacked = jnp.stack(
        [
            packing(select_fwd, x_forward[0]),
            packing(select_bwd, x_backward[0]),
            packing(select_bwd, scaled_grad),
        ]
    )
    stacked = stacked.reshape(3, experts_here, capacity, feature_width)
    split_rows = stacked.reshape(3, experts_here, capacity, 2, feature_width // 2).transpose(
        0, 1, 3, 2, 4
    )
    split_rows = split_rows.reshape(3, groups, capacity, feature_width // 2)
    own_half = lax.all_to_all(split_rows, "expert", split_axis=1, concat_axis=1, tiled=True)
    partner_half = from_partner(own_half, "expert", 0)
    arrived = jnp.where(
        pair_side == 0,
        jnp.concatenate([own_half, partner_half], axis=3),
        jnp.concatenate([partner_half, own_half], axis=3),
    )
    expert_rows = arrived.reshape(3, groups * capacity, feature_width)
    expert_out, grad_rows = expert_pass(
        expert_rows[0], expert_rows[1], expert_rows[2], gate_full, up_full, down_full
    )
    results = jnp.stack([expert_out, grad_rows]).reshape(2, groups, capacity, feature_width)
    quarters = results.reshape(2, groups, capacity, 2, feature_width // 2)
    keep_part = jnp.where(pair_side == 0, quarters[:, :, :, 0], quarters[:, :, :, 1])
    give_part = jnp.where(pair_side == 0, quarters[:, :, :, 1], quarters[:, :, :, 0])
    finished = keep_part + from_partner(give_part.astype(jnp.bfloat16), "expert", 0).astype(
        give_part.dtype
    )
    returned = lax.all_to_all(finished, "expert", split_axis=1, concat_axis=1, tiled=True)
    combined = returned.reshape(2, experts_here, 2, capacity, feature_width // 2).transpose(
        0, 1, 3, 2, 4
    )
    combined = combined.reshape(2, experts_here, capacity, feature_width)
    flat_out = combined.reshape(2, experts_here * capacity, feature_width)
    moved_fwd = jnp.take(flat_out[0], pos_fwd, axis=0)
    moved_bwd = jnp.take(flat_out[1], pos_bwd, axis=0)
    layer_out = (x_forward[0].astype(jnp.float32) + prob_forward[0][:, None] * moved_fwd).astype(
        jnp.bfloat16
    )
    grad_in = (grad_output[0].astype(jnp.float32) + moved_bwd).astype(jnp.bfloat16)
    sent_fwd = shifted(layer_out, "pipe", 1)
    sent_bwd = shifted(grad_in, "pipe", -1)
    return (sent_fwd[None], sent_bwd[None])


def solution(mesh):
    few = mesh.shape["expert"] == 4
    return jax.shard_map(
        few_experts if few else many_experts,
        mesh=mesh,
        in_specs=(
            P("pipe", ("expert", "dp"), None),
            P("pipe", ("expert", "dp"), None),
            P("pipe", ("expert", "dp")),
            P("pipe", ("expert", "dp"), None),
            P("pipe", ("expert", "dp"), None),
            P("pipe", ("expert", "dp")),
            P("pipe", ("expert", "dp"), None),
            P("pipe", "expert", None, "dp"),
            P("pipe", "expert", None, "dp"),
            P("pipe", "expert", "dp", None),
        ),
        out_specs=(P("pipe", ("expert", "dp"), None), P("pipe", ("expert", "dp"), None)),
        check_vma=False,
    )
```

```python
import functools
import math

import jax
import jax.numpy as jnp
from jax import lax
from jax.experimental import pallas as pl
from jax.experimental.pallas import tpu as pltpu
from jax.sharding import PartitionSpec as P

BF16, F32 = jnp.bfloat16, jnp.float32
VMEM_LIMIT = 44 * 1024 * 1024
ROW_PARTS = 2
TAG_COLUMNS = 128


def contract_last(left_side, weights):
    return lax.dot_general(
        left_side, weights, (((1,), (1,)), ((), ())), preferred_element_type=F32
    )


def flipped(block, axis, stride):
    route = [(i, i ^ stride) for i in range(lax.axis_size(axis))]
    return lax.ppermute(block, axis, route)


def shifted(block, axis, distance):
    count = lax.axis_size(axis)
    return lax.ppermute(block, axis, [((i - distance) % count, i) for i in range(count)])


def chunk_of(width, most):
    best = 128
    for size in range(128, most + 1, 128):
        if width % size == 0:
            best = size
    return best


def gathered_rows(refs):
    return jnp.concatenate([ref[0] for ref in refs], axis=0)


def chained_rows(refs):
    others = len(refs) // 2
    own, below, above = refs[0][...], refs[1 : 1 + others], refs[1 + others :]
    return jnp.concatenate(
        [own] + [above[away][...] + below[others - 1 - away][...] for away in range(others)],
        axis=0,
    )


def gathered_input(x, begin, rows):
    count, unit = x.shape[0], math.gcd(begin, rows)
    arrays, specs = [], []
    for turn in range(count):
        for piece in range(begin // unit, (begin + rows) // unit):
            arrays.append(x)
            specs.append(
                lambda chunk, column, turn=turn, piece=piece: pl.BlockSpec(
                    (1, unit, chunk),
                    lambda i, at: (lax.rem(at[0] + turn, count), piece, column(i)),
                )
            )
    return gathered_rows, arrays, specs


def chained_input(hops, begin, rows):
    (own, _), *others = hops
    from_below, from_above = zip(*others)
    spec = lambda chunk, column: pl.BlockSpec(
        (rows, chunk), lambda i, at: (begin // rows, column(i))
    )
    arrays = [own, *from_below, *from_above]
    return chained_rows, arrays, [spec] * len(arrays)


def weight_copies(chunk, steps, gate_ups, downs, gate_up_held, down_held, sems):
    by_chunk = []
    for step in range(steps):
        part = pl.ds(step * chunk, chunk)
        by_chunk.append(
            (
                [
                    pltpu.make_async_copy(
                        ref.at[:, part, :], gate_up_held.at[i, :, part, :], sems.at[0, step, i]
                    )
                    for i, ref in enumerate(gate_ups)
                ],
                [
                    pltpu.make_async_copy(
                        ref.at[:, part], down_held.at[i, :, part], sems.at[1, step, i]
                    )
                    for i, ref in enumerate(downs)
                ],
            )
        )
    return by_chunk


def own_hidden(at_ref, tags, column, hidden):
    mine = tags[:, column : column + 1].astype(jnp.int32) == at_ref[1]
    unit = lax.broadcasted_iota(jnp.int32, (tags.shape[0], hidden), 1)
    return mine == (unit < hidden // 2)


def joined(refs, axis, index=None):
    pick = (lambda ref: ref[...]) if index is None else (lambda ref: ref[index])
    return jnp.concatenate([pick(ref) for ref in refs], axis=axis)


def put_blocks(outs, total):
    rows = outs[0].shape[0]
    for index, ref in enumerate(outs):
        ref[...] = total[index * rows : (index + 1) * rows].astype(ref.dtype)


def compiler_params():
    return pltpu.CompilerParams(vmem_limit_bytes=VMEM_LIMIT)


def small_cost(many, hidden):
    return pl.CostEstimate(flops=many * hidden, bytes_accessed=many, transcendentals=0)


def home_shapes(count, rows, width, parts=1):
    own, others = (jax.ShapeDtypeStruct((rows // parts, width), kind) for kind in (F32, BF16))
    return [own] * parts + [others] * (parts * (count - 1))


def hidden_kernel(count, pieces, steps, at_ref, *refs):
    tags, rows_in, gate_ups = refs[:count], refs[count : 2 * count], refs[2 * count : -3]
    out_ref, gate_ref, up_ref = refs[-3:]
    step = pl.program_id(0)

    @pl.when(step == 0)
    def _():
        gate_ref[...] = jnp.zeros_like(gate_ref)
        up_ref[...] = jnp.zeros_like(up_ref)

    x = gathered_rows(rows_in)
    gate_ref[...] += jnp.dot(x, joined(gate_ups, 1, 0), preferred_element_type=F32)
    up_ref[...] += jnp.dot(x, joined(gate_ups, 1, 1), preferred_element_type=F32)

    @pl.when(step == steps - 1)
    def _():
        gate, up = gate_ref[...], up_ref[...]
        keep = own_hidden(at_ref, gathered_rows(tags), 0, gate.shape[1])
        out_ref[...] = jnp.where(keep, gate * jax.nn.sigmoid(gate) * up, 0.0).astype(BF16)


def hidden_call(at, x_gathered, rows, width, gate_ups):
    count, pieces, hid = x_gathered.shape[0], len(gate_ups), gate_ups[0].shape[2]
    chunk = chunk_of(width, 1792)
    steps, hidden, many = width // chunk, pieces * hid, count * rows
    _, arrays, specs = gathered_input(x_gathered, 0, rows)
    return pl.pallas_call(
        functools.partial(hidden_kernel, count, pieces, steps),
        grid_spec=pltpu.PrefetchScalarGridSpec(
            num_scalar_prefetch=1,
            grid=(steps,),
            in_specs=[spec(TAG_COLUMNS, lambda i: width // TAG_COLUMNS) for spec in specs]
            + [spec(chunk, lambda i: i) for spec in specs]
            + [pl.BlockSpec((2, chunk, hid), lambda i, at: (0, i, 0))] * pieces,
            out_specs=pl.BlockSpec((many, hidden), lambda i, at: (0, 0)),
            scratch_shapes=[pltpu.VMEM((many, hidden), F32)] * 2,
        ),
        out_shape=jax.ShapeDtypeStruct((many, hidden), BF16),
        compiler_params=compiler_params(),
        cost_estimate=small_cost(many, hidden),
    )(at, *arrays, *arrays, *gate_ups)


def down_kernel(pieces, hidden_ref, *refs):
    downs, outs = refs[:pieces], refs[pieces:]
    total = jnp.dot(hidden_ref[...], joined(downs, 0), preferred_element_type=F32)
    put_blocks(outs, total)


def down_call(hidden_rows, count, downs):
    many, hidden = hidden_rows.shape
    pieces, (hid, width), rows = len(downs), downs[0].shape, many // count
    chunk = chunk_of(width, 1792)
    return pl.pallas_call(
        functools.partial(down_kernel, pieces),
        grid=(width // chunk,),
        in_specs=[pl.BlockSpec((many, hidden), lambda i: (0, 0))]
        + [pl.BlockSpec((hid, chunk), lambda i: (0, i))] * pieces,
        out_specs=[pl.BlockSpec((rows, chunk), lambda i: (0, i))] * count,
        out_shape=home_shapes(count, rows, width),
        compiler_params=compiler_params(),
        cost_estimate=small_cost(many, hidden),
    )(hidden_rows, *downs)


def backward_kernel(inputs, count, pieces, chunk, steps, at_ref, *refs):
    tags, refs = refs[:count], refs[count:]
    rows_in, scaled_in, refs = refs[:inputs], refs[inputs : 2 * inputs], refs[2 * inputs :]
    gate_ups, downs, outs = refs[:pieces], refs[pieces : 2 * pieces], refs[2 * pieces : -8]
    gate_ref, up_ref, grad_ref, grad_gate_ref, grad_up_ref = refs[-8:-3]
    gate_up_held, down_held, sems = refs[-3:]
    step = pl.program_id(0)
    copies = weight_copies(chunk, steps, gate_ups, downs, gate_up_held, down_held, sems)

    @pl.when(step == 0)
    def _():
        for of_gate_up, of_down in copies:
            for copy in of_gate_up + of_down:
                copy.start()
        for total in (gate_ref, up_ref, grad_ref):
            total[...] = jnp.zeros_like(total)

    for number, (of_gate_up, of_down) in enumerate(copies):

        @pl.when(step == number)
        def _(waited=of_gate_up + of_down):
            for copy in waited:
                copy.wait()

    at_chunk = pl.ds(pl.multiple_of(lax.rem(step, steps) * chunk, chunk), chunk)

    def gate_or_up(which):
        return jnp.concatenate(
            [gate_up_held[i, which, at_chunk, :] for i in range(pieces)], axis=1
        )

    @pl.when(step < steps)
    def _():
        x = chained_rows(rows_in)
        gate_ref[...] += jnp.dot(x, gate_or_up(0), preferred_element_type=F32)
        up_ref[...] += jnp.dot(x, gate_or_up(1), preferred_element_type=F32)
        down = jnp.concatenate([down_held[i, :, at_chunk] for i in range(pieces)], axis=0)
        grad_ref[...] += contract_last(chained_rows(scaled_in), down)

    @pl.when(step == steps - 1)
    def _():
        gate, up, grad = gate_ref[...], up_ref[...], grad_ref[...]
        keep = own_hidden(at_ref, gathered_rows(tags), TAG_COLUMNS // 2, gate.shape[1])
        s = jax.nn.sigmoid(gate)
        silu = gate * s
        grad_gate = grad * up * (s + silu * (1.0 - s))
        grad_gate_ref[...] = jnp.where(keep, grad_gate, 0.0).astype(BF16)
        grad_up_ref[...] = jnp.where(keep, grad * silu, 0.0).astype(BF16)

    @pl.when(step >= steps)
    def _():
        total = contract_last(grad_gate_ref[...], gate_or_up(0))
        total += contract_last(grad_up_ref[...], gate_or_up(1))
        put_blocks(outs, total)


def backward_call(at, x_gathered, rows, parts, hops, gate_ups, downs):
    count, width = x_gathered.shape[0], hops[0][0].shape[1]
    pieces, hid = len(downs), downs[0].shape[0]
    chunk = chunk_of(width, 1792)
    steps, hidden, many = width // chunk, pieces * hid, count * rows
    first = lambda i: jnp.minimum(i, steps - 1)
    second = lambda i: jnp.maximum(i - steps, 0)
    _, tags, tag_specs = gathered_input(x_gathered, 0, rows)
    _, rows_in, row_specs = chained_input(hops, 0, rows)
    _, _, scaled_specs = chained_input(hops, rows, rows)
    return pl.pallas_call(
        functools.partial(backward_kernel, len(rows_in), count, pieces, chunk, steps),
        grid_spec=pltpu.PrefetchScalarGridSpec(
            num_scalar_prefetch=1,
            grid=(2 * steps,),
            in_specs=[spec(TAG_COLUMNS, lambda i: width // TAG_COLUMNS) for spec in tag_specs]
            + [spec(chunk, first) for spec in row_specs + scaled_specs]
            + [pl.BlockSpec(memory_space=pl.ANY)] * (2 * pieces),
            out_specs=[pl.BlockSpec((rows // parts, chunk), lambda i, at: (0, second(i)))]
            * (parts * count),
            scratch_shapes=[pltpu.VMEM((many, hidden), F32)] * 3
            + [pltpu.VMEM((many, hidden), BF16)] * 2
            + [
                pltpu.VMEM((pieces, 2, width, hid), BF16),
                pltpu.VMEM((pieces, hid, width), BF16),
                pltpu.SemaphoreType.DMA((2, steps, pieces)),
            ],
        ),
        out_shape=home_shapes(count, rows, width, parts),
        compiler_params=compiler_params(),
        cost_estimate=small_cost(many, hidden),
    )(at, *tags, *rows_in, *rows_in, *gate_ups, *downs)


def after(value, *earlier):
    return lax.optimization_barrier((value, earlier))[0]


def hop(below, above, axis, step):
    count = lax.axis_size(axis)
    up = [(i, i + 1) for i in range(step - 1, count - 1)]
    down = [(i, i - 1) for i in range(1, count - step + 1)]
    return lax.ppermute(below, axis, up), lax.ppermute(above, axis, down)


def summands(blocks, step, arrived):
    pair = (blocks[len(blocks) - step], blocks[step])
    if arrived is None:
        return pair
    return tuple(
        (own.astype(F32) + other.astype(F32)).astype(BF16) for own, other in zip(pair, arrived)
    )


def step_home(pair, axis, step):
    count = lax.axis_size(axis)
    up = lax.ppermute(pair[0], axis, [(i, i + 1) for i in range(step)])
    down = lax.ppermute(pair[1], axis, [(i, i - 1) for i in range(count - step, count)])
    return up, down


def summed(block, arrived):
    for part in arrived:
        block = block + part.astype(F32)
    return block


def few_experts(
    x_forward,
    route_forward,
    prob_forward,
    x_backward,
    route_backward,
    prob_backward,
    grad_output,
    w_gate,
    w_up,
    w_down,
):
    tokens_here, width = x_forward.shape[1:]
    expert_here = lax.axis_index("expert") // 2
    count = lax.axis_size("dp")
    at = jnp.stack([lax.axis_index("dp"), expert_here]).astype(jnp.int32)
    half_tag = (tokens_here, TAG_COLUMNS // 2)
    tagged = jnp.concatenate(
        [x_forward[0]]
        + [jnp.broadcast_to(r[0].astype(BF16), half_tag) for r in (route_forward, route_backward)],
        axis=1,
    )
    scaled_grad = (prob_backward[0][:, None] * grad_output[0].astype(F32)).astype(BF16)
    back_rows = jnp.concatenate([x_backward[0], scaled_grad], axis=0)
    gate_up, down = jnp.concatenate([w_gate[0], w_up[0]], axis=0), w_down[0, 0]

    x_gathered = lax.all_gather(tagged, "dp")
    across_down = flipped(down, "expert", 2)
    gate_up, back_rows = after((gate_up, back_rows), across_down)
    across_gate_up = flipped(gate_up, "expert", 2)
    hops = [(back_rows, back_rows)]
    for step in range(1, count):
        hops.append(hop(*hops[-1], "dp", step))
    gate_ups = [gate_up, flipped(after(gate_up, hops[1]), "expert", 1), across_gate_up]
    downs = [down, flipped(down, "expert", 1), across_down, flipped(across_down, "expert", 1)]
    gate_ups.append(flipped(after(across_gate_up, x_gathered, hops[1], downs[1:]), "expert", 1))
    hidden_fwd = hidden_call(at, x_gathered, tokens_here, width, gate_ups)
    partial_fwd = down_call(hidden_fwd, count, downs)

    arrived_fwd = step_home(summands(partial_fwd, 1, None), "dp", 1)
    arrived_fwd = after(arrived_fwd, hops[2])
    arrived_fwd = step_home(summands(partial_fwd, 2, arrived_fwd), "dp", 2)
    sends_fwd = summands(partial_fwd, 3, arrived_fwd)
    arrived_fwd = step_home(sends_fwd, "dp", 3)
    hops[0] = after(hops[0], sends_fwd)
    partial_bwd = backward_call(at, x_gathered, tokens_here, ROW_PARTS, hops, gate_ups, downs)

    arrived_fwd = after(arrived_fwd, partial_bwd[-1])
    total_fwd = summed(partial_fwd[0], arrived_fwd)
    layer_out = (x_forward[0].astype(F32) + prob_forward[0][:, None] * total_fwd).astype(BF16)
    sent_fwd = shifted(layer_out, "pipe", 1)
    size = tokens_here // ROW_PARTS
    partial_bwd = after(tuple(partial_bwd), arrived_fwd)
    blocks = [partial_bwd[part::ROW_PARTS] for part in range(ROW_PARTS)]
    arrived = [None] * ROW_PARTS
    for step in range(1, count):
        for part in range(ROW_PARTS):
            if step == 3 and part == 0:
                arrived[0] = after(arrived[0], sent_fwd)
            arrived[part] = step_home(summands(blocks[part], step, arrived[part]), "dp", step)
    sent_bwd = []
    for part in range(ROW_PARTS):
        rows = slice(part * size, (part + 1) * size)
        total = summed(blocks[part][0], after(arrived[part], sent_bwd))
        grad_in = (grad_output[0, rows].astype(F32) + total).astype(BF16)
        sent_bwd.append(shifted(grad_in, "pipe", -1))
    return (sent_fwd[None], jnp.concatenate(sent_bwd, axis=0)[None])


def from_partner(block, axis, stride):
    count = lax.axis_size(axis)
    route = []
    for low in range(count):
        high = low | 1 << stride
        if high != low and high < count:
            route += [(low, high), (high, low)]
    return lax.ppermute(block, axis, route)


def silu_parts(pre_gate):
    sigma_gate = jax.nn.sigmoid(pre_gate)
    return (pre_gate * sigma_gate, sigma_gate)


def expert_pass(forward_rows, backward_rows, scaled_rows, gate_weight, up_weight, down_weight):
    gate_fwd = jnp.dot(forward_rows, gate_weight, preferred_element_type=jnp.float32)
    up_fwd = jnp.dot(forward_rows, up_weight, preferred_element_type=jnp.float32)
    silu_fwd, sigma_fwd = silu_parts(gate_fwd)
    hidden_fwd = (silu_fwd * up_fwd).astype(jnp.bfloat16)
    expert_out = jnp.dot(hidden_fwd, down_weight, preferred_element_type=jnp.float32)
    gate_bwd = jnp.dot(backward_rows, gate_weight, preferred_element_type=jnp.float32)
    up_bwd = jnp.dot(backward_rows, up_weight, preferred_element_type=jnp.float32)
    silu_bwd, sigma_bwd = silu_parts(gate_bwd)
    grad_hidden = contract_last(scaled_rows, down_weight)
    grad_gate = (grad_hidden * up_bwd * (sigma_bwd + silu_bwd * (1.0 - sigma_bwd))).astype(
        jnp.bfloat16
    )
    grad_up = (grad_hidden * silu_bwd).astype(jnp.bfloat16)
    grad_rows = contract_last(grad_gate, gate_weight) + contract_last(grad_up, up_weight)
    return (expert_out, grad_rows)


def placing(routes, experts_here, capacity):
    route_hits = (routes[:, None] == jnp.arange(experts_here, dtype=jnp.int32)[None, :]).astype(
        jnp.int32
    )
    before = jnp.cumsum(route_hits, axis=0) - route_hits
    slot_index = jnp.sum(before * route_hits, axis=1)
    position = routes * capacity + slot_index
    selector = (
        position[None, :] == jnp.arange(experts_here * capacity, dtype=jnp.int32)[:, None]
    ).astype(jnp.bfloat16)
    return (position, selector)


def packing(selector, values):
    return jnp.dot(selector, values, preferred_element_type=jnp.float32).astype(jnp.bfloat16)


def many_experts(
    x_forward,
    route_forward,
    prob_forward,
    x_backward,
    route_backward,
    prob_backward,
    grad_output,
    w_gate,
    w_up,
    w_down,
):
    tokens_here = x_forward.shape[1]
    feature_width = x_forward.shape[2]
    groups = lax.axis_size("expert")
    experts_here = groups // 2
    capacity = min(tokens_here, (tokens_here * 5 + 4 * experts_here - 1) // (4 * experts_here))
    pair_side = lax.axis_index("expert") % 2
    gate_full, up_full, down_full = (
        lax.all_gather(w_gate[0, 0], "dp", axis=1, tiled=True),
        lax.all_gather(w_up[0, 0], "dp", axis=1, tiled=True),
        lax.all_gather(w_down[0, 0], "dp", axis=0, tiled=True),
    )
    pos_fwd, select_fwd = placing(route_forward[0, :, 0], experts_here, capacity)
    pos_bwd, select_bwd = placing(route_backward[0, :, 0], experts_here, capacity)
    scaled_grad = (prob_backward[0][:, None] * grad_output[0].astype(jnp.float32)).astype(
        jnp.bfloat16
    )
    stacked = jnp.stack(
        [
            packing(select_fwd, x_forward[0]),
            packing(select_bwd, x_backward[0]),
            packing(select_bwd, scaled_grad),
        ]
    )
    stacked = stacked.reshape(3, experts_here, capacity, feature_width)
    split_rows = stacked.reshape(3, experts_here, capacity, 2, feature_width // 2).transpose(
        0, 1, 3, 2, 4
    )
    split_rows = split_rows.reshape(3, groups, capacity, feature_width // 2)
    own_half = lax.all_to_all(split_rows, "expert", split_axis=1, concat_axis=1, tiled=True)
    partner_half = from_partner(own_half, "expert", 0)
    arrived = jnp.where(
        pair_side == 0,
        jnp.concatenate([own_half, partner_half], axis=3),
        jnp.concatenate([partner_half, own_half], axis=3),
    )
    expert_rows = arrived.reshape(3, groups * capacity, feature_width)
    expert_out, grad_rows = expert_pass(
        expert_rows[0], expert_rows[1], expert_rows[2], gate_full, up_full, down_full
    )
    results = jnp.stack([expert_out, grad_rows]).reshape(2, groups, capacity, feature_width)
    quarters = results.reshape(2, groups, capacity, 2, feature_width // 2)
    keep_part = jnp.where(pair_side == 0, quarters[:, :, :, 0], quarters[:, :, :, 1])
    give_part = jnp.where(pair_side == 0, quarters[:, :, :, 1], quarters[:, :, :, 0])
    finished = keep_part + from_partner(give_part.astype(jnp.bfloat16), "expert", 0).astype(
        give_part.dtype
    )
    returned = lax.all_to_all(finished, "expert", split_axis=1, concat_axis=1, tiled=True)
    combined = returned.reshape(2, experts_here, 2, capacity, feature_width // 2).transpose(
        0, 1, 3, 2, 4
    )
    combined = combined.reshape(2, experts_here, capacity, feature_width)
    flat_out = combined.reshape(2, experts_here * capacity, feature_width)
    moved_fwd = jnp.take(flat_out[0], pos_fwd, axis=0)
    moved_bwd = jnp.take(flat_out[1], pos_bwd, axis=0)
    layer_out = (x_forward[0].astype(jnp.float32) + prob_forward[0][:, None] * moved_fwd).astype(
        jnp.bfloat16
    )
    grad_in = (grad_output[0].astype(jnp.float32) + moved_bwd).astype(jnp.bfloat16)
    sent_fwd = shifted(layer_out, "pipe", 1)
    sent_bwd = shifted(grad_in, "pipe", -1)
    return (sent_fwd[None], sent_bwd[None])


def solution(mesh):
    few = mesh.shape["expert"] == 4
    return jax.shard_map(
        few_experts if few else many_experts,
        mesh=mesh,
        in_specs=(
            P("pipe", ("expert", "dp"), None),
            P("pipe", ("expert", "dp"), None),
            P("pipe", ("expert", "dp")),
            P("pipe", ("expert", "dp"), None),
            P("pipe", ("expert", "dp"), None),
            P("pipe", ("expert", "dp")),
            P("pipe", ("expert", "dp"), None),
            P("pipe", "expert", None, "dp"),
            P("pipe", "expert", None, "dp"),
            P("pipe", "expert", "dp", None),
        ),
        out_specs=(P("pipe", ("expert", "dp"), None), P("pipe", ("expert", "dp"), None)),
        check_vma=False,
    )
```

```python
import functools
import math

import jax
import jax.numpy as jnp
from jax import lax
from jax.experimental import pallas as pl
from jax.experimental.pallas import tpu as pltpu
from jax.sharding import PartitionSpec as P

BF16, F32 = jnp.bfloat16, jnp.float32
VMEM_LIMIT = 38 * 1024 * 1024
ROW_PARTS = 2
TAG_COLUMNS = 128


def contract_last(left_side, weights):
    return lax.dot_general(
        left_side, weights, (((1,), (1,)), ((), ())), preferred_element_type=F32
    )


def flipped(block, axis, stride):
    route = [(i, i ^ stride) for i in range(lax.axis_size(axis))]
    return lax.ppermute(block, axis, route)


def shifted(block, axis, distance):
    count = lax.axis_size(axis)
    return lax.ppermute(block, axis, [((i - distance) % count, i) for i in range(count)])


def chunk_of(width, most):
    best = 128
    for size in range(128, most + 1, 128):
        if width % size == 0:
            best = size
    return best


def gathered_rows(refs):
    return jnp.concatenate([ref[0] for ref in refs], axis=0)


def chained_rows(refs):
    others = len(refs) // 2
    own, below, above = refs[0][...], refs[1 : 1 + others], refs[1 + others :]
    return jnp.concatenate(
        [own] + [above[away][...] + below[others - 1 - away][...] for away in range(others)],
        axis=0,
    )


def gathered_input(x, begin, rows):
    count, unit = x.shape[0], math.gcd(begin, rows)
    arrays, specs = [], []
    for turn in range(count):
        for piece in range(begin // unit, (begin + rows) // unit):
            arrays.append(x)
            specs.append(
                lambda chunk, column, turn=turn, piece=piece: pl.BlockSpec(
                    (1, unit, chunk),
                    lambda i, at: (lax.rem(at[0] + turn, count), piece, column(i)),
                )
            )
    return gathered_rows, arrays, specs


def chained_input(hops, begin, rows):
    (own, _), *others = hops
    from_below, from_above = zip(*others)
    spec = lambda chunk, column: pl.BlockSpec(
        (rows, chunk), lambda i, at: (begin // rows, column(i))
    )
    arrays = [own, *from_below, *from_above]
    return chained_rows, arrays, [spec] * len(arrays)


def weight_copies(chunk, steps, gate_ups, downs, gate_up_held, down_held, sems):
    by_chunk = []
    for step in range(steps):
        part = pl.ds(step * chunk, chunk)
        by_chunk.append(
            (
                [
                    pltpu.make_async_copy(
                        ref.at[:, part, :], gate_up_held.at[i, :, part, :], sems.at[0, step, i]
                    )
                    for i, ref in enumerate(gate_ups)
                ],
                [
                    pltpu.make_async_copy(
                        ref.at[:, part], down_held.at[i, :, part], sems.at[1, step, i]
                    )
                    for i, ref in enumerate(downs)
                ],
            )
        )
    return by_chunk


def own_hidden(at_ref, tags, column, hidden):
    mine = tags[:, column : column + 1].astype(jnp.int32) == at_ref[1]
    unit = lax.broadcasted_iota(jnp.int32, (tags.shape[0], hidden), 1)
    return mine == (unit < hidden // 2)


def joined(refs, axis, index=None):
    pick = (lambda ref: ref[...]) if index is None else (lambda ref: ref[index])
    return jnp.concatenate([pick(ref) for ref in refs], axis=axis)


def put_blocks(outs, total):
    rows = outs[0].shape[0]
    for index, ref in enumerate(outs):
        ref[...] = total[index * rows : (index + 1) * rows].astype(ref.dtype)


def compiler_params():
    return pltpu.CompilerParams(vmem_limit_bytes=VMEM_LIMIT)


def small_cost(many, hidden):
    return pl.CostEstimate(flops=many * hidden, bytes_accessed=many, transcendentals=0)


def home_shapes(count, rows, width, parts=1):
    own, others = (jax.ShapeDtypeStruct((rows // parts, width), kind) for kind in (F32, BF16))
    return [own] * parts + [others] * (parts * (count - 1))


def hidden_kernel(count, pieces, steps, at_ref, *refs):
    tags, rows_in, gate_ups = refs[:count], refs[count : 2 * count], refs[2 * count : -3]
    out_ref, gate_ref, up_ref = refs[-3:]
    step = pl.program_id(0)

    @pl.when(step == 0)
    def _():
        gate_ref[...] = jnp.zeros_like(gate_ref)
        up_ref[...] = jnp.zeros_like(up_ref)

    x = gathered_rows(rows_in)
    gate_ref[...] += jnp.dot(x, joined(gate_ups, 1, 0), preferred_element_type=F32)
    up_ref[...] += jnp.dot(x, joined(gate_ups, 1, 1), preferred_element_type=F32)

    @pl.when(step == steps - 1)
    def _():
        gate, up = gate_ref[...], up_ref[...]
        keep = own_hidden(at_ref, gathered_rows(tags), 0, gate.shape[1])
        out_ref[...] = jnp.where(keep, gate * jax.nn.sigmoid(gate) * up, 0.0).astype(BF16)


def hidden_call(at, x_gathered, rows, width, gate_ups):
    count, pieces, hid = x_gathered.shape[0], len(gate_ups), gate_ups[0].shape[2]
    chunk = chunk_of(width, 1792)
    steps, hidden, many = width // chunk, pieces * hid, count * rows
    _, arrays, specs = gathered_input(x_gathered, 0, rows)
    return pl.pallas_call(
        functools.partial(hidden_kernel, count, pieces, steps),
        grid_spec=pltpu.PrefetchScalarGridSpec(
            num_scalar_prefetch=1,
            grid=(steps,),
            in_specs=[spec(TAG_COLUMNS, lambda i: width // TAG_COLUMNS) for spec in specs]
            + [spec(chunk, lambda i: i) for spec in specs]
            + [pl.BlockSpec((2, chunk, hid), lambda i, at: (0, i, 0))] * pieces,
            out_specs=pl.BlockSpec((many, hidden), lambda i, at: (0, 0)),
            scratch_shapes=[pltpu.VMEM((many, hidden), F32)] * 2,
        ),
        out_shape=jax.ShapeDtypeStruct((many, hidden), BF16),
        compiler_params=compiler_params(),
        cost_estimate=small_cost(many, hidden),
    )(at, *arrays, *arrays, *gate_ups)


def down_kernel(pieces, hidden_ref, *refs):
    downs, outs = refs[:pieces], refs[pieces:]
    total = jnp.dot(hidden_ref[...], joined(downs, 0), preferred_element_type=F32)
    put_blocks(outs, total)


def down_call(hidden_rows, count, downs):
    many, hidden = hidden_rows.shape
    pieces, (hid, width), rows = len(downs), downs[0].shape, many // count
    chunk = chunk_of(width, 1792)
    return pl.pallas_call(
        functools.partial(down_kernel, pieces),
        grid=(width // chunk,),
        in_specs=[pl.BlockSpec((many, hidden), lambda i: (0, 0))]
        + [pl.BlockSpec((hid, chunk), lambda i: (0, i))] * pieces,
        out_specs=[pl.BlockSpec((rows, chunk), lambda i: (0, i))] * count,
        out_shape=home_shapes(count, rows, width),
        compiler_params=compiler_params(),
        cost_estimate=small_cost(many, hidden),
    )(hidden_rows, *downs)


def backward_kernel(inputs, count, pieces, chunk, steps, at_ref, *refs):
    tags, refs = refs[:count], refs[count:]
    rows_in, scaled_in, refs = refs[:inputs], refs[inputs : 2 * inputs], refs[2 * inputs :]
    gate_ups, downs, outs = refs[:pieces], refs[pieces : 2 * pieces], refs[2 * pieces : -8]
    gate_ref, up_ref, grad_ref, grad_gate_ref, grad_up_ref = refs[-8:-3]
    gate_up_held, down_held, sems = refs[-3:]
    step = pl.program_id(0)
    copies = weight_copies(chunk, steps, gate_ups, downs, gate_up_held, down_held, sems)

    @pl.when(step == 0)
    def _():
        for of_gate_up, of_down in copies:
            for copy in of_gate_up + of_down:
                copy.start()
        for total in (gate_ref, up_ref, grad_ref):
            total[...] = jnp.zeros_like(total)

    for number, (of_gate_up, of_down) in enumerate(copies):

        @pl.when(step == number)
        def _(waited=of_gate_up + of_down):
            for copy in waited:
                copy.wait()

    at_chunk = pl.ds(pl.multiple_of(lax.rem(step, steps) * chunk, chunk), chunk)

    def gate_or_up(which):
        return jnp.concatenate(
            [gate_up_held[i, which, at_chunk, :] for i in range(pieces)], axis=1
        )

    @pl.when(step < steps)
    def _():
        x = chained_rows(rows_in)
        gate_ref[...] += jnp.dot(x, gate_or_up(0), preferred_element_type=F32)
        up_ref[...] += jnp.dot(x, gate_or_up(1), preferred_element_type=F32)
        down = jnp.concatenate([down_held[i, :, at_chunk] for i in range(pieces)], axis=0)
        grad_ref[...] += contract_last(chained_rows(scaled_in), down)

    @pl.when(step == steps - 1)
    def _():
        gate, up, grad = gate_ref[...], up_ref[...], grad_ref[...]
        keep = own_hidden(at_ref, gathered_rows(tags), TAG_COLUMNS // 2, gate.shape[1])
        s = jax.nn.sigmoid(gate)
        silu = gate * s
        grad_gate = grad * up * (s + silu * (1.0 - s))
        grad_gate_ref[...] = jnp.where(keep, grad_gate, 0.0).astype(BF16)
        grad_up_ref[...] = jnp.where(keep, grad * silu, 0.0).astype(BF16)

    @pl.when(step >= steps)
    def _():
        total = contract_last(grad_gate_ref[...], gate_or_up(0))
        total += contract_last(grad_up_ref[...], gate_or_up(1))
        put_blocks(outs, total)


def backward_call(at, x_gathered, rows, parts, hops, gate_ups, downs):
    count, width = x_gathered.shape[0], hops[0][0].shape[1]
    pieces, hid = len(downs), downs[0].shape[0]
    chunk = chunk_of(width, 1792)
    steps, hidden, many = width // chunk, pieces * hid, count * rows
    first = lambda i: jnp.minimum(i, steps - 1)
    second = lambda i: jnp.maximum(i - steps, 0)
    _, tags, tag_specs = gathered_input(x_gathered, 0, rows)
    _, rows_in, row_specs = chained_input(hops, 0, rows)
    _, _, scaled_specs = chained_input(hops, rows, rows)
    return pl.pallas_call(
        functools.partial(backward_kernel, len(rows_in), count, pieces, chunk, steps),
        grid_spec=pltpu.PrefetchScalarGridSpec(
            num_scalar_prefetch=1,
            grid=(2 * steps,),
            in_specs=[spec(TAG_COLUMNS, lambda i: width // TAG_COLUMNS) for spec in tag_specs]
            + [spec(chunk, first) for spec in row_specs + scaled_specs]
            + [pl.BlockSpec(memory_space=pl.ANY)] * (2 * pieces),
            out_specs=[pl.BlockSpec((rows // parts, chunk), lambda i, at: (0, second(i)))]
            * (parts * count),
            scratch_shapes=[pltpu.VMEM((many, hidden), F32)] * 3
            + [pltpu.VMEM((many, hidden), BF16)] * 2
            + [
                pltpu.VMEM((pieces, 2, width, hid), BF16),
                pltpu.VMEM((pieces, hid, width), BF16),
                pltpu.SemaphoreType.DMA((2, steps, pieces)),
            ],
        ),
        out_shape=home_shapes(count, rows, width, parts),
        compiler_params=compiler_params(),
        cost_estimate=small_cost(many, hidden),
    )(at, *tags, *rows_in, *rows_in, *gate_ups, *downs)


def after(value, *earlier):
    return lax.optimization_barrier((value, earlier))[0]


def hop(below, above, axis, step):
    count = lax.axis_size(axis)
    up = [(i, i + 1) for i in range(step - 1, count - 1)]
    down = [(i, i - 1) for i in range(1, count - step + 1)]
    return lax.ppermute(below, axis, up), lax.ppermute(above, axis, down)


def summands(blocks, step, arrived):
    pair = (blocks[len(blocks) - step], blocks[step])
    if arrived is None:
        return pair
    return tuple(
        (own.astype(F32) + other.astype(F32)).astype(BF16) for own, other in zip(pair, arrived)
    )


def step_home(pair, axis, step):
    count = lax.axis_size(axis)
    up = lax.ppermute(pair[0], axis, [(i, i + 1) for i in range(step)])
    down = lax.ppermute(pair[1], axis, [(i, i - 1) for i in range(count - step, count)])
    return up, down


def summed(block, arrived):
    for part in arrived:
        block = block + part.astype(F32)
    return block


def few_experts(
    x_forward,
    route_forward,
    prob_forward,
    x_backward,
    route_backward,
    prob_backward,
    grad_output,
    w_gate,
    w_up,
    w_down,
):
    tokens_here, width = x_forward.shape[1:]
    expert_here = lax.axis_index("expert") // 2
    count = lax.axis_size("dp")
    at = jnp.stack([lax.axis_index("dp"), expert_here]).astype(jnp.int32)
    half_tag = (tokens_here, TAG_COLUMNS // 2)
    tagged = jnp.concatenate(
        [x_forward[0]]
        + [jnp.broadcast_to(r[0].astype(BF16), half_tag) for r in (route_forward, route_backward)],
        axis=1,
    )
    scaled_grad = (prob_backward[0][:, None] * grad_output[0].astype(F32)).astype(BF16)
    back_rows = jnp.concatenate([x_backward[0], scaled_grad], axis=0)
    gate_up, down = jnp.concatenate([w_gate[0], w_up[0]], axis=0), w_down[0, 0]

    x_gathered = lax.all_gather(tagged, "dp")
    across_down = flipped(down, "expert", 2)
    gate_up, back_rows = after((gate_up, back_rows), across_down)
    across_gate_up = flipped(gate_up, "expert", 2)
    hops = [(back_rows, back_rows)]
    for step in range(1, count):
        hops.append(hop(*hops[-1], "dp", step))
    gate_ups = [gate_up, flipped(after(gate_up, hops[1]), "expert", 1), across_gate_up]
    downs = [down, flipped(down, "expert", 1), across_down, flipped(across_down, "expert", 1)]
    gate_ups.append(flipped(after(across_gate_up, x_gathered, hops[1], downs[1:]), "expert", 1))
    hidden_fwd = hidden_call(at, x_gathered, tokens_here, width, gate_ups)
    partial_fwd = down_call(hidden_fwd, count, downs)

    arrived_fwd = step_home(summands(partial_fwd, 1, None), "dp", 1)
    arrived_fwd = after(arrived_fwd, hops[2])
    arrived_fwd = step_home(summands(partial_fwd, 2, arrived_fwd), "dp", 2)
    sends_fwd = summands(partial_fwd, 3, arrived_fwd)
    arrived_fwd = step_home(sends_fwd, "dp", 3)
    hops[0] = after(hops[0], sends_fwd)
    partial_bwd = backward_call(at, x_gathered, tokens_here, ROW_PARTS, hops, gate_ups, downs)

    arrived_fwd = after(arrived_fwd, partial_bwd[-1])
    total_fwd = summed(partial_fwd[0], arrived_fwd)
    layer_out = (x_forward[0].astype(F32) + prob_forward[0][:, None] * total_fwd).astype(BF16)
    sent_fwd = shifted(layer_out, "pipe", 1)
    size = tokens_here // ROW_PARTS
    partial_bwd = after(tuple(partial_bwd), arrived_fwd)
    blocks = [partial_bwd[part::ROW_PARTS] for part in range(ROW_PARTS)]
    arrived = [None] * ROW_PARTS
    for step in range(1, count):
        for part in range(ROW_PARTS):
            if step == 3 and part == 0:
                arrived[0] = after(arrived[0], sent_fwd)
            arrived[part] = step_home(summands(blocks[part], step, arrived[part]), "dp", step)
    sent_bwd = []
    for part in range(ROW_PARTS):
        rows = slice(part * size, (part + 1) * size)
        total = summed(blocks[part][0], after(arrived[part], sent_bwd))
        grad_in = (grad_output[0, rows].astype(F32) + total).astype(BF16)
        sent_bwd.append(shifted(grad_in, "pipe", -1))
    return (sent_fwd[None], jnp.concatenate(sent_bwd, axis=0)[None])


def from_partner(block, axis, stride):
    count = lax.axis_size(axis)
    route = []
    for low in range(count):
        high = low | 1 << stride
        if high != low and high < count:
            route += [(low, high), (high, low)]
    return lax.ppermute(block, axis, route)


def silu_parts(pre_gate):
    sigma_gate = jax.nn.sigmoid(pre_gate)
    return (pre_gate * sigma_gate, sigma_gate)


def expert_pass(forward_rows, backward_rows, scaled_rows, gate_weight, up_weight, down_weight):
    gate_fwd = jnp.dot(forward_rows, gate_weight, preferred_element_type=jnp.float32)
    up_fwd = jnp.dot(forward_rows, up_weight, preferred_element_type=jnp.float32)
    silu_fwd, sigma_fwd = silu_parts(gate_fwd)
    hidden_fwd = (silu_fwd * up_fwd).astype(jnp.bfloat16)
    expert_out = jnp.dot(hidden_fwd, down_weight, preferred_element_type=jnp.float32)
    gate_bwd = jnp.dot(backward_rows, gate_weight, preferred_element_type=jnp.float32)
    up_bwd = jnp.dot(backward_rows, up_weight, preferred_element_type=jnp.float32)
    silu_bwd, sigma_bwd = silu_parts(gate_bwd)
    grad_hidden = contract_last(scaled_rows, down_weight)
    grad_gate = (grad_hidden * up_bwd * (sigma_bwd + silu_bwd * (1.0 - sigma_bwd))).astype(
        jnp.bfloat16
    )
    grad_up = (grad_hidden * silu_bwd).astype(jnp.bfloat16)
    grad_rows = contract_last(grad_gate, gate_weight) + contract_last(grad_up, up_weight)
    return (expert_out, grad_rows)


def placing(routes, experts_here, capacity):
    route_hits = (routes[:, None] == jnp.arange(experts_here, dtype=jnp.int32)[None, :]).astype(
        jnp.int32
    )
    before = jnp.cumsum(route_hits, axis=0) - route_hits
    slot_index = jnp.sum(before * route_hits, axis=1)
    position = routes * capacity + slot_index
    selector = (
        position[None, :] == jnp.arange(experts_here * capacity, dtype=jnp.int32)[:, None]
    ).astype(jnp.bfloat16)
    return (position, selector)


def packing(selector, values):
    return jnp.dot(selector, values, preferred_element_type=jnp.float32).astype(jnp.bfloat16)


def many_experts(
    x_forward,
    route_forward,
    prob_forward,
    x_backward,
    route_backward,
    prob_backward,
    grad_output,
    w_gate,
    w_up,
    w_down,
):
    tokens_here = x_forward.shape[1]
    feature_width = x_forward.shape[2]
    groups = lax.axis_size("expert")
    experts_here = groups // 2
    capacity = min(tokens_here, (tokens_here * 5 + 4 * experts_here - 1) // (4 * experts_here))
    pair_side = lax.axis_index("expert") % 2
    gate_full, up_full, down_full = (
        lax.all_gather(w_gate[0, 0], "dp", axis=1, tiled=True),
        lax.all_gather(w_up[0, 0], "dp", axis=1, tiled=True),
        lax.all_gather(w_down[0, 0], "dp", axis=0, tiled=True),
    )
    pos_fwd, select_fwd = placing(route_forward[0, :, 0], experts_here, capacity)
    pos_bwd, select_bwd = placing(route_backward[0, :, 0], experts_here, capacity)
    scaled_grad = (prob_backward[0][:, None] * grad_output[0].astype(jnp.float32)).astype(
        jnp.bfloat16
    )
    stacked = jnp.stack(
        [
            packing(select_fwd, x_forward[0]),
            packing(select_bwd, x_backward[0]),
            packing(select_bwd, scaled_grad),
        ]
    )
    stacked = stacked.reshape(3, experts_here, capacity, feature_width)
    split_rows = stacked.reshape(3, experts_here, capacity, 2, feature_width // 2).transpose(
        0, 1, 3, 2, 4
    )
    split_rows = split_rows.reshape(3, groups, capacity, feature_width // 2)
    own_half = lax.all_to_all(split_rows, "expert", split_axis=1, concat_axis=1, tiled=True)
    partner_half = from_partner(own_half, "expert", 0)
    arrived = jnp.where(
        pair_side == 0,
        jnp.concatenate([own_half, partner_half], axis=3),
        jnp.concatenate([partner_half, own_half], axis=3),
    )
    expert_rows = arrived.reshape(3, groups * capacity, feature_width)
    expert_out, grad_rows = expert_pass(
        expert_rows[0], expert_rows[1], expert_rows[2], gate_full, up_full, down_full
    )
    results = jnp.stack([expert_out, grad_rows]).reshape(2, groups, capacity, feature_width)
    quarters = results.reshape(2, groups, capacity, 2, feature_width // 2)
    keep_part = jnp.where(pair_side == 0, quarters[:, :, :, 0], quarters[:, :, :, 1])
    give_part = jnp.where(pair_side == 0, quarters[:, :, :, 1], quarters[:, :, :, 0])
    finished = keep_part + from_partner(give_part.astype(jnp.bfloat16), "expert", 0).astype(
        give_part.dtype
    )
    returned = lax.all_to_all(finished, "expert", split_axis=1, concat_axis=1, tiled=True)
    combined = returned.reshape(2, experts_here, 2, capacity, feature_width // 2).transpose(
        0, 1, 3, 2, 4
    )
    combined = combined.reshape(2, experts_here, capacity, feature_width)
    flat_out = combined.reshape(2, experts_here * capacity, feature_width)
    moved_fwd = jnp.take(flat_out[0], pos_fwd, axis=0)
    moved_bwd = jnp.take(flat_out[1], pos_bwd, axis=0)
    layer_out = (x_forward[0].astype(jnp.float32) + prob_forward[0][:, None] * moved_fwd).astype(
        jnp.bfloat16
    )
    grad_in = (grad_output[0].astype(jnp.float32) + moved_bwd).astype(jnp.bfloat16)
    sent_fwd = shifted(layer_out, "pipe", 1)
    sent_bwd = shifted(grad_in, "pipe", -1)
    return (sent_fwd[None], sent_bwd[None])


def solution(mesh):
    few = mesh.shape["expert"] == 4
    return jax.shard_map(
        few_experts if few else many_experts,
        mesh=mesh,
        in_specs=(
            P("pipe", ("expert", "dp"), None),
            P("pipe", ("expert", "dp"), None),
            P("pipe", ("expert", "dp")),
            P("pipe", ("expert", "dp"), None),
            P("pipe", ("expert", "dp"), None),
            P("pipe", ("expert", "dp")),
            P("pipe", ("expert", "dp"), None),
            P("pipe", "expert", None, "dp"),
            P("pipe", "expert", None, "dp"),
            P("pipe", "expert", "dp", None),
        ),
        out_specs=(P("pipe", ("expert", "dp"), None), P("pipe", ("expert", "dp"), None)),
        check_vma=False,
    )
```
